512 devices in a mesh: shot: 8 (over y_lo, x), slab: 64 (over y_hi, z, core).
Axes of the slice: x: 4, y: 4 (y_hi: 2, y_lo: 2; y = y_hi * 2 + y_lo), z: 16, core: 2. Of those that a mesh axis runs over, the one named last changes fastest.
Arguments:
- src_prev: float32 [8, 64, 512, 128], P('shot', None, 'slab'), may hold values from -6 to 6
- src_cur: float32 [8, 64, 512, 128], P('shot', None, 'slab'), may hold values from -6 to 6
- rec_cur: float32 [8, 64, 512, 128], P('shot', None, 'slab'), may hold values from -6 to 6
- rec_next: float32 [8, 64, 512, 128], P('shot', None, 'slab'), may hold values from -6 to 6
- velocity: float32 [512, 512, 128], P('shot', 'slab'), may hold values from 0.15 to 0.42
- aperture_tiles: int32 [8, 8], replicated, may hold values from 0 to 63, as said below
- wavelet: float32 [8, 4], replicated, may hold values from -8 to 8
- src_x: int32 [8], replicated, may hold values from 0 to 63
- src_z: int32 [8], replicated, may hold values from 0 to 511
- src_y: int32 [8], replicated, may hold values from 0 to 127
- rec_depth: int32 [8], replicated, may hold values from 0 to 511
- rec_data: bfloat16 [8, 4, 64, 128], P('shot'), may hold values from -6 to 6
Outputs:
- image_model: float32 [512, 512, 128], P('shot', 'slab')
- src_last: float32 [8, 64, 512, 128], P('shot', None, 'slab')
- rec_first: float32 [8, 64, 512, 128], P('shot', None, 'slab')
The draws below stay inside these ranges and needn't reach their ends.
Inputs may be any that keep to these rules, and one draw needn't show every extreme that they name: `aperture_tiles`: each row lists 8 distinct model tiles in increasing order; tile t is held by index t // 8 of shot; a row takes at most 2 tiles held by one index, and exactly 2 from some index in every row.
All inputs are finite; a program needn't handle non-finite values.
Results may differ from the reference program's by a relative error of at most 0.0003.
Values sent between devices are 32-bit elements; how exact they have to be, the bound alone decides.
No kernel may reach another device: no remote copies, remote signals or barrier semaphores. Data moves between devices by JAX's collectives and lax.ppermute only.
A program may use at most 64 MiB of HBM per device.

```python
import jax
import jax.numpy as jnp

BX = 8
KT = 8
XT_DEV = 8
AY = 128
STEPS = 4
SHOTS = 8
CAP = 2
AX = 64
TILES = 64
MX = 512
NZ = 512
N_SHOT = 8


def draw_aperture_tiles(key, part):
    key = jax.random.fold_in(key, 11)
    rows = []
    for shot_number in range(N_SHOT):
        shot_key = jax.random.fold_in(key, shot_number)
        offset_rows = []
        for owner_number in range(N_SHOT):
            owner_key = jax.random.fold_in(shot_key, 1000 + owner_number)
            offset_rows.append(jax.random.permutation(owner_key, XT_DEV)[:CAP])
        offsets = jnp.stack(offset_rows)
        candidates = (jnp.arange(N_SHOT)[:, None] * XT_DEV + offsets).reshape(-1)
        scores = jax.random.permutation(jax.random.fold_in(shot_key, 7), N_SHOT * CAP)
        chosen = jax.random.randint(jax.random.fold_in(shot_key, 9), (), 0, N_SHOT)
        owner_of = jnp.repeat(jnp.arange(N_SHOT), CAP)
        slot_of = jnp.tile(jnp.arange(CAP), N_SHOT)
        scores = jnp.where(owner_of == chosen, -1 - slot_of, scores)
        order = jnp.argsort(scores, stable=True)
        picked = candidates[order[:KT]]
        rows.append(jnp.sort(picked))
    return jnp.stack(rows).astype(jnp.int32)


def touch_ends(values, stream_key, smallest, largest):
    extent = values.shape
    index_at = [jax.random.randint(jax.random.fold_in(stream_key, axis), (), 0, extent[axis]) for axis in range(len(extent))]
    values = values.at[tuple(index_at)].set(smallest)
    longest = extent.index(max(extent))
    index_at[longest] = (index_at[longest] + 1) % extent[longest]
    return values.at[tuple(index_at)].set(largest)


def steps_of(own_key, shape, shards, low, largest):
    def one(axis_at, shards_of):
        draws = jax.random.uniform(jax.random.fold_in(jax.random.fold_in(own_key, 6), axis_at), (shards_of,), jnp.float32, low / len(shards), largest / len(shards))
        return jnp.repeat(jnp.exp(draws), shape[axis_at] // shards_of).reshape((-1,) + (1,) * (len(shape) - axis_at - 1))

    level = one(*shards[0])
    for cut in shards[1:]:
        level = level * one(*cut)
    return level


def noise(key, extent, scale, most, pieces=(), kind=jnp.bfloat16):
    array = scale * jax.random.normal(key, extent, jnp.float32)
    if pieces:
        array = array * steps_of(key, extent, pieces, -0.22, 0.18)
    return jnp.clip(array, -most, most).astype(kind)


def setup_inputs(seed: int = 0) -> dict:
    key_of = jax.random.split(jax.random.key(seed), 13)
    src_prev = noise(key_of[0], (SHOTS, AX, NZ, AY), 1.0, 6.0, ((0, 8), (2, 64)), jnp.float32)
    src_cur = noise(key_of[1], (SHOTS, AX, NZ, AY), 1.0, 6.0, ((0, 8), (2, 64)), jnp.float32)
    rec_cur = noise(key_of[2], (SHOTS, AX, NZ, AY), 1.0, 6.0, ((0, 8), (2, 64)), jnp.float32)
    rec_next = noise(key_of[3], (SHOTS, AX, NZ, AY), 1.0, 6.0, ((0, 8), (2, 64)), jnp.float32)
    velocity = jnp.clip(0.15 + 0.26999998 * jax.random.uniform(key_of[4], (MX, NZ, AY), jnp.float32) ** steps_of(key_of[4], (MX, NZ, AY), ((0, 8), (1, 64)), -0.2, 0.2), 0.15, 0.42)
    aperture_tiles = draw_aperture_tiles(jax.random.fold_in(key_of[12], 71), 0)
    wavelet = noise(key_of[6], (SHOTS, STEPS), 2.0, 8.0, (), jnp.float32)
    src_x = touch_ends(jax.random.randint(key_of[7], (SHOTS,), 0, AX), jax.random.fold_in(key_of[7], 1), 0, AX - 1).astype(jnp.int32)
    src_z = touch_ends(jax.random.randint(key_of[8], (SHOTS,), 0, NZ), jax.random.fold_in(key_of[8], 1), 0, NZ - 1).astype(jnp.int32)
    src_y = touch_ends(jax.random.randint(key_of[9], (SHOTS,), 0, AY), jax.random.fold_in(key_of[9], 1), 0, AY - 1).astype(jnp.int32)
    rec_depth = touch_ends(jax.random.randint(key_of[10], (SHOTS,), 0, NZ), jax.random.fold_in(key_of[10], 1), 0, NZ - 1).astype(jnp.int32)
    rec_data = noise(key_of[11], (SHOTS, STEPS, AX, AY), 1.0, 6.0, ((0, 8),))
    return {"src_prev": src_prev, "src_cur": src_cur, "rec_cur": rec_cur, "rec_next": rec_next, "velocity": velocity, "aperture_tiles": aperture_tiles, "wavelet": wavelet, "src_x": src_x, "src_z": src_z, "src_y": src_y, "rec_depth": rec_depth, "rec_data": rec_data}


COEFFS = (-205.0 / 72.0, 8.0 / 5.0, -1.0 / 5.0, 8.0 / 315.0, -1.0 / 560.0)


def laplace(extended):
    size_x, size_e, size_y = extended.shape
    size_z = size_e - 8
    padded = jnp.pad(extended, ((4, 4), (0, 0), (4, 4)))
    centre = padded[4:4 + size_x, 4:4 + size_z, 4:4 + size_y]
    result = (3.0 * COEFFS[0]) * centre
    for reach in range(1, 5):
        along_z = padded[4:4 + size_x, 4 + reach:4 + reach + size_z, 4:4 + size_y] + padded[4:4 + size_x, 4 - reach:4 - reach + size_z, 4:4 + size_y]
        along_x = padded[4 + reach:4 + reach + size_x, 4:4 + size_z, 4:4 + size_y] + padded[4 - reach:4 - reach + size_x, 4:4 + size_z, 4:4 + size_y]
        along_y = padded[4:4 + size_x, 4:4 + size_z, 4 + reach:4 + reach + size_y] + padded[4:4 + size_x, 4:4 + size_z, 4 - reach:4 - reach + size_y]
        result = result + COEFFS[reach] * (along_z + along_x + along_y)
    return result


def zpad(field):
    return jnp.pad(field, ((0, 0), (4, 4), (0, 0)))


def reference(src_prev, src_cur, rec_cur, rec_next, velocity, aperture_tiles, wavelet, src_x, src_z, src_y, rec_depth, rec_data):
    image_model = jnp.zeros((TILES, BX, NZ, AY), jnp.float32)
    tiled_model = velocity.reshape(TILES, BX, NZ, AY)
    cells_x = jnp.arange(AX)
    cells_z = jnp.arange(NZ)
    cells_y = jnp.arange(AY)
    finals_src = []
    finals_rec = []
    for shot_index in range(SHOTS):
        my_tiles = aperture_tiles[shot_index]
        aperture_vel = tiled_model[my_tiles].reshape(AX, NZ, AY)
        rate_field = aperture_vel * aperture_vel
        spot = ((cells_x == src_x[shot_index])[:, None, None] & (cells_z == src_z[shot_index])[None, :, None] & (cells_y == src_y[shot_index])[None, None, :]).astype(jnp.float32)
        plane = (cells_z == rec_depth[shot_index]).astype(jnp.float32)[None, :, None]
        src_old = src_prev[shot_index]
        src_now = src_cur[shot_index]
        src_snaps = [src_now]
        for step_index in range(STEPS):
            src_new = 2.0 * src_now - src_old + rate_field * laplace(zpad(src_now)) + wavelet[shot_index, step_index] * spot
            src_old, src_now = src_now, src_new
            src_snaps.append(src_now)
        rec_later = rec_next[shot_index]
        rec_now = rec_cur[shot_index]
        rec_snaps = [rec_now]
        for step_index in range(STEPS):
            later_step = STEPS - 1 - step_index
            traces = rec_data[shot_index, later_step].astype(jnp.float32)[:, None, :]
            rec_new = 2.0 * rec_now - rec_later + rate_field * laplace(zpad(rec_now)) + plane * traces
            rec_later, rec_now = rec_now, rec_new
            rec_snaps.append(rec_now)
        image_sum = src_snaps[STEPS] * rec_snaps[0]
        for back in range(1, STEPS + 1):
            image_sum = image_sum + src_snaps[STEPS - back] * rec_snaps[back]
        image_model = image_model.at[my_tiles].add(image_sum.reshape(KT, BX, NZ, AY))
        finals_src.append(src_now)
        finals_rec.append(rec_now)
    return image_model.reshape(MX, NZ, AY), jnp.stack(finals_src), jnp.stack(finals_rec)
```

```python
import functools

import jax
import jax.numpy as jnp
from jax import lax
from jax.experimental import pallas as pl
from jax.experimental.pallas import tpu as pltpu
from jax.sharding import PartitionSpec as P

BX = 8
KT = 8
STEPS = 4
CAP = 2
REACH = 4
CHUNK = 8
VMEM = pltpu.VMEM
SMEM = pltpu.SMEM

COEFFS = (-205.0 / 72.0, 8.0 / 5.0, -1.0 / 5.0, 8.0 / 315.0, -1.0 / 560.0)


def call(body, outs, in_spaces, *args, scratch=(), flops=0, bytes_accessed=0):
    return pl.pallas_call(
        body,
        out_shape=[jax.ShapeDtypeStruct(s, jnp.float32) for s in outs],
        in_specs=[pl.BlockSpec(memory_space=s) for s in in_spaces],
        out_specs=[pl.BlockSpec(memory_space=VMEM) for _ in outs],
        scratch_shapes=list(scratch),
        compiler_params=pltpu.CompilerParams(vmem_limit_bytes=24 * 1024 * 1024),
        cost_estimate=pl.CostEstimate(
            flops=flops, bytes_accessed=bytes_accessed, transcendentals=0
        ),
    )(*args)


def rows_of(shape):
    return lax.broadcasted_iota(jnp.int32, shape, len(shape) - 2)


def pack_pairs(field, low_ref, high_ref, at, odd):
    pairs = field.reshape(field.shape[0] // 2, 2, 8, field.shape[2])
    first, second = pairs[:, 0], pairs[:, 1]
    top = rows_of(first.shape) < REACH
    low = jnp.where(top, first, pltpu.roll(second, REACH, 1))
    high = jnp.where(top, pltpu.roll(first, REACH, 1), second)
    low_ref[at] = jnp.where(odd, high, low)
    high_ref[at] = jnp.where(odd, low, high)


def pack_kernel(tiles, vel, src, rec, send, to_far, to_near):
    shot = lax.axis_index("shot")
    odd = lax.rem(lax.axis_index("slab"), 2) == 1
    n_shot = send.shape[0]

    def one_shot(g, _):
        before = jnp.int32(0)
        for k in range(KT):
            before += (tiles[g, k] < shot * BX).astype(jnp.int32)
        for j in range(CAP):
            k = jnp.minimum(before + j, KT - 1)
            own = jnp.clip(tiles[g, k] - shot * BX, 0, vel.shape[0] // BX - 1)
            send[g, pl.ds(j * BX, BX)] = vel[pl.ds(own * BX, BX)]
        return 0

    lax.fori_loop(0, n_shot, one_shot, 0)
    half = src.shape[0] // 2
    for f, field in enumerate((src, rec)):

        def one_chunk(c, _):
            at = pl.ds(f * half + c * (CHUNK // 2), CHUNK // 2)
            pack_pairs(field[pl.ds(c * CHUNK, CHUNK)], to_far, to_near, at, odd)
            return 0

        lax.fori_loop(0, field.shape[0] // CHUNK, one_chunk, 0)


def interior_kernel(src, rec, src_lap, rec_lap, padded):
    size_x, size_z, size_y = src.shape
    zeros = jnp.zeros((REACH, size_z, size_y), jnp.float32)
    shape = (1, size_z, size_y)
    row = rows_of(shape)
    lane = lax.broadcasted_iota(jnp.int32, shape, 2)
    padded[pl.ds(0, REACH)] = zeros
    padded[pl.ds(REACH + size_x, REACH)] = zeros
    for field, out in ((src, src_lap), (rec, rec_lap)):
        padded[pl.ds(REACH, size_x)] = field[...]

        def one_chunk(c, _):
            base = c * CHUNK
            wide = padded[pl.ds(base, CHUNK + 2 * REACH)]
            centre = wide[REACH : REACH + CHUNK]
            total = (3.0 * COEFFS[0]) * centre
            for r in range(1, REACH + 1):
                terms = wide[REACH + r : REACH + r + CHUNK] + wide[REACH - r : REACH - r + CHUNK]
                terms += jnp.where(row < size_z - r, pltpu.roll(centre, size_z - r, 1), 0.0)
                terms += jnp.where(row >= r, pltpu.roll(centre, r, 1), 0.0)
                terms += jnp.where(lane < size_y - r, pltpu.roll(centre, size_y - r, 2), 0.0)
                terms += jnp.where(lane >= r, pltpu.roll(centre, r, 2), 0.0)
                total += COEFFS[r] * terms
            out[pl.ds(base, CHUNK)] = total
            return 0

        lax.fori_loop(0, size_x // CHUNK, one_chunk, 0)


def finish_kernel(
    step,
    tiles,
    wavelet,
    spot_x,
    spot_z,
    spot_y,
    depth,
    traces,
    far,
    near,
    src,
    src_old,
    src_lap,
    rec,
    rec_old,
    rec_lap,
    *rest,
):
    shot = lax.axis_index("shot")
    slab = lax.axis_index("slab")
    last_slab = lax.axis_size("slab") - 1
    odd = lax.rem(slab, 2) == 1
    first, last = step == 0, step == STEPS - 1
    rest = list(rest)
    if first:
        vel_got = rest.pop(0)
    else:
        rate = rest.pop(0)
    if last:
        partial, src_first, rec_first = rest[:3]
        rest = rest[3:]
    src_new, rec_new = rest[:2]
    rest = rest[2:]
    if first:
        rate = rest.pop(0)
    if last:
        send = rest.pop(0)
    else:
        to_far, to_near = rest[:2]
        rest = rest[2:]
    (plane_rows,) = rest
    size_x, size_z, size_y = src.shape

    def place_of(k):
        owner = lax.shift_right_logical(tiles[shot, k], 3)
        before = lax.shift_right_logical(tiles[shot, max(k - 1, 0)], 3)
        slot = (before == owner).astype(jnp.int32) if k else jnp.int32(0)
        return owner, pl.ds(slot * BX, BX)

    if first:
        for k in range(KT):
            owner, at = place_of(k)
            block = vel_got[owner, at]
            rate[pl.ds(k * BX, BX)] = block * block

    row = rows_of((1, size_z, size_y))
    top = row < REACH
    mine = jnp.where(odd, 0, 1)
    has_left, has_right = slab > 0, slab < last_slab
    keep = (top & has_right) | (jnp.logical_not(top) & has_left)
    weights = []
    for shift in range(1, size_z):
        weight = jnp.zeros((1, size_z, size_y), jnp.float32)
        if shift <= REACH:
            weight = jnp.where(row < shift, COEFFS[shift], weight)
        if size_z - shift <= REACH:
            weight = jnp.where(row >= shift, COEFFS[size_z - shift], weight)
        weights.append(weight)
    half = size_x // 2
    for f, (now, old, lap, new) in enumerate(
        ((src, src_old, src_lap, src_new), (rec, rec_old, rec_lap, rec_new))
    ):

        def one_chunk(c, _):
            at = pl.ds(c * CHUNK, CHUNK)
            packed = pl.ds(f * half + c * (CHUNK // 2), CHUNK // 2)
            from_far, from_near = far[packed], near[mine, packed]
            left = jnp.where(odd, from_near, from_far)
            right = jnp.where(odd, from_far, from_near)
            even_x = jnp.where(top, right, pltpu.roll(left, REACH, 1))
            odd_x = jnp.where(top, pltpu.roll(right, REACH, 1), left)
            halo = jnp.stack([even_x, odd_x], axis=1).reshape(CHUNK, size_z, size_y)
            halo = jnp.where(keep, halo, 0.0)
            total = lap[at]
            for shift in range(1, size_z):
                total += weights[shift - 1] * pltpu.roll(halo, shift, 1)
            value = now[at]
            new[at] = 2.0 * value - old[at] + rate[at] * total
            return 0

        lax.fori_loop(0, size_x // CHUNK, one_chunk, 0)

    local_spot = spot_z[shot] - slab * size_z
    row2 = lax.broadcasted_iota(jnp.int32, (size_z, size_y), 0)
    lane2 = lax.broadcasted_iota(jnp.int32, (size_z, size_y), 1)

    @pl.when((local_spot >= 0) & (local_spot < size_z))
    def _():
        x = spot_x[shot]
        here = (row2 == local_spot) & (lane2 == spot_y[shot])
        src_new[x] += jnp.where(here, wavelet[shot, step], 0.0)

    local_plane = depth[shot] - slab * size_z

    @pl.when((local_plane >= 0) & (local_plane < size_z))
    def _():
        plane_rows[...] = traces[STEPS - 1 - step].astype(jnp.float32)

        def one_x(x, _):
            line = plane_rows[pl.ds(x, 1)]
            rec_new[x] += jnp.where(row2 == local_plane, line, 0.0)
            return 0

        lax.fori_loop(0, size_x, one_x, 0)

    if last:
        send[...] = jnp.zeros(send.shape, jnp.float32)
        for k in range(KT):
            owner, slot = place_of(k)
            at = pl.ds(k * BX, BX)
            image = partial[at] + src_new[at] * rec_first[at] + src_first[at] * rec_new[at]
            send[owner, slot] = image
    else:
        for f, field in enumerate((src_new, rec_new)):

            def one_pack(c, _):
                packed = pl.ds(f * half + c * (CHUNK // 2), CHUNK // 2)
                pack_pairs(field[pl.ds(c * CHUNK, CHUNK)], to_far, to_near, packed, odd)
                return 0

            lax.fori_loop(0, size_x // CHUNK, one_pack, 0)


def gather_kernel(tiles, got, out):
    shot = lax.axis_index("shot")
    out[...] = jnp.zeros(out.shape, jnp.float32)

    def one_shot(g, _):
        before = jnp.int32(0)
        for k in range(KT):
            before += (tiles[g, k] < shot * BX).astype(jnp.int32)
        for j in range(CAP):
            k = jnp.minimum(before + j, KT - 1)
            own = tiles[g, k] - shot * BX

            @pl.when((before + j < KT) & (own >= 0) & (own < out.shape[0] // BX))
            def _():
                out[pl.ds(own * BX, BX)] += got[g, pl.ds(j * BX, BX)]

        return 0

    lax.fori_loop(0, got.shape[0], one_shot, 0)


def image_part(s1, s2, s3, r1, r2, r3):
    return s3 * r1 + s2 * r2 + s1 * r3


def local(
    src_prev,
    src_cur,
    rec_cur,
    rec_next,
    velocity,
    aperture_tiles,
    wavelet,
    src_x,
    src_z,
    src_y,
    rec_depth,
    rec_data,
):
    slabs = lax.axis_size("slab")
    shots = lax.axis_size("shot")
    far_pairs = []
    for i in range(1, slabs - 1, 2):
        far_pairs += [(i, i + 1), (i + 1, i)]
    near_groups = [[i, i + 1] for i in range(0, slabs, 2)]

    def exchange(to_far, to_near):
        far = lax.ppermute(to_far, "slab", far_pairs)
        near = lax.all_gather(to_near, "slab", axis_index_groups=near_groups)
        return far, near

    src_old, src = src_prev[0], src_cur[0]
    rec_old, rec = rec_next[0], rec_cur[0]
    block = src.shape
    buffer = (shots, CAP * BX) + block[1:]
    send, to_far, to_near = call(
        pack_kernel, [buffer, block, block], [SMEM] + [VMEM] * 3,
        aperture_tiles, velocity, src, rec,
    )
    vel_got = lax.all_to_all(send, "shot", 0, 0)
    snaps = [(src, rec)]
    rate = None
    for step in range(STEPS):
        first, last = step == 0, step == STEPS - 1
        far, near = exchange(to_far, to_near)
        src_lap, rec_lap = call(
            interior_kernel, [block, block], [VMEM] * 2, src, rec,
            scratch=[VMEM((block[0] + 2 * REACH,) + block[1:], jnp.float32)],
            flops=2 * 45 * src.size, bytes_accessed=4 * 4 * src.size,
        )
        args = [aperture_tiles, wavelet, src_x, src_z, src_y, rec_depth]
        args += [rec_data[0], far, near, src, src_old, src_lap, rec, rec_old, rec_lap]
        args += [vel_got] if first else [rate]
        outs = [block, block]
        if last:
            (s0, r0), (s1, r1), (s2, r2), (s3, r3) = snaps
            args += [image_part(s1, s2, s3, r1, r2, r3), s0, r0]
            outs += [buffer]
        else:
            outs += [block] * (3 if first else 2)
        spaces = [SMEM] * 6 + [VMEM] * (len(args) - 6)
        got = call(
            functools.partial(finish_kernel, step), outs, spaces, *args,
            scratch=[VMEM((block[0], block[2]), jnp.float32)],
            flops=2 * 30 * src.size, bytes_accessed=10 * 4 * src.size,
        )
        src_old, rec_old = src, rec
        src, rec = got[:2]
        snaps.append((src, rec))
        if last:
            send = got[2]
        elif first:
            rate, to_far, to_near = got[2:]
        else:
            to_far, to_near = got[2:]
    image_got = lax.all_to_all(send, "shot", 0, 0)
    (image,) = call(gather_kernel, [velocity.shape], [SMEM, VMEM], aperture_tiles, image_got)
    return image, src[None], rec[None]


def solution(mesh):
    wave = P("shot", None, "slab", None)
    model = P("shot", "slab", None)
    return jax.shard_map(
        local,
        mesh=mesh,
        in_specs=(wave,) * 4 + (model,) + (P(),) * 6 + (P("shot", None, None, None),),
        out_specs=(model, wave, wave),
        check_vma=False,
    )
```

```python
import jax
import jax.numpy as jnp
from jax import lax
from jax.experimental import pallas as pl
from jax.experimental.pallas import tpu as pltpu
from jax.sharding import PartitionSpec as P

BX = 8
KT = 8
STEPS = 4
CAP = 2
REACH = 4
CHUNK = 8
VMEM = pltpu.VMEM
SMEM = pltpu.SMEM


SCALE = 5040.0
TAPS = (-43050.0, 8064.0, -1008.0, 128.0, -9.0)
WHOLE = 16


def call(body, outs, in_spaces, *args, scratch=(), flops=0, bytes_accessed=0):
    outs = [o if isinstance(o, tuple) and isinstance(o[0], tuple) else (o, VMEM) for o in outs]
    outs = [o if len(o) == 3 else o + (jnp.float32,) for o in outs]
    return pl.pallas_call(
        body,
        out_shape=[jax.ShapeDtypeStruct(s, t) for s, _, t in outs],
        in_specs=[pl.BlockSpec(memory_space=s) for s in in_spaces],
        out_specs=[pl.BlockSpec(memory_space=m) for _, m, _ in outs],
        scratch_shapes=list(scratch),
        compiler_params=pltpu.CompilerParams(vmem_limit_bytes=24 * 1024 * 1024),
        cost_estimate=pl.CostEstimate(
            flops=flops, bytes_accessed=bytes_accessed, transcendentals=0
        ),
    )(*args)


def rows_of(shape):
    return lax.broadcasted_iota(jnp.int32, shape, len(shape) - 2)


def pack_pairs(field, low_ref, high_ref, at, odd):
    pairs = field.reshape(field.shape[0] // 2, 2, 8, field.shape[2])
    first, second = pairs[:, 0], pairs[:, 1]
    top = rows_of(first.shape) < REACH
    low = jnp.where(top, first, pltpu.roll(second, REACH, 1))
    high = jnp.where(top, pltpu.roll(first, REACH, 1), second)
    low_ref[at] = jnp.where(odd, high, low)
    high_ref[at] = jnp.where(odd, low, high)


def pack_kernel(
    tiles_in, vel_in, src_in, rec_in, send, to_far, to_near, src, rec, tiles_out, vel, tiles, sems
):
    shot = lax.axis_index("shot")
    odd = lax.rem(lax.axis_index("slab"), 2) == 1
    moves = ((src_in, src), (rec_in, rec), (tiles_in, tiles), (tiles_in, tiles_out), (vel_in, vel))
    copies = [pltpu.make_async_copy(a, b, sems.at[i]) for i, (a, b) in enumerate(moves)]
    for copy in copies:
        copy.start()
    half = src.shape[0] // 2
    for f, field in enumerate((src, rec)):
        copies[f].wait()

        def one_chunk(c, _):
            at = pl.ds(f * half + c * (CHUNK // 2), CHUNK // 2)
            pack_pairs(field[pl.ds(c * CHUNK, CHUNK)], to_far, to_near, at, odd)
            return 0

        lax.fori_loop(0, field.shape[0] // CHUNK, one_chunk, 0)
    for copy in copies[2:]:
        copy.wait()
    n_shot = send.shape[0]

    def one_shot(g, _):
        before = jnp.int32(0)
        for k in range(KT):
            before += (tiles[g, k] < shot * BX).astype(jnp.int32)
        for j in range(CAP):
            k = jnp.minimum(before + j, KT - 1)
            own = jnp.clip(tiles[g, k] - shot * BX, 0, vel.shape[0] // BX - 1)
            send[g, pl.ds(j * BX, BX)] = vel[pl.ds(own * BX, BX)]
        return 0

    lax.fori_loop(0, n_shot, one_shot, 0)


def tap_of(reach):
    weight = jnp.zeros(reach.shape, jnp.float32)
    for r in range(1, REACH + 1):
        weight = jnp.where(reach == r, TAPS[r], weight)
    return weight


def split(values, axis):
    high = values.astype(jnp.bfloat16)
    low = (values - high.astype(jnp.float32)).astype(jnp.bfloat16)
    return jnp.concatenate([high, low], axis=axis)


def along_y_matrix(size_y):
    shape = (2 * size_y, size_y)
    row = lax.rem(lax.broadcasted_iota(jnp.int32, shape, 0), size_y)
    return tap_of(jnp.abs(row - lax.broadcasted_iota(jnp.int32, shape, 1))).astype(jnp.bfloat16)


def halo_matrix(size_z, odd):
    rows, packed = WHOLE * size_z, WHOLE * REACH
    shape = (rows, 2 * packed)
    out = lax.broadcasted_iota(jnp.int32, shape, 0)
    at = lax.broadcasted_iota(jnp.int32, shape, 1)
    x, z = out // size_z, lax.rem(out, size_z)
    inner = lax.rem(at, packed)
    x_at, plane = inner // REACH, lax.rem(inner, REACH)
    left = (at < packed) != odd
    reach = jnp.where(left, z + REACH - plane, size_z + plane - z)
    weight = jnp.where(x == x_at, tap_of(reach), 0.0).astype(jnp.bfloat16)
    return jnp.concatenate([weight, weight], axis=1)


def around(field, base):
    size_x = field.shape[0]
    low, high = max(base - REACH, 0), min(base + WHOLE + REACH, size_x)
    wide = field[pl.ds(low, high - low)]
    zeros = jnp.zeros((REACH,) + field.shape[1:], jnp.float32)
    if base - REACH < 0:
        wide = jnp.concatenate([zeros, wide], axis=0)
    if base + WHOLE + REACH > size_x:
        wide = jnp.concatenate([wide, zeros], axis=0)
    return wide


def flat_sums(wide, to_y):
    centre = wide[REACH : REACH + WHOLE]
    lines = split(centre.reshape(-1, centre.shape[2]), 1)
    total = jnp.dot(lines, to_y, preferred_element_type=jnp.float32)
    total = total.reshape(centre.shape) + TAPS[0] * centre
    for r in range(1, REACH + 1):
        terms = wide[REACH + r : REACH + r + WHOLE] + wide[REACH - r : REACH - r + WHOLE]
        total += TAPS[r] * terms
    return total, centre


def up_down(up, down, r):
    size_z = up.shape[1]
    return pltpu.roll(up, size_z - r, 1) + pltpu.roll(down, r, 1)


def own_depth_sums(own, halo):
    size_z = own.shape[1]
    row = rows_of((1,) + own.shape[1:])
    total = 0.0
    for r in range(1, REACH + 1):
        up = jnp.where(row < r, halo, own)
        down = jnp.where(row >= size_z - r, halo, own)
        total += TAPS[r] * up_down(up, down, r)
    return total


def halo_depth_sums(own, halo, outer):
    size_z = own.shape[1]
    row = rows_of((1,) + own.shape[1:])
    top = row < REACH
    above, below = jnp.where(top, own, outer), jnp.where(top, outer, own)
    total = 0.0
    for r in range(1, REACH + 1):
        up_same = (lax.rem(row + size_z - r, size_z) < REACH) == top
        down_same = (lax.rem(row + r, size_z) < REACH) == top
        up, down = jnp.where(up_same, halo, above), jnp.where(down_same, halo, below)
        total += TAPS[r] * up_down(up, down, r)
    return total


def inner_sums(field, base, to_y):
    total, centre = flat_sums(around(field, base), to_y)
    return total + own_depth_sums(centre, jnp.zeros((1,) + centre.shape[1:], jnp.float32)), centre


def unpack_pairs(left, right):
    top = rows_of((1,) + left.shape[1:]) < REACH
    even_x = jnp.where(top, right, pltpu.roll(left, REACH, 1))
    odd_x = jnp.where(top, pltpu.roll(right, REACH, 1), left)
    pairs = jnp.stack([even_x, odd_x], axis=1)
    return pairs.reshape((2 * left.shape[0],) + left.shape[1:])


def add_sources(step, new, spots, plane_rows, slab, shot, halo=None):
    wavelet, spot_x, spot_z, spot_y, depth, traces = spots
    src_new, rec_new = new
    size_x, size_z, size_y = src_new.shape
    row = lax.broadcasted_iota(jnp.int32, (size_z, size_y), 0)
    lane = lax.broadcasted_iota(jnp.int32, (size_z, size_y), 1)
    reach = 0 if halo is None else REACH
    local_spot = spot_z[shot] - slab * size_z
    local_plane = depth[shot] - slab * size_z
    at_spot = lax.rem(local_spot + size_z, size_z)
    at_plane = lax.rem(local_plane + size_z, size_z)

    def add_spot(field):
        x = spot_x[shot]
        here = (row == at_spot) & (lane == spot_y[shot])
        field[x] += jnp.where(here, wavelet[shot, step], 0.0)

    def add_plane(field):
        plane_rows[...] = traces[STEPS - 1 - step].astype(jnp.float32)

        def one_x(x, _):
            line = plane_rows[pl.ds(x, 1)]
            field[x] += jnp.where(row == at_plane, line, 0.0)
            return 0

        lax.fori_loop(0, size_x, one_x, 0, unroll=8)

    def inside(at, edge):
        return (at >= -edge) & (at < size_z + edge)

    pl.when(inside(local_spot, 0))(lambda: add_spot(src_new))
    pl.when(inside(local_plane, 0))(lambda: add_plane(rec_new))
    if halo is not None:
        here = inside(local_spot, reach) & jnp.logical_not(inside(local_spot, 0))
        pl.when(here)(lambda: add_spot(halo[0]))
        here = inside(local_plane, reach) & jnp.logical_not(inside(local_plane, 0))
        pl.when(here)(lambda: add_plane(halo[1]))


def first_interior_kernel(src, src_old, rec, rec_old, src_lap, src_base, rec_lap, rec_base, halo_mat):
    odd = lax.rem(lax.axis_index("slab"), 2) == 1
    to_y = along_y_matrix(src.shape[2])
    halo_mat[...] = halo_matrix(src.shape[1], odd)
    for now, old, lap, out in (
        (src, src_old, src_lap, src_base),
        (rec, rec_old, rec_lap, rec_base),
    ):
        for base in range(0, src.shape[0], WHOLE):
            at = pl.ds(base, WHOLE)
            total, centre = inner_sums(now, base, to_y)
            lap[at] = total
            out[at] = 2.0 * centre - old[at]


def wide_interior_kernel(now, src_old, rec_old, rate, far, near, base, old_halo):
    odd = lax.rem(lax.axis_index("slab"), 2) == 1
    mine = jnp.where(odd, 0, 1)
    size_x = src_old.shape[0]
    to_y = along_y_matrix(src_old.shape[2])
    for f, old in enumerate((src_old, rec_old)):
        for start in range(0, size_x, WHOLE):
            at, own = pl.ds(f * size_x + start, WHOLE), pl.ds(start, WHOLE)
            total, centre = flat_sums(around(now.at[pl.ds(f * size_x, size_x)], start), to_y)
            base[at] = 2.0 * centre - old[own] + rate[own] * total
            packed = pl.ds((f * size_x + start) // 2, WHOLE // 2)
            from_far, from_near = far[packed], near[mine, packed]
            left = jnp.where(odd, from_near, from_far)
            right = jnp.where(odd, from_far, from_near)
            old_halo[at] = unpack_pairs(left, right)


def interior_kernel(now, src_old, rec_old, older, rate, base, partial):
    size_x = src_old.shape[0]
    to_y = along_y_matrix(src_old.shape[2])
    for f, old in enumerate((src_old, rec_old)):
        field = now.at[pl.ds(f * size_x, size_x)]
        for start in range(0, size_x, WHOLE):
            at, own = pl.ds(f * size_x + start, WHOLE), pl.ds(start, WHOLE)
            total, centre = inner_sums(field, start, to_y)
            base[at] = 2.0 * centre - old[own] + rate[own] * total
    for start in range(0, size_x, WHOLE):
        at, other = pl.ds(start, WHOLE), pl.ds(size_x + start, WHOLE)
        partial[at] = now[at] * older[other] + src_old[at] * rec_old[at] + older[at] * now[other]


def place_of(tiles, shot, k):
    owner = lax.shift_right_logical(tiles[shot, k], 3)
    before = lax.shift_right_logical(tiles[shot, max(k - 1, 0)], 3)
    slot = (before == owner).astype(jnp.int32) if k else jnp.int32(0)
    return owner, pl.ds(slot * BX, BX)


def halo_sums(f, start, far, near, mine, halo_mat, shape):
    size_x, size_z, size_y = shape
    span = WHOLE // 2
    groups = []
    for g in range(2):
        at = pl.ds((f * size_x + start) // 2 + g * span, span)
        both = jnp.concatenate([far[at], near[mine, at]], axis=0)
        groups.append(both.reshape(2 * span * size_z, size_y))
    lines = split(jnp.concatenate(groups, axis=1), 0)
    sums = jnp.dot(halo_mat[...], lines, preferred_element_type=jnp.float32)
    halves = [sums[:, g * size_y : (g + 1) * size_y] for g in range(2)]
    return jnp.concatenate([h.reshape(WHOLE, size_z, size_y) for h in halves], axis=0)


def first_kernel(
    tiles, wavelet, spot_x, spot_z, spot_y, depth, traces, far, near, halo_mat,
    src_base, rec_base, src_lap, rec_lap, vel_got,
    rate, to_far, to_near, plane_rows,
):
    shot, slab = lax.axis_index("shot"), lax.axis_index("slab")
    odd = lax.rem(slab, 2) == 1
    mine = jnp.where(odd, 0, 1)
    shape = src_base.shape
    size_x = shape[0]
    for k in range(KT):
        owner, at = place_of(tiles, shot, k)
        block = vel_got[owner, at]
        rate[pl.ds(k * BX, BX)] = block * block * (1.0 / SCALE)
    for f, (base, lap) in enumerate(((src_base, src_lap), (rec_base, rec_lap))):
        for start in range(0, size_x, 2 * WHOLE):
            at = pl.ds(start, 2 * WHOLE)
            total = lap[at] + halo_sums(f, start, far, near, mine, halo_mat, shape)
            to_far[pl.ds(f * size_x + start, 2 * WHOLE)] = base[at] + rate[at] * total
    new = [to_far.at[pl.ds(f * size_x, size_x)] for f in range(2)]
    spots = (wavelet, spot_x, spot_z, spot_y, depth, traces)
    add_sources(0, new, spots, plane_rows, slab, shot)
    to_near[pl.ds(0, 2 * size_x)] = to_far[pl.ds(0, 2 * size_x)]
    for start in range(0, size_x, WHOLE):
        packed = pl.ds(2 * size_x + start // 2, WHOLE // 2)
        pack_pairs(rate[pl.ds(start, WHOLE)], to_far, to_near, packed, odd)


def wide_kernel(
    wavelet, spot_x, spot_z, spot_y, depth, traces, far, near, now, base, old_halo, rate,
    src_mid, rec_mid, new, to_far, to_near, halo_now, halo_mid, plane_rows,
):
    shot, slab = lax.axis_index("shot"), lax.axis_index("slab")
    odd = lax.rem(slab, 2) == 1
    size_x, size_z, size_y = src_mid.shape
    to_y = along_y_matrix(size_y)
    from_near = (rows_of((1, size_z, size_y)) < REACH) != odd
    for start in range(0, 2 * size_x, WHOLE):
        at = pl.ds(start, WHOLE)
        halo_now[at] = jnp.where(from_near, near[at], far[at])
    for f, mid in enumerate((src_mid, rec_mid)):
        halo_field = halo_now.at[pl.ds(f * size_x, size_x)]
        for start in range(0, size_x, WHOLE):
            at, own_at = pl.ds(f * size_x + start, WHOLE), pl.ds(start, WHOLE)
            total, halo = flat_sums(around(halo_field, start), to_y)
            own = now[at]
            mid[own_at] = base[at] + rate[own_at] * own_depth_sums(own, halo)
            outer = jnp.where(from_near, far[at], near[at])
            total += halo_depth_sums(own, halo, outer)
            packed = pl.ds(2 * size_x + start // 2, WHOLE // 2)
            rate_far, rate_near = far[packed], near[packed]
            left = jnp.where(odd, rate_near, rate_far)
            right = jnp.where(odd, rate_far, rate_near)
            halo_mid[at] = 2.0 * halo - old_halo[at] + unpack_pairs(left, right) * total
    spots = (wavelet, spot_x, spot_z, spot_y, depth, traces)
    halves = [halo_mid.at[pl.ds(f * size_x, size_x)] for f in range(2)]
    add_sources(1, (src_mid, rec_mid), spots, plane_rows, slab, shot, halves)
    for f, mid in enumerate((src_mid, rec_mid)):
        for start in range(0, size_x, WHOLE):
            at, own_at = pl.ds(f * size_x + start, WHOLE), pl.ds(start, WHOLE)
            total, centre = flat_sums(around(mid, start), to_y)
            total += own_depth_sums(centre, halo_mid[at])
            new[at] = 2.0 * centre - now[at] + rate[own_at] * total
    fields = [new.at[pl.ds(f * size_x, size_x)] for f in range(2)]
    add_sources(2, fields, spots, plane_rows, slab, shot)
    for start in range(0, 2 * size_x, WHOLE):
        packed = pl.ds(start // 2, WHOLE // 2)
        pack_pairs(new[pl.ds(start, WHOLE)], to_far, to_near, packed, odd)


def last_kernel(
    tiles, wavelet, spot_x, spot_z, spot_y, depth, traces, far, near, halo_mat,
    base, rate, partial, src_first, rec_first,
    src_new, rec_new, send, plane_rows,
):
    shot, slab = lax.axis_index("shot"), lax.axis_index("slab")
    mine = jnp.where(lax.rem(slab, 2) == 1, 0, 1)
    shape = src_new.shape
    size_x = shape[0]
    for f, new in enumerate((src_new, rec_new)):
        for start in range(0, size_x, 2 * WHOLE):
            at = pl.ds(start, 2 * WHOLE)
            total = halo_sums(f, start, far, near, mine, halo_mat, shape)
            new[at] = base[pl.ds(f * size_x + start, 2 * WHOLE)] + rate[at] * total
    spots = (wavelet, spot_x, spot_z, spot_y, depth, traces)
    add_sources(STEPS - 1, (src_new, rec_new), spots, plane_rows, slab, shot)
    send[...] = jnp.zeros(send.shape, jnp.float32)
    for k in range(KT):
        owner, slot = place_of(tiles, shot, k)
        at = pl.ds(k * BX, BX)
        image = partial[at] + src_new[at] * rec_first[at] + src_first[at] * rec_new[at]
        send[owner, slot] = image


def gather_kernel(tiles, got, src, rec, out, src_out, rec_out, total, sems):
    shot = lax.axis_index("shot")
    copies = [
        pltpu.make_async_copy(src, src_out, sems.at[0]),
        pltpu.make_async_copy(rec, rec_out, sems.at[1]),
    ]
    for copy in copies:
        copy.start()
    total[...] = jnp.zeros(total.shape, jnp.float32)
    for g in range(got.shape[0]):
        before = jnp.int32(0)
        for k in range(KT):
            before += (tiles[g, k] < shot * BX).astype(jnp.int32)
        for j in range(CAP):
            k = jnp.minimum(before + j, KT - 1)
            own = jnp.clip(tiles[g, k] - shot * BX, 0, total.shape[0] // BX - 1)
            total[pl.ds(own * BX, BX)] += got[g, pl.ds(j * BX, BX)]
    copies.append(pltpu.make_async_copy(total, out, sems.at[2]))
    copies[2].start()
    for copy in copies:
        copy.wait()


def local(
    src_prev,
    src_cur,
    rec_cur,
    rec_next,
    velocity,
    aperture_tiles,
    wavelet,
    src_x,
    src_z,
    src_y,
    rec_depth,
    rec_data,
):
    slabs = lax.axis_size("slab")
    shots = lax.axis_size("shot")
    far_pairs = []
    for i in range(1, slabs - 1, 2):
        far_pairs += [(i, i + 1), (i + 1, i)]
    near_groups = [[i, i + 1] for i in range(0, slabs, 2)]
    near_pairs = [(i, i ^ 1) for i in range(slabs)]

    def exchange(to_far, to_near):
        far = lax.ppermute(to_far, "slab", far_pairs)
        near = lax.all_gather(to_near, "slab", axis_index_groups=near_groups)
        return far, near

    src_old, rec_old = src_prev[0], rec_next[0]
    block = src_old.shape
    both = (2 * block[0],) + block[1:]
    wide = (2 * block[0] + block[0] // 2,) + block[1:]
    buffer = (shots, CAP * BX) + block[1:]
    dma = pltpu.SemaphoreType.DMA
    rows = VMEM((block[0], block[2]), jnp.float32)
    cost = dict(flops=2 * 45 * src_old.size, bytes_accessed=8 * 4 * src_old.size)
    given = (aperture_tiles, velocity, src_cur[0], rec_cur[0])
    send, to_far, to_near, src, rec, tiles = call(
        pack_kernel,
        [buffer, block, block, block, block, (aperture_tiles.shape, VMEM, jnp.int32)],
        [pltpu.HBM] * 4, *[pltpu.with_memory_space_constraint(a, pltpu.HBM) for a in given],
        scratch=[
            VMEM(velocity.shape, jnp.float32),
            SMEM(aperture_tiles.shape, jnp.int32),
            dma((5,)),
        ],
    )
    spots = (wavelet, src_x, src_z, src_y, rec_depth, rec_data[0])

    vel_got = lax.all_to_all(send, "shot", 0, 0)
    far, near = exchange(to_far, to_near)
    src_lap, src_base, rec_lap, rec_base, halo_mat = call(
        first_interior_kernel,
        [block] * 4 + [((WHOLE * block[1], 4 * WHOLE * REACH), VMEM, jnp.bfloat16)],
        [VMEM] * 4, src, src_old, rec, rec_old, **cost,
    )
    rate, now, now_near = call(
        first_kernel, [block, wide, wide], [SMEM] * 6 + [VMEM] * 9,
        tiles, *spots, far, near, halo_mat, src_base, rec_base, src_lap, rec_lap, vel_got,
        scratch=[rows], **cost,
    )

    wide_far = lax.ppermute(now, "slab", far_pairs)
    wide_near = lax.ppermute(now_near, "slab", near_pairs)
    base, old_halo = call(
        wide_interior_kernel, [both] * 2, [VMEM] * 6, now, src, rec, rate, far, near, **cost
    )
    src_mid, rec_mid, new, to_far, to_near = call(
        wide_kernel, [block, block, both, block, block], [SMEM] * 5 + [VMEM] * 7,
        *spots, wide_far, wide_near, now, base, old_halo, rate,
        scratch=[VMEM(both, jnp.float32), VMEM(both, jnp.float32), rows], **cost,
    )

    far, near = exchange(to_far, to_near)
    base, partial = call(
        interior_kernel, [both, block], [VMEM] * 5, new, src_mid, rec_mid, now, rate, **cost
    )
    src, rec, send = call(
        last_kernel, [block, block, buffer], [SMEM] * 6 + [VMEM] * 9,
        tiles, *spots, far, near, halo_mat, base, rate, partial, src, rec,
        scratch=[rows], **cost,
    )
    image_got = lax.all_to_all(send, "shot", 0, 0)
    image, src, rec = call(
        gather_kernel,
        [(velocity.shape, pltpu.HBM), (block, pltpu.HBM), (block, pltpu.HBM)],
        [SMEM] + [VMEM] * 3, tiles, image_got, src, rec,
        scratch=[VMEM(velocity.shape, jnp.float32), dma((3,))],
    )
    return image, src[None], rec[None]


def solution(mesh):
    wave = P("shot", None, "slab", None)
    model = P("shot", "slab", None)
    return jax.shard_map(
        local,
        mesh=mesh,
        in_specs=(wave,) * 4 + (model,) + (P(),) * 6 + (P("shot", None, None, None),),
        out_specs=(model, wave, wave),
        check_vma=False,
    )
```

```python
import jax
import jax.numpy as jnp
from jax import lax
from jax.experimental import pallas as pl
from jax.experimental.pallas import tpu as pltpu
from jax.sharding import PartitionSpec as P

BX = 8
KT = 8
STEPS = 4
CAP = 2
REACH = 4
CHUNK = 8
VMEM = pltpu.VMEM
SMEM = pltpu.SMEM


SCALE = 5040.0
TAPS = (-43050.0, 8064.0, -1008.0, 128.0, -9.0)
WHOLE = 16


def call(body, outs, in_spaces, *args, scratch=(), flops=0, bytes_accessed=0):
    outs = [o if isinstance(o, tuple) and isinstance(o[0], tuple) else (o, VMEM) for o in outs]
    outs = [o if len(o) == 3 else o + (jnp.float32,) for o in outs]
    return pl.pallas_call(
        body,
        out_shape=[jax.ShapeDtypeStruct(s, t) for s, _, t in outs],
        in_specs=[pl.BlockSpec(memory_space=s) for s in in_spaces],
        out_specs=[pl.BlockSpec(memory_space=m) for _, m, _ in outs],
        scratch_shapes=list(scratch),
        compiler_params=pltpu.CompilerParams(vmem_limit_bytes=24 * 1024 * 1024),
        cost_estimate=pl.CostEstimate(
            flops=flops, bytes_accessed=bytes_accessed, transcendentals=0
        ),
    )(*args)


def rows_of(shape):
    return lax.broadcasted_iota(jnp.int32, shape, len(shape) - 2)


def pack_pairs(field, to_far, to_near, at, odd):
    pairs = field.reshape(field.shape[0] // 2, 2, 8, field.shape[2])
    first, second = pairs[:, 0], pairs[:, 1]
    top = rows_of(first.shape) < REACH
    low = jnp.where(top, first, pltpu.roll(second, REACH, 1))
    high = jnp.where(top, pltpu.roll(first, REACH, 1), second)
    if to_far is not None:
        to_far[at] = jnp.where(odd, high, low)
    if to_near is not None:
        to_near[at] = jnp.where(odd, low, high)


def pack_kernel(
    tiles_in, vel_in, src_in, rec_in, x_in, z_in, y_in, depth_in,
    send, to_far, to_near, src, rec, tiles_out, x_out, z_out, y_out, depth_out, vel, tiles, sems,
):
    shot = lax.axis_index("shot")
    odd = lax.rem(lax.axis_index("slab"), 2) == 1
    moves = [(src_in, src), (rec_in, rec), (tiles_in, tiles), (tiles_in, tiles_out), (vel_in, vel)]
    moves += [(x_in, x_out), (z_in, z_out), (y_in, y_out), (depth_in, depth_out)]
    copies = [pltpu.make_async_copy(a, b, sems.at[i]) for i, (a, b) in enumerate(moves)]
    for copy in copies:
        copy.start()
    half = src.shape[0] // 2
    for f, field in enumerate((src, rec)):
        copies[f].wait()

        def one_chunk(c, _):
            at = pl.ds(f * half + c * (CHUNK // 2), CHUNK // 2)
            pack_pairs(field[pl.ds(c * CHUNK, CHUNK)], to_far, to_near, at, odd)
            return 0

        lax.fori_loop(0, field.shape[0] // CHUNK, one_chunk, 0)
    for copy in copies[2:]:
        copy.wait()
    n_shot = send.shape[0]

    def one_shot(g, _):
        before = jnp.int32(0)
        for k in range(KT):
            before += (tiles[g, k] < shot * BX).astype(jnp.int32)
        for j in range(CAP):
            k = jnp.minimum(before + j, KT - 1)
            own = jnp.clip(tiles[g, k] - shot * BX, 0, vel.shape[0] // BX - 1)
            send[g, pl.ds(j * BX, BX)] = vel[pl.ds(own * BX, BX)]
        return 0

    lax.fori_loop(0, n_shot, one_shot, 0)


def tap_of(reach):
    weight = jnp.zeros(reach.shape, jnp.float32)
    for r in range(1, REACH + 1):
        weight = jnp.where(reach == r, TAPS[r], weight)
    return weight


def split(values, axis):
    high = values.astype(jnp.bfloat16)
    low = (values - high.astype(jnp.float32)).astype(jnp.bfloat16)
    return jnp.concatenate([high, low], axis=axis)


def along_y_matrix(size_y):
    shape = (2 * size_y, size_y)
    row = lax.rem(lax.broadcasted_iota(jnp.int32, shape, 0), size_y)
    return tap_of(jnp.abs(row - lax.broadcasted_iota(jnp.int32, shape, 1))).astype(jnp.bfloat16)


def halo_matrix(size_z, odd):
    rows, packed = WHOLE * size_z, WHOLE * REACH
    shape = (rows, 2 * packed)
    out = lax.broadcasted_iota(jnp.int32, shape, 0)
    at = lax.broadcasted_iota(jnp.int32, shape, 1)
    x, z = out // size_z, lax.rem(out, size_z)
    inner = lax.rem(at, packed)
    x_at, plane = inner // REACH, lax.rem(inner, REACH)
    left = (at < packed) != odd
    reach = jnp.where(left, z + REACH - plane, size_z + plane - z)
    weight = jnp.where(x == x_at, tap_of(reach), 0.0).astype(jnp.bfloat16)
    return jnp.concatenate([weight, weight], axis=1)


def around(field, base):
    size_x = field.shape[0]
    low, high = max(base - REACH, 0), min(base + WHOLE + REACH, size_x)
    wide = field[pl.ds(low, high - low)]
    zeros = jnp.zeros((REACH,) + field.shape[1:], jnp.float32)
    if base - REACH < 0:
        wide = jnp.concatenate([zeros, wide], axis=0)
    if base + WHOLE + REACH > size_x:
        wide = jnp.concatenate([wide, zeros], axis=0)
    return wide


def flat_sums(wide, to_y):
    centre = wide[REACH : REACH + WHOLE]
    lines = split(centre.reshape(-1, centre.shape[2]), 1)
    total = jnp.dot(lines, to_y, preferred_element_type=jnp.float32)
    total = total.reshape(centre.shape) + TAPS[0] * centre
    for r in range(1, REACH + 1):
        terms = wide[REACH + r : REACH + r + WHOLE] + wide[REACH - r : REACH - r + WHOLE]
        total += TAPS[r] * terms
    return total, centre


def up_down(up, down, r):
    size_z = up.shape[1]
    return pltpu.roll(up, size_z - r, 1) + pltpu.roll(down, r, 1)


def own_depth_sums(own, halo):
    size_z = own.shape[1]
    row = rows_of((1,) + own.shape[1:])
    total = 0.0
    for r in range(1, REACH + 1):
        up = jnp.where(row < r, halo, own)
        down = jnp.where(row >= size_z - r, halo, own)
        total += TAPS[r] * up_down(up, down, r)
    return total


def halo_depth_sums(own, halo, outer):
    size_z = own.shape[1]
    row = rows_of((1,) + own.shape[1:])
    top = row < REACH
    above, below = jnp.where(top, own, outer), jnp.where(top, outer, own)
    total = 0.0
    for r in range(1, REACH + 1):
        up_same = (lax.rem(row + size_z - r, size_z) < REACH) == top
        down_same = (lax.rem(row + r, size_z) < REACH) == top
        up, down = jnp.where(up_same, halo, above), jnp.where(down_same, halo, below)
        total += TAPS[r] * up_down(up, down, r)
    return total


def inner_sums(field, base, to_y):
    total, centre = flat_sums(around(field, base), to_y)
    return total + own_depth_sums(centre, jnp.zeros((1,) + centre.shape[1:], jnp.float32)), centre


def unpack_pairs(left, right):
    top = rows_of((1,) + left.shape[1:]) < REACH
    even_x = jnp.where(top, right, pltpu.roll(left, REACH, 1))
    odd_x = jnp.where(top, pltpu.roll(right, REACH, 1), left)
    pairs = jnp.stack([even_x, odd_x], axis=1)
    return pairs.reshape((2 * left.shape[0],) + left.shape[1:])


def add_sources(step, new, spots, plane_rows, slab, shot, halo=None):
    wavelet, spot_x, spot_z, spot_y, depth, traces = spots
    src_new, rec_new = new
    size_x, size_z, size_y = src_new.shape
    row = lax.broadcasted_iota(jnp.int32, (size_z, size_y), 0)
    lane = lax.broadcasted_iota(jnp.int32, (size_z, size_y), 1)
    reach = 0 if halo is None else REACH
    local_spot = spot_z[shot] - slab * size_z
    local_plane = depth[shot] - slab * size_z
    at_spot = lax.rem(local_spot + size_z, size_z)
    at_plane = lax.rem(local_plane + size_z, size_z)

    def add_spot(field):
        x = spot_x[shot]
        here = (row == at_spot) & (lane == spot_y[shot])
        field[x] += jnp.where(here, wavelet[shot, step], 0.0)

    def add_plane(field):
        plane_rows[...] = traces[STEPS - 1 - step].astype(jnp.float32)

        def one_x(x, _):
            line = plane_rows[pl.ds(x, 1)]
            field[x] += jnp.where(row == at_plane, line, 0.0)
            return 0

        lax.fori_loop(0, size_x, one_x, 0, unroll=8)

    def inside(at, edge):
        return (at >= -edge) & (at < size_z + edge)

    pl.when(inside(local_spot, 0))(lambda: add_spot(src_new))
    pl.when(inside(local_plane, 0))(lambda: add_plane(rec_new))
    if halo is not None:
        here = inside(local_spot, reach) & jnp.logical_not(inside(local_spot, 0))
        pl.when(here)(lambda: add_spot(halo[0]))
        here = inside(local_plane, reach) & jnp.logical_not(inside(local_plane, 0))
        pl.when(here)(lambda: add_plane(halo[1]))


def first_interior_kernel(src, src_old, rec, rec_old, src_lap, src_base, rec_lap, rec_base, halo_mat):
    odd = lax.rem(lax.axis_index("slab"), 2) == 1
    to_y = along_y_matrix(src.shape[2])
    halo_mat[...] = halo_matrix(src.shape[1], odd)
    for now, old, lap, out in (
        (src, src_old, src_lap, src_base),
        (rec, rec_old, rec_lap, rec_base),
    ):
        for base in range(0, src.shape[0], WHOLE):
            at = pl.ds(base, WHOLE)
            total, centre = inner_sums(now, base, to_y)
            lap[at] = total
            out[at] = 2.0 * centre - old[at]


def wide_interior_kernel(now, src_old, rec_old, rate, far, near, base, old_halo, to_near):
    odd = lax.rem(lax.axis_index("slab"), 2) == 1
    mine = jnp.where(odd, 0, 1)
    size_x = src_old.shape[0]
    to_y = along_y_matrix(src_old.shape[2])
    to_near[pl.ds(0, 2 * size_x)] = now[pl.ds(0, 2 * size_x)]
    for start in range(0, size_x, WHOLE):
        packed = pl.ds(2 * size_x + start // 2, WHOLE // 2)
        pack_pairs(rate[pl.ds(start, WHOLE)], None, to_near, packed, odd)
    for f, old in enumerate((src_old, rec_old)):
        for start in range(0, size_x, WHOLE):
            at, own = pl.ds(f * size_x + start, WHOLE), pl.ds(start, WHOLE)
            total, centre = flat_sums(around(now.at[pl.ds(f * size_x, size_x)], start), to_y)
            base[at] = 2.0 * centre - old[own] + rate[own] * total
            packed = pl.ds((f * size_x + start) // 2, WHOLE // 2)
            from_far, from_near = far[packed], near[mine, packed]
            left = jnp.where(odd, from_near, from_far)
            right = jnp.where(odd, from_far, from_near)
            old_halo[at] = unpack_pairs(left, right)


def interior_kernel(now, src_old, rec_old, older, rate, base, partial):
    size_x = src_old.shape[0]
    to_y = along_y_matrix(src_old.shape[2])
    for f, old in enumerate((src_old, rec_old)):
        field = now.at[pl.ds(f * size_x, size_x)]
        for start in range(0, size_x, WHOLE):
            at, own = pl.ds(f * size_x + start, WHOLE), pl.ds(start, WHOLE)
            total, centre = inner_sums(field, start, to_y)
            base[at] = 2.0 * centre - old[own] + rate[own] * total
    for start in range(0, size_x, WHOLE):
        at, other = pl.ds(start, WHOLE), pl.ds(size_x + start, WHOLE)
        partial[at] = now[at] * older[other] + src_old[at] * rec_old[at] + older[at] * now[other]


def place_of(tiles, shot, k):
    owner = lax.shift_right_logical(tiles[shot, k], 3)
    before = lax.shift_right_logical(tiles[shot, max(k - 1, 0)], 3)
    slot = (before == owner).astype(jnp.int32) if k else jnp.int32(0)
    return owner, pl.ds(slot * BX, BX)


def halo_sums(f, start, far, near, mine, halo_mat, shape):
    size_x, size_z, size_y = shape
    span = WHOLE // 2
    groups = []
    for g in range(2):
        at = pl.ds((f * size_x + start) // 2 + g * span, span)
        both = jnp.concatenate([far[at], near[mine, at]], axis=0)
        groups.append(both.reshape(2 * span * size_z, size_y))
    lines = split(jnp.concatenate(groups, axis=1), 0)
    sums = jnp.dot(halo_mat[...], lines, preferred_element_type=jnp.float32)
    halves = [sums[:, g * size_y : (g + 1) * size_y] for g in range(2)]
    return jnp.concatenate([h.reshape(WHOLE, size_z, size_y) for h in halves], axis=0)


def first_kernel(
    tiles, wavelet, spot_x, spot_z, spot_y, depth, traces, far, near, halo_mat,
    src_base, rec_base, src_lap, rec_lap, vel_got,
    rate, to_far, plane_rows,
):
    shot, slab = lax.axis_index("shot"), lax.axis_index("slab")
    odd = lax.rem(slab, 2) == 1
    mine = jnp.where(odd, 0, 1)
    shape = src_base.shape
    size_x = shape[0]
    for k in range(KT):
        owner, at = place_of(tiles, shot, k)
        block = vel_got[owner, at]
        rate[pl.ds(k * BX, BX)] = block * block * (1.0 / SCALE)
    for f, (base, lap) in enumerate(((src_base, src_lap), (rec_base, rec_lap))):
        for start in range(0, size_x, 2 * WHOLE):
            at = pl.ds(start, 2 * WHOLE)
            total = lap[at] + halo_sums(f, start, far, near, mine, halo_mat, shape)
            to_far[pl.ds(f * size_x + start, 2 * WHOLE)] = base[at] + rate[at] * total
    new = [to_far.at[pl.ds(f * size_x, size_x)] for f in range(2)]
    spots = (wavelet, spot_x, spot_z, spot_y, depth, traces)
    add_sources(0, new, spots, plane_rows, slab, shot)
    for start in range(0, size_x, WHOLE):
        packed = pl.ds(2 * size_x + start // 2, WHOLE // 2)
        pack_pairs(rate[pl.ds(start, WHOLE)], to_far, None, packed, odd)


def wide_kernel(
    wavelet, spot_x, spot_z, spot_y, depth, traces, far, near, now, base, old_halo, rate,
    src_mid, rec_mid, new, to_far, to_near, halo_now, halo_mid, plane_rows,
):
    shot, slab = lax.axis_index("shot"), lax.axis_index("slab")
    odd = lax.rem(slab, 2) == 1
    size_x, size_z, size_y = src_mid.shape
    to_y = along_y_matrix(size_y)
    from_near = (rows_of((1, size_z, size_y)) < REACH) != odd
    for start in range(0, 2 * size_x, WHOLE):
        at = pl.ds(start, WHOLE)
        halo_now[at] = jnp.where(from_near, near[at], far[at])
    for f, mid in enumerate((src_mid, rec_mid)):
        halo_field = halo_now.at[pl.ds(f * size_x, size_x)]
        for start in range(0, size_x, WHOLE):
            at, own_at = pl.ds(f * size_x + start, WHOLE), pl.ds(start, WHOLE)
            total, halo = flat_sums(around(halo_field, start), to_y)
            own = now[at]
            mid[own_at] = base[at] + rate[own_at] * own_depth_sums(own, halo)
            outer = jnp.where(from_near, far[at], near[at])
            total += halo_depth_sums(own, halo, outer)
            packed = pl.ds(2 * size_x + start // 2, WHOLE // 2)
            rate_far, rate_near = far[packed], near[packed]
            left = jnp.where(odd, rate_near, rate_far)
            right = jnp.where(odd, rate_far, rate_near)
            halo_mid[at] = 2.0 * halo - old_halo[at] + unpack_pairs(left, right) * total
    spots = (wavelet, spot_x, spot_z, spot_y, depth, traces)
    halves = [halo_mid.at[pl.ds(f * size_x, size_x)] for f in range(2)]
    add_sources(1, (src_mid, rec_mid), spots, plane_rows, slab, shot, halves)
    for f, mid in enumerate((src_mid, rec_mid)):
        for start in range(0, size_x, WHOLE):
            at, own_at = pl.ds(f * size_x + start, WHOLE), pl.ds(start, WHOLE)
            total, centre = flat_sums(around(mid, start), to_y)
            total += own_depth_sums(centre, halo_mid[at])
            new[at] = 2.0 * centre - now[at] + rate[own_at] * total
    fields = [new.at[pl.ds(f * size_x, size_x)] for f in range(2)]
    add_sources(2, fields, spots, plane_rows, slab, shot)
    for start in range(0, 2 * size_x, WHOLE):
        packed = pl.ds(start // 2, WHOLE // 2)
        pack_pairs(new[pl.ds(start, WHOLE)], to_far, to_near, packed, odd)


def last_kernel(
    tiles, wavelet, spot_x, spot_z, spot_y, depth, traces, far, near, halo_mat,
    base, rate, partial, src_first, rec_first,
    src_new, rec_new, send, plane_rows,
):
    shot, slab = lax.axis_index("shot"), lax.axis_index("slab")
    mine = jnp.where(lax.rem(slab, 2) == 1, 0, 1)
    shape = src_new.shape
    size_x = shape[0]
    for f, new in enumerate((src_new, rec_new)):
        for start in range(0, size_x, 2 * WHOLE):
            at = pl.ds(start, 2 * WHOLE)
            total = halo_sums(f, start, far, near, mine, halo_mat, shape)
            new[at] = base[pl.ds(f * size_x + start, 2 * WHOLE)] + rate[at] * total
    spots = (wavelet, spot_x, spot_z, spot_y, depth, traces)
    add_sources(STEPS - 1, (src_new, rec_new), spots, plane_rows, slab, shot)
    send[...] = jnp.zeros(send.shape, jnp.float32)
    for k in range(KT):
        owner, slot = place_of(tiles, shot, k)
        at = pl.ds(k * BX, BX)
        image = partial[at] + src_new[at] * rec_first[at] + src_first[at] * rec_new[at]
        send[owner, slot] = image


def gather_kernel(tiles, got, src, rec, out, src_out, rec_out, total, sems):
    shot = lax.axis_index("shot")
    copies = [
        pltpu.make_async_copy(src, src_out, sems.at[0]),
        pltpu.make_async_copy(rec, rec_out, sems.at[1]),
    ]
    for copy in copies:
        copy.start()
    total[...] = jnp.zeros(total.shape, jnp.float32)
    for g in range(got.shape[0]):
        before = jnp.int32(0)
        for k in range(KT):
            before += (tiles[g, k] < shot * BX).astype(jnp.int32)
        for j in range(CAP):
            k = jnp.minimum(before + j, KT - 1)
            own = jnp.clip(tiles[g, k] - shot * BX, 0, total.shape[0] // BX - 1)
            total[pl.ds(own * BX, BX)] += got[g, pl.ds(j * BX, BX)]
    copies.append(pltpu.make_async_copy(total, out, sems.at[2]))
    copies[2].start()
    for copy in copies:
        copy.wait()


def local(
    src_prev,
    src_cur,
    rec_cur,
    rec_next,
    velocity,
    aperture_tiles,
    wavelet,
    src_x,
    src_z,
    src_y,
    rec_depth,
    rec_data,
):
    slabs = lax.axis_size("slab")
    shots = lax.axis_size("shot")
    far_pairs = []
    for i in range(1, slabs - 1, 2):
        far_pairs += [(i, i + 1), (i + 1, i)]
    near_groups = [[i, i + 1] for i in range(0, slabs, 2)]
    near_pairs = [(i, i ^ 1) for i in range(slabs)]

    def exchange(to_far, to_near):
        far = lax.ppermute(to_far, "slab", far_pairs)
        near = lax.all_gather(to_near, "slab", axis_index_groups=near_groups)
        return far, near

    src_old, rec_old = src_prev[0], rec_next[0]
    block = src_old.shape
    both = (2 * block[0],) + block[1:]
    wide = (2 * block[0] + block[0] // 2,) + block[1:]
    buffer = (shots, CAP * BX) + block[1:]
    dma = pltpu.SemaphoreType.DMA
    rows = VMEM((block[0], block[2]), jnp.float32)
    cost = dict(flops=2 * 45 * src_old.size, bytes_accessed=8 * 4 * src_old.size)
    given = (aperture_tiles, velocity, src_cur[0], rec_cur[0], src_x, src_z, src_y, rec_depth)
    whole_numbers = [(a.shape, VMEM, jnp.int32) for a in (aperture_tiles, *given[4:])]
    send, to_far, to_near, src, rec, tiles, *places = call(
        pack_kernel, [buffer, block, block, block, block] + whole_numbers,
        [pltpu.HBM] * 8, *[pltpu.with_memory_space_constraint(a, pltpu.HBM) for a in given],
        scratch=[
            VMEM(velocity.shape, jnp.float32),
            SMEM(aperture_tiles.shape, jnp.int32),
            dma((9,)),
        ],
    )
    spots = (wavelet, *places, rec_data[0])

    vel_got = lax.all_to_all(send, "shot", 0, 0)
    far, near = exchange(to_far, to_near)
    src_lap, src_base, rec_lap, rec_base, halo_mat = call(
        first_interior_kernel,
        [block] * 4 + [((WHOLE * block[1], 4 * WHOLE * REACH), VMEM, jnp.bfloat16)],
        [VMEM] * 4, src, src_old, rec, rec_old, **cost,
    )
    rate, now = call(
        first_kernel, [block, wide], [SMEM] * 6 + [VMEM] * 9,
        tiles, *spots, far, near, halo_mat, src_base, rec_base, src_lap, rec_lap, vel_got,
        scratch=[rows], **cost,
    )

    wide_far = lax.ppermute(now, "slab", far_pairs)
    base, old_halo, now_near = call(
        wide_interior_kernel, [both, both, wide], [VMEM] * 6, now, src, rec, rate, far, near, **cost
    )
    wide_near = lax.ppermute(now_near, "slab", near_pairs)
    src_mid, rec_mid, new, to_far, to_near = call(
        wide_kernel, [block, block, both, block, block], [SMEM] * 5 + [VMEM] * 7,
        *spots, wide_far, wide_near, now, base, old_halo, rate,
        scratch=[VMEM(both, jnp.float32), VMEM(both, jnp.float32), rows], **cost,
    )

    far, near = exchange(to_far, to_near)
    base, partial = call(
        interior_kernel, [both, block], [VMEM] * 5, new, src_mid, rec_mid, now, rate, **cost
    )
    src, rec, send = call(
        last_kernel, [block, block, buffer], [SMEM] * 6 + [VMEM] * 9,
        tiles, *spots, far, near, halo_mat, base, rate, partial, src, rec,
        scratch=[rows], **cost,
    )
    image_got = lax.all_to_all(send, "shot", 0, 0)
    image, src, rec = call(
        gather_kernel,
        [(velocity.shape, pltpu.HBM), (block, pltpu.HBM), (block, pltpu.HBM)],
        [SMEM] + [VMEM] * 3, tiles, image_got, src, rec,
        scratch=[VMEM(velocity.shape, jnp.float32), dma((3,))],
    )
    return image, src[None], rec[None]


def solution(mesh):
    wave = P("shot", None, "slab", None)
    model = P("shot", "slab", None)
    return jax.shard_map(
        local,
        mesh=mesh,
        in_specs=(wave,) * 4 + (model,) + (P(),) * 6 + (P("shot", None, None, None),),
        out_specs=(model, wave, wave),
        check_vma=False,
    )
```

```python
import jax
import jax.numpy as jnp
from jax import lax
from jax.experimental import pallas as pl
from jax.experimental.pallas import tpu as pltpu
from jax.sharding import PartitionSpec as P


BX = 8
KT = 8
STEPS = 4
CAP = 2
REACH = 4
PAD = 8
VMEM = pltpu.VMEM
SMEM = pltpu.SMEM
HBM = pltpu.HBM

SCALE = 5040.0
TAPS = (-43050.0, 8064.0, -1008.0, 128.0, -9.0)


def call(body, outs, in_spaces, *args, scratch=()):
    outs = [o if isinstance(o[0], tuple) else (o, VMEM) for o in outs]
    outs = [o if len(o) == 3 else o + (jnp.float32,) for o in outs]
    size = 8 * 64 * 128
    return pl.pallas_call(
        body,
        out_shape=[jax.ShapeDtypeStruct(s, t) for s, _, t in outs],
        in_specs=[pl.BlockSpec(memory_space=s) for s in in_spaces],
        out_specs=[pl.BlockSpec(memory_space=m) for _, m, _ in outs],
        scratch_shapes=list(scratch),
        compiler_params=pltpu.CompilerParams(vmem_limit_bytes=24 * 1024 * 1024),
        cost_estimate=pl.CostEstimate(
            flops=90 * size, bytes_accessed=32 * size, transcendentals=0
        ),
    )(*args)


def is_odd():
    return lax.rem(lax.axis_index("slab"), 2) == 1


def partner():
    return jnp.where(is_odd(), 0, 1)


def z_of(plane, depth):
    return jnp.where(is_odd(), plane, depth - 1 - plane)


def tap_of(reach):
    weight = jnp.zeros(reach.shape, jnp.float32)
    for r in range(1, REACH + 1):
        weight = jnp.where(reach == r, TAPS[r], weight)
    return weight


def along_y_matrix(size_y):
    shape = (2 * size_y, size_y)
    row = lax.rem(lax.broadcasted_iota(jnp.int32, shape, 0), size_y)
    return tap_of(jnp.abs(row - lax.broadcasted_iota(jnp.int32, shape, 1))).astype(jnp.bfloat16)


def along_y(planes, to_y):
    rows = planes.reshape(-1, planes.shape[2])
    high = rows.astype(jnp.bfloat16)
    low = (rows - high.astype(jnp.float32)).astype(jnp.bfloat16)
    sums = jnp.dot(
        jnp.concatenate([high, low], axis=1), to_y, preferred_element_type=jnp.float32
    )
    return sums.reshape(planes.shape)


def clear_edges(padded):
    count, rows, size_y = padded.shape
    zeros = jnp.zeros((count, PAD, size_y), jnp.float32)
    padded[:, pl.ds(0, PAD)] = zeros
    padded[:, pl.ds(rows - PAD, PAD)] = zeros


def full_sums(padded, planes, first, plane_at, to_y):
    count, size_x, _ = planes.shape
    padded[pl.ds(0, count), pl.ds(PAD, size_x)] = planes
    lines = along_y(planes, to_y)
    sums = []
    for p in range(count):
        total = lines[p] + TAPS[0] * planes[p]
        for r in range(1, REACH + 1):
            terms = padded[p, pl.ds(PAD + r, size_x)] + padded[p, pl.ds(PAD - r, size_x)]
            for other in (plane_at(first + p + r), plane_at(first + p - r)):
                if other is not None:
                    terms += other
            total += TAPS[r] * terms
        sums.append(total)
    return sums


def beyond_sums(plane, plane_at):
    total = 0.0
    for r in range(1, REACH + 1):
        for other in (plane_at(plane + r), plane_at(plane - r)):
            if other is not None:
                total += TAPS[r] * other
    return total


def add_spot(step, fields, places, depth):
    wavelet, spot_x, spot_z, spot_y = places
    shot = lax.axis_index("shot")
    local = spot_z[shot] - lax.axis_index("slab") * depth
    plane = z_of(local, depth)
    x = spot_x[shot]
    for first, last, ref, index in fields:

        @pl.when((plane >= first) & (plane <= last))
        def _():
            row = lax.broadcasted_iota(jnp.int32, (8, ref.shape[2]), 0)
            lane = lax.broadcasted_iota(jnp.int32, (8, ref.shape[2]), 1)
            here = (row == lax.rem(x, 8)) & (lane == spot_y[shot])
            rows = pl.ds(pl.multiple_of(lax.div(x, 8) * 8, 8), 8)
            ref[index(plane), rows] += jnp.where(here, wavelet[shot, step], 0.0)


def add_traces(step, fields, depth_at, traces, depth):
    local = depth_at[lax.axis_index("shot")] - lax.axis_index("slab") * depth
    plane = z_of(local, depth)
    for first, last, ref, index in fields:

        @pl.when((plane >= first) & (plane <= last))
        def _():
            ref[index(plane)] += traces[STEPS - 1 - step].astype(jnp.float32)


def add_sources(step, src_fields, rec_fields, places, depth):
    wavelet, spot_x, spot_z, spot_y, depth_at, traces = places
    add_spot(step, src_fields, (wavelet, spot_x, spot_z, spot_y), depth)
    add_traces(step, rec_fields, depth_at, traces, depth)


def first_slot(tiles, shot, g):
    before = jnp.int32(0)
    for k in range(KT):
        before += (tiles[g, k] < shot * BX).astype(jnp.int32)
    return before


def place_of(tiles, shot, k):
    owner = lax.shift_right_logical(tiles[shot, k], 3)
    before = lax.shift_right_logical(tiles[shot, max(k - 1, 0)], 3)
    slot = (before == owner).astype(jnp.int32) if k else jnp.int32(0)
    return owner, slot


def start_kernel(
    src_in, rec_in, vel_in, tiles_in, x_in, z_in, y_in, depth_in,
    send, to_far, src, rec, tiles_out, x_out, z_out, y_out, depth_out,
    src_raw, rec_raw, vel, tiles, sems,
):
    shot = lax.axis_index("shot")
    moves = [(src_in, src_raw), (rec_in, rec_raw), (vel_in, vel), (tiles_in, tiles)]
    moves += [(tiles_in, tiles_out), (x_in, x_out), (z_in, z_out), (y_in, y_out)]
    moves += [(depth_in, depth_out)]
    copies = [pltpu.make_async_copy(a, b, sems.at[i]) for i, (a, b) in enumerate(moves)]
    for copy in copies:
        copy.start()
    depth, size_x, _ = src.shape
    for f, (raw, field) in enumerate(((src_raw, src), (rec_raw, rec))):
        copies[f].wait()
        for p in range(depth):
            plane = raw[pl.ds(z_of(p, depth), size_x, stride=depth)]
            field[p] = plane
            if p >= depth - REACH:
                to_far[f * REACH + p - (depth - REACH)] = plane
    for copy in copies[2:]:
        copy.wait()
    held = vel.shape[0] // (BX * depth)

    def one_shot(g, _):
        before = first_slot(tiles, shot, g)
        for j in range(CAP):
            k = jnp.minimum(before + j, KT - 1)
            own = jnp.clip(tiles[g, k] - shot * BX, 0, held - 1)
            for p in range(depth):
                at = own * (BX * depth) + z_of(p, depth)
                send[g, j * depth + p] = vel[pl.ds(at, BX, stride=depth)]
        return 0

    lax.fori_loop(0, send.shape[0], one_shot, 0)


def first_interior_kernel(src, rec, src_old, rec_old, to_near, sums, base, to_y, padded):
    depth, size_x, size_y = src.shape
    to_y[...] = along_y_matrix(size_y)
    clear_edges(padded)
    for f, (field, old) in enumerate(((src, src_old), (rec, rec_old))):

        def plane_at(m):
            return field[m] if 0 <= m < depth else None

        for first in range(0, depth, REACH):
            planes = field[pl.ds(first, REACH)]
            if first == 0:
                to_near[pl.ds(f * REACH, REACH)] = planes
            for i, total in enumerate(full_sums(padded, planes, first, plane_at, to_y[...])):
                p = first + i
                sums[f * depth + p] = total
                before = old[pl.ds(z_of(p, depth), size_x, stride=depth)]
                base[f * depth + p] = 2.0 * planes[i] - before


def rate_kernel(tiles, vel_got, near, sums, base, rate, part):
    shot = lax.axis_index("shot")
    mine = partner()
    depth = rate.shape[0]
    for k in range(KT):
        owner, slot = place_of(tiles, shot, k)
        for p in range(depth):
            tile = vel_got[owner, slot * depth + p]
            rate[p, pl.ds(k * BX, BX)] = tile * tile * (1.0 / SCALE)
    for f in range(2):

        def plane_at(m):
            return near[mine, f * REACH - 1 - m] if m < 0 else None

        for p in range(depth):
            total = sums[f * depth + p]
            if p < REACH:
                total += beyond_sums(p, plane_at)
            part[f * depth + p] = base[f * depth + p] + rate[p] * total


def first_kernel(wavelet, spot_x, spot_z, spot_y, depth_at, traces, far, part, rate, now):
    depth = rate.shape[0]
    for f in range(2):

        def plane_at(m):
            return far[f * REACH + REACH - 1 - (m - depth)] if m >= depth else None

        for p in range(depth):
            value = part[f * depth + p]
            if p >= depth - REACH:
                value += rate[p] * beyond_sums(p, plane_at)
            now[f * depth + p] = value
    now[pl.ds(2 * depth, REACH)] = rate[pl.ds(depth - REACH, REACH)]
    places = (wavelet, spot_x, spot_z, spot_y, depth_at, traces)
    own = (0, depth - 1, now)
    add_sources(0, [own + (lambda m: m,)], [own + (lambda m: depth + m,)], places, depth)


def wide_interior_kernel(now, src_old, rec_old, rate, to_y, to_near, base, padded):
    depth = rate.shape[0]
    clear_edges(padded)
    to_near[pl.ds(0, 2 * depth)] = now[pl.ds(0, 2 * depth)]
    to_near[pl.ds(2 * depth, REACH)] = rate[pl.ds(0, REACH)]
    for f, old in enumerate((src_old, rec_old)):

        def plane_at(m):
            return now[f * depth + m] if 0 <= m < depth else None

        for first in range(0, depth, REACH):
            planes = now[pl.ds(f * depth + first, REACH)]
            for i, total in enumerate(full_sums(padded, planes, first, plane_at, to_y[...])):
                p = first + i
                base[f * depth + p] = 2.0 * planes[i] - old[p] + rate[p] * total


def wide_near_kernel(
    wavelet, spot_x, spot_z, spot_y, depth_at, traces, near, near_old, now, base, rate, to_y,
    mid_near, mid_low, mid_part, padded,
):
    depth = rate.shape[0]
    mine = partner()
    clear_edges(padded)
    for f in range(2):

        def plane_at(m):
            if m >= 0:
                return now[f * depth + m]
            return near[f * depth - 1 - m]

        planes = near[pl.ds(f * depth, REACH)]
        totals = full_sums(padded, planes, 0, lambda m: plane_at(-1 - m), to_y[...])
        for i, total in enumerate(totals):
            value = 2.0 * planes[i] - near_old[mine, f * REACH + i]
            mid_near[f * REACH + i] = value + near[2 * depth + i] * total
        for p in range(depth):
            if p < REACH:
                share = beyond_sums(p, lambda m: plane_at(m) if m < 0 else None)
                mid_low[f * REACH + p] = base[f * depth + p] + rate[p] * share
            else:
                mid_part[f * REACH + p - REACH] = base[f * depth + p]
    places = (wavelet, spot_x, spot_z, spot_y, depth_at, traces)
    fields = [
        [
            (0, REACH - 1, mid_low, lambda m, f=f: f * REACH + m),
            (-REACH, -1, mid_near, lambda m, f=f: f * REACH - 1 - m),
        ]
        for f in range(2)
    ]
    add_sources(1, *fields, places, depth)


def wide_far_kernel(
    wavelet, spot_x, spot_z, spot_y, depth_at, traces, far, far_old, now, mid_low, mid_part, rate,
    to_y, mid_high, to_far, mid_far, padded,
):
    depth = rate.shape[0]
    high = depth - REACH
    clear_edges(padded)
    places = (wavelet, spot_x, spot_z, spot_y, depth_at, traces)
    for f in range(2):

        def plane_at(m):
            if m < depth:
                return now[f * depth + m]
            return far[f * depth + 2 * depth - 1 - m]

        planes = jnp.stack([plane_at(depth + i) for i in range(REACH)])
        totals = full_sums(padded, planes, depth, plane_at, to_y[...])
        for i, total in enumerate(totals):
            value = 2.0 * planes[i] - far_old[f * REACH + REACH - 1 - i]
            mid_far[f * REACH + i] = value + far[2 * depth + REACH - 1 - i] * total
        for p in range(high, depth):
            share = beyond_sums(p, lambda m: plane_at(m) if m >= depth else None)
            mid_high[f * REACH + p - high] = mid_part[f * REACH + p - high] + rate[p] * share
    fields = [
        [
            (high, depth - 1, mid_high, lambda m, f=f: f * REACH + m - high),
            (depth, depth + REACH - 1, mid_far, lambda m, f=f: f * REACH + m - depth),
        ]
        for f in range(2)
    ]
    add_sources(1, *fields, places, depth)
    for f in range(2):

        def mid_at(m):
            if m < high:
                return mid_low[f * REACH + m]
            return mid_high[f * REACH + m - high] if m < depth else mid_far[f * REACH + m - depth]

        planes = mid_high[pl.ds(f * REACH, REACH)]
        for i, total in enumerate(full_sums(padded, planes, high, mid_at, to_y[...])):
            p = high + i
            value = 2.0 * planes[i] - now[f * depth + p]
            to_far[f * REACH + i] = value + rate[p] * total
    fields = [
        [(high, depth - 1, to_far, lambda m, f=f: f * REACH + m - high)] for f in range(2)
    ]
    add_sources(2, *fields, places, depth)


def interior_kernel(
    wavelet, spot_x, spot_z, spot_y, depth_at, traces, now, mid_near, mid_low, mid_high, new_high,
    rate, to_y, new_low, base, partial, padded,
):
    depth = rate.shape[0]
    high = depth - REACH
    clear_edges(padded)
    places = (wavelet, spot_x, spot_z, spot_y, depth_at, traces)

    def mid_at(f, m):
        if m < 0:
            return mid_near[f * REACH - 1 - m]
        return mid_low[f * REACH + m] if m < high else mid_high[f * REACH + m - high]

    def new_at(f, m):
        return new_low[f * REACH + m] if m < high else new_high[f * REACH + m - high]

    for f in range(2):
        planes = mid_low[pl.ds(f * REACH, REACH)]
        totals = full_sums(padded, planes, 0, lambda m: mid_at(f, m), to_y[...])
        for p, total in enumerate(totals):
            new_low[f * REACH + p] = 2.0 * planes[p] - now[f * depth + p] + rate[p] * total
    fields = [[(0, high - 1, new_low, lambda m, f=f: f * REACH + m)] for f in range(2)]
    add_sources(2, *fields, places, depth)
    for f in range(2):
        for first, part in ((0, new_low), (high, new_high)):
            planes = part[pl.ds(f * REACH, REACH)]

            def plane_at(m):
                return new_at(f, m) if 0 <= m < depth else None

            for i, total in enumerate(full_sums(padded, planes, first, plane_at, to_y[...])):
                p = first + i
                base[f * depth + p] = 2.0 * planes[i] - mid_at(f, p) + rate[p] * total
    for p in range(depth):
        total = new_at(0, p) * now[depth + p] + mid_at(0, p) * mid_at(1, p)
        partial[p] = total + now[p] * new_at(1, p)


def last_kernel(
    tiles, wavelet, spot_x, spot_z, spot_y, depth_at, traces, far, near, base, rate, partial,
    src_first, rec_first, new, send,
):
    shot = lax.axis_index("shot")
    mine = partner()
    depth = rate.shape[0]
    for f in range(2):

        def plane_at(m):
            if m < 0:
                return near[mine, f * REACH - 1 - m]
            return far[f * REACH + REACH - 1 - (m - depth)] if m >= depth else None

        for p in range(depth):
            new[f * depth + p] = base[f * depth + p] + rate[p] * beyond_sums(p, plane_at)
    places = (wavelet, spot_x, spot_z, spot_y, depth_at, traces)
    own = (0, depth - 1, new)
    add_sources(STEPS - 1, [own + (lambda m: m,)], [own + (lambda m: depth + m,)], places, depth)
    send[...] = jnp.zeros(send.shape, jnp.float32)
    for k in range(KT):
        owner, slot = place_of(tiles, shot, k)
        at = pl.ds(k * BX, BX)
        for p in range(depth):
            total = partial[p, at] + new[p, at] * rec_first[p, at]
            send[owner, slot * depth + p] = total + src_first[p, at] * new[depth + p, at]


def gather_kernel(
    tiles, got, new, out, src_out, rec_out, total, out_rows, src_rows, rec_rows, sems
):
    shot = lax.axis_index("shot")
    depth = new.shape[0] // 2
    size_x = new.shape[1]
    held = total.shape[0] // depth
    total[...] = jnp.zeros(total.shape, jnp.float32)
    for g in range(got.shape[0]):
        before = first_slot(tiles, shot, g)
        for j in range(CAP):
            k = jnp.minimum(before + j, KT - 1)
            own = jnp.clip(tiles[g, k] - shot * BX, 0, held - 1)
            total[pl.ds(own * depth, depth)] += got[g, pl.ds(j * depth, depth)]
    for t in range(held):
        for p in range(depth):
            at = t * BX * depth + z_of(p, depth)
            out_rows[pl.ds(at, BX, stride=depth)] = total[t * depth + p]
    copies = [pltpu.make_async_copy(out_rows, out, sems.at[0])]
    copies[0].start()
    for f, (rows, to) in enumerate(((src_rows, src_out), (rec_rows, rec_out))):
        for p in range(depth):
            rows[pl.ds(z_of(p, depth), size_x, stride=depth)] = new[f * depth + p]
        copies.append(pltpu.make_async_copy(rows, to, sems.at[1 + f]))
        copies[-1].start()
    for copy in copies:
        copy.wait()


def local(
    src_prev,
    src_cur,
    rec_cur,
    rec_next,
    velocity,
    aperture_tiles,
    wavelet,
    src_x,
    src_z,
    src_y,
    rec_depth,
    rec_data,
):
    slabs = lax.axis_size("slab")
    shots = lax.axis_size("shot")
    far_pairs = []
    for i in range(1, slabs - 1, 2):
        far_pairs += [(i, i + 1), (i + 1, i)]
    near_groups = [[i, i + 1] for i in range(0, slabs, 2)]
    near_pairs = [(i, i ^ 1) for i in range(slabs)]

    def flat(array):
        return array.reshape(-1, array.shape[-1])

    _, size_x, depth, size_y = src_cur.shape
    raw = (depth * size_x, size_y)
    model = (velocity.shape[0] * depth, size_y)
    one, two = (depth, size_x, size_y), (2 * depth, size_x, size_y)
    halo = (2 * REACH, size_x, size_y)
    wide = (2 * depth + REACH, size_x, size_y)
    buffer = (shots, CAP * depth, BX, size_y)
    dma = pltpu.SemaphoreType.DMA
    padded = VMEM((REACH, size_x + 2 * PAD, size_y), jnp.float32)
    given = (flat(src_cur), flat(rec_cur), flat(velocity), aperture_tiles)
    given += (src_x, src_z, src_y, rec_depth)
    whole_numbers = [(a.shape, VMEM, jnp.int32) for a in given[3:]]
    send, to_far, src, rec, tiles, *places = call(
        start_kernel, [buffer, halo, one, one] + whole_numbers, [HBM] * 8,
        *[pltpu.with_memory_space_constraint(a, HBM) for a in given],
        scratch=[
            VMEM(raw, jnp.float32), VMEM(raw, jnp.float32), VMEM(model, jnp.float32),
            SMEM(aperture_tiles.shape, jnp.int32), dma((9,)),
        ],
    )
    places = (wavelet, *places, rec_data[0])
    place_spaces = [SMEM] * 5 + [VMEM]

    vel_got = lax.all_to_all(send, "shot", 0, 0)
    far = lax.ppermute(to_far, "slab", far_pairs)
    to_near, sums, base, to_y = call(
        first_interior_kernel, [halo, two, two, ((2 * size_y, size_y), VMEM, jnp.bfloat16)],
        [VMEM] * 4, src, rec, flat(src_prev), flat(rec_next), scratch=[padded],
    )
    near = lax.all_gather(to_near, "slab", axis_index_groups=near_groups)
    rate, part = call(
        rate_kernel, [one, two], [SMEM] + [VMEM] * 4, tiles, vel_got, near, sums, base
    )
    (now,) = call(first_kernel, [wide], place_spaces + [VMEM] * 3, *places, far, part, rate)

    wide_far = lax.ppermute(now, "slab", far_pairs)
    to_near, base = call(
        wide_interior_kernel, [wide, two], [VMEM] * 5, now, src, rec, rate, to_y, scratch=[padded]
    )
    wide_near = lax.ppermute(to_near, "slab", near_pairs)
    mid_near, mid_low, mid_part = call(
        wide_near_kernel, [halo] * 3, place_spaces + [VMEM] * 6,
        *places, wide_near, near, now, base, rate, to_y, scratch=[padded],
    )
    mid_high, new_high = call(
        wide_far_kernel, [halo] * 2, place_spaces + [VMEM] * 7,
        *places, wide_far, far, now, mid_low, mid_part, rate, to_y,
        scratch=[VMEM(halo, jnp.float32), padded],
    )

    far = lax.ppermute(new_high, "slab", far_pairs)
    new_low, base, partial = call(
        interior_kernel, [halo, two, one], place_spaces + [VMEM] * 7,
        *places, now, mid_near, mid_low, mid_high, new_high, rate, to_y, scratch=[padded],
    )
    near = lax.all_gather(new_low, "slab", axis_index_groups=near_groups)
    new, send = call(
        last_kernel, [two, buffer], [SMEM] + place_spaces + [VMEM] * 7,
        tiles, *places, far, near, base, rate, partial, src, rec,
    )
    image_got = lax.all_to_all(send, "shot", 0, 0)
    image, src, rec = call(
        gather_kernel, [(model, HBM), (raw, HBM), (raw, HBM)], [SMEM] + [VMEM] * 2,
        tiles, image_got, new,
        scratch=[
            VMEM((velocity.shape[0] // BX * depth, BX, size_y), jnp.float32),
            VMEM(model, jnp.float32), VMEM(raw, jnp.float32), VMEM(raw, jnp.float32), dma((3,)),
        ],
    )
    return image.reshape(velocity.shape), src.reshape(src_cur.shape), rec.reshape(src_cur.shape)


def solution(mesh):
    wave = P("shot", None, "slab", None)
    model = P("shot", "slab", None)
    return jax.shard_map(
        local,
        mesh=mesh,
        in_specs=(wave,) * 4 + (model,) + (P(),) * 6 + (P("shot", None, None, None),),
        out_specs=(model, wave, wave),
        check_vma=False,
    )
```

```python
import jax
import jax.numpy as jnp
from jax import lax
from jax.experimental import pallas as pl
from jax.experimental.pallas import tpu as pltpu
from jax.sharding import PartitionSpec as P


BX = 8
KT = 8
STEPS = 4
CAP = 2
REACH = 4
PAD = 8
VMEM = pltpu.VMEM
SMEM = pltpu.SMEM
HBM = pltpu.HBM

SCALE = 5040.0
TAPS = (-43050.0, 8064.0, -1008.0, 128.0, -9.0)


def call(body, outs, in_spaces, *args, scratch=()):
    outs = [o if isinstance(o[0], tuple) else (o, VMEM) for o in outs]
    outs = [o if len(o) == 3 else o + (jnp.float32,) for o in outs]
    size = 8 * 64 * 128
    return pl.pallas_call(
        body,
        out_shape=[jax.ShapeDtypeStruct(s, t) for s, _, t in outs],
        in_specs=[pl.BlockSpec(memory_space=s) for s in in_spaces],
        out_specs=[pl.BlockSpec(memory_space=m) for _, m, _ in outs],
        scratch_shapes=list(scratch),
        compiler_params=pltpu.CompilerParams(vmem_limit_bytes=24 * 1024 * 1024),
        cost_estimate=pl.CostEstimate(
            flops=90 * size, bytes_accessed=32 * size, transcendentals=0
        ),
    )(*args)


def is_odd():
    return lax.rem(lax.axis_index("slab"), 2) == 1


def partner():
    return jnp.where(is_odd(), 0, 1)


def z_of(plane, depth):
    return jnp.where(is_odd(), plane, depth - 1 - plane)


def tap_of(reach):
    weight = jnp.zeros(reach.shape, jnp.float32)
    for r in range(1, REACH + 1):
        weight = jnp.where(reach == r, TAPS[r], weight)
    return weight


def along_y_matrix(size_y):
    shape = (2 * size_y, size_y)
    row = lax.rem(lax.broadcasted_iota(jnp.int32, shape, 0), size_y)
    return tap_of(jnp.abs(row - lax.broadcasted_iota(jnp.int32, shape, 1))).astype(jnp.bfloat16)


def along_y(planes, to_y):
    rows = planes.reshape(-1, planes.shape[2])
    high = rows.astype(jnp.bfloat16)
    low = (rows - high.astype(jnp.float32)).astype(jnp.bfloat16)
    sums = jnp.dot(
        jnp.concatenate([high, low], axis=1), to_y, preferred_element_type=jnp.float32
    )
    return sums.reshape(planes.shape)


def clear_edges(padded):
    count, rows, size_y = padded.shape
    zeros = jnp.zeros((count, PAD, size_y), jnp.float32)
    padded[:, pl.ds(0, PAD)] = zeros
    padded[:, pl.ds(rows - PAD, PAD)] = zeros


def full_sums(padded, planes, first, plane_at, to_y):
    count, size_x, _ = planes.shape
    padded[pl.ds(0, count), pl.ds(PAD, size_x)] = planes
    lines = along_y(planes, to_y)
    sums = []
    for p in range(count):
        total = lines[p] + TAPS[0] * planes[p]
        for r in range(1, REACH + 1):
            terms = padded[p, pl.ds(PAD + r, size_x)] + padded[p, pl.ds(PAD - r, size_x)]
            for other in (plane_at(first + p + r), plane_at(first + p - r)):
                if other is not None:
                    terms += other
            total += TAPS[r] * terms
        sums.append(total)
    return sums


def beyond_sums(plane, plane_at):
    total = 0.0
    for r in range(1, REACH + 1):
        for other in (plane_at(plane + r), plane_at(plane - r)):
            if other is not None:
                total += TAPS[r] * other
    return total


def sources_at(f, number, step, sources):
    where, spots, traces = sources
    added = traces[STEPS - 1 - step].astype(jnp.float32) if f else spots[step]
    here = (where[f] == float(number))[None]
    return jnp.where(here, added.reshape(-1, 8, added.shape[1]), 0.0).reshape(added.shape)


def start_kernel(
    src_in, rec_in, vel_in, tiles_in, x_in, z_in, y_in, depth_in, wavelet_in,
    send, to_far, src, rec, pick, put, where, spots,
    src_raw, rec_raw, vel, tiles, spot_x, spot_z, spot_y, depth_at, wavelet, sems, send_sems,
):
    shot = lax.axis_index("shot")
    moves = [(tiles_in, tiles), (vel_in, vel), (src_in, src_raw), (rec_in, rec_raw)]
    moves += [(x_in, spot_x), (z_in, spot_z), (y_in, spot_y), (depth_in, depth_at)]
    moves += [(wavelet_in, wavelet)]
    copies = [pltpu.make_async_copy(a, b, sems.at[i]) for i, (a, b) in enumerate(moves)]
    for copy in copies:
        copy.start()
    depth, size_x, size_y = src.shape
    rows = BX * depth
    held = vel.shape[0] // rows
    copies[0].wait()
    copies[1].wait()
    places = []
    for g in range(send.shape[0]):
        before = jnp.int32(0)
        for k in range(KT):
            before += (tiles[g, k] < shot * BX).astype(jnp.int32)
        for j in range(CAP):
            own = tiles[g, jnp.minimum(before + j, KT - 1)] - shot * BX
            filled = (before + j < KT) & (own >= 0) & (own < held)
            places.append(jnp.where(filled, own, -1))
            at = pl.multiple_of(jnp.clip(own, 0, held - 1) * rows, rows)
            copy = pltpu.make_async_copy(
                vel.at[pl.ds(at, rows)], send.at[g, j], send_sems.at[g * CAP + j]
            )
            copy.start()
            copies.append(copy)
    for f, (raw, field) in enumerate(((src_raw, src), (rec_raw, rec))):
        copies[2 + f].wait()
        for p in range(depth):
            plane = raw[pl.ds(z_of(p, depth), size_x, stride=depth)]
            field[p] = plane
            if p >= depth - REACH:
                to_far[f * REACH + p - (depth - REACH)] = plane
    tile = (8, size_y)
    for c, own in enumerate(places):
        own = jnp.full(tile, own)
        for t in range(held):
            put[c, t] = jnp.where(own == t, 1.0, 0.0)
    previous = jnp.int32(-1)
    for k in range(KT):
        owner = lax.shift_right_logical(tiles[shot, k], 3)
        place = owner * CAP + (previous == owner).astype(jnp.int32)
        previous = owner
        place = jnp.full(tile, place)
        for c in range(pick.shape[1]):
            pick[k, c] = jnp.where(place == c, 1.0, 0.0)
    for copy in copies[4:9]:
        copy.wait()
    first = lax.axis_index("slab") * depth
    for f, local in enumerate((spot_z[shot] - first, depth_at[shot] - first)):
        where[f] = jnp.full(tile, z_of(local, depth)).astype(jnp.float32)
    row = lax.broadcasted_iota(jnp.int32, (size_x, size_y), 0)
    lane = lax.broadcasted_iota(jnp.int32, (size_x, size_y), 1)
    here = (row == spot_x[shot]) & (lane == spot_y[shot])
    for step in range(STEPS):
        spots[step] = jnp.where(here, wavelet[step, shot], 0.0)
    for copy in copies[9:]:
        copy.wait()


def first_interior_kernel(src, rec, src_old, rec_old, to_near, sums, base, to_y, padded):
    depth, size_x, size_y = src.shape
    to_y[...] = along_y_matrix(size_y)
    clear_edges(padded)
    for f, (field, old) in enumerate(((src, src_old), (rec, rec_old))):

        def plane_at(m):
            return field[m] if 0 <= m < depth else None

        for first in range(0, depth, REACH):
            planes = field[pl.ds(first, REACH)]
            if first == 0:
                to_near[pl.ds(f * REACH, REACH)] = planes
            for i, total in enumerate(full_sums(padded, planes, first, plane_at, to_y[...])):
                p = first + i
                sums[f * depth + p] = total
                before = old[pl.ds(z_of(p, depth), size_x, stride=depth)]
                base[f * depth + p] = 2.0 * planes[i] - before


def rate_kernel(pick, vel_got, near, sums, base, where, spots, traces, rate, part):
    mine = partner()
    depth = rate.shape[0]
    count = pick.shape[1]
    for p in range(depth):
        at = pl.ds(z_of(p, depth), BX, stride=depth)
        tiles = [vel_got[c // CAP, c % CAP, at] for c in range(count)]
        for k in range(KT):
            tile = 0.0
            for c in range(k, count - (KT - 1 - k)):
                tile += pick[k, c] * tiles[c]
            rate[p, pl.ds(k * BX, BX)] = tile * tile * (1.0 / SCALE)
    for f in range(2):

        def plane_at(m):
            return near[mine, f * REACH - 1 - m] if m < 0 else None

        for p in range(depth):
            total = sums[f * depth + p]
            if p < REACH:
                total += beyond_sums(p, plane_at)
            added = sources_at(f, p, 0, (where, spots, traces))
            part[f * depth + p] = base[f * depth + p] + rate[p] * total + added


def first_kernel(far, part, rate, now):
    depth = rate.shape[0]
    for f in range(2):

        def plane_at(m):
            return far[f * REACH + REACH - 1 - (m - depth)] if m >= depth else None

        for p in range(depth):
            value = part[f * depth + p]
            if p >= depth - REACH:
                value += rate[p] * beyond_sums(p, plane_at)
            now[f * depth + p] = value
    now[pl.ds(2 * depth, REACH)] = rate[pl.ds(depth - REACH, REACH)]


def wide_interior_kernel(
    now, src_old, rec_old, rate, to_y, src_near, rec_near, base, padded
):
    depth = rate.shape[0]
    clear_edges(padded)
    src_near[pl.ds(0, depth)] = now[pl.ds(0, depth)]
    src_near[pl.ds(depth, REACH)] = rate[pl.ds(0, REACH)]
    rec_near[...] = now[pl.ds(depth, depth)]
    for f, old in enumerate((src_old, rec_old)):

        def plane_at(m):
            return now[f * depth + m] if 0 <= m < depth else None

        for first in range(0, depth, REACH):
            planes = now[pl.ds(f * depth + first, REACH)]
            for i, total in enumerate(full_sums(padded, planes, first, plane_at, to_y[...])):
                p = first + i
                base[f * depth + p] = 2.0 * planes[i] - old[p] + rate[p] * total


def wide_near_kernel(
    where, spots, traces, src_near, rec_near, near_old, now, base, rate, to_y,
    mid_near, mid_low, mid_part, padded,
):
    depth = rate.shape[0]
    mine = partner()
    sources = (where, spots, traces)
    clear_edges(padded)
    for f, near in enumerate((src_near, rec_near)):

        def plane_at(m):
            if m >= 0:
                return now[f * depth + m]
            return near[mine, -1 - m]

        planes = near[mine, pl.ds(0, REACH)]
        totals = full_sums(padded, planes, 0, lambda m: plane_at(-1 - m), to_y[...])
        for i, total in enumerate(totals):
            value = 2.0 * planes[i] - near_old[mine, f * REACH + i]
            value += src_near[mine, depth + i] * total
            mid_near[f * REACH + i] = value + sources_at(f, -1 - i, 1, sources)
        for p in range(depth):
            value = base[f * depth + p] + sources_at(f, p, 1, sources)
            if p < REACH:
                share = beyond_sums(p, lambda m: plane_at(m) if m < 0 else None)
                mid_low[f * REACH + p] = value + rate[p] * share
            else:
                mid_part[f * REACH + p - REACH] = value


def wide_far_kernel(
    where, spots, traces, far, far_old, now, mid_low, mid_part, rate, to_y,
    mid_high, to_far, mid_far, padded,
):
    depth = rate.shape[0]
    high = depth - REACH
    sources = (where, spots, traces)
    clear_edges(padded)
    for f in range(2):

        def plane_at(m):
            if m < depth:
                return now[f * depth + m]
            return far[f * depth + 2 * depth - 1 - m]

        def mid_at(m):
            if m < high:
                return mid_low[f * REACH + m]
            return mid_high[f * REACH + m - high] if m < depth else mid_far[f * REACH + m - depth]

        planes = jnp.stack([plane_at(depth + i) for i in range(REACH)])
        totals = full_sums(padded, planes, depth, plane_at, to_y[...])
        for i, total in enumerate(totals):
            value = 2.0 * planes[i] - far_old[f * REACH + REACH - 1 - i]
            value += far[2 * depth + REACH - 1 - i] * total
            mid_far[f * REACH + i] = value + sources_at(f, depth + i, 1, sources)
        for p in range(high, depth):
            share = beyond_sums(p, lambda m: plane_at(m) if m >= depth else None)
            mid_high[f * REACH + p - high] = mid_part[f * REACH + p - high] + rate[p] * share
        planes = mid_high[pl.ds(f * REACH, REACH)]
        for i, total in enumerate(full_sums(padded, planes, high, mid_at, to_y[...])):
            p = high + i
            value = 2.0 * planes[i] - now[f * depth + p] + rate[p] * total
            to_far[f * REACH + i] = value + sources_at(f, p, 2, sources)


def interior_kernel(
    where, spots, traces, now, mid_near, mid_low, mid_high, new_high, rate, to_y,
    new_low, base, partial, padded,
):
    depth = rate.shape[0]
    high = depth - REACH
    sources = (where, spots, traces)
    clear_edges(padded)

    def mid_at(f, m):
        if m < 0:
            return mid_near[f * REACH - 1 - m]
        return mid_low[f * REACH + m] if m < high else mid_high[f * REACH + m - high]

    def new_at(f, m):
        return new_low[f * REACH + m] if m < high else new_high[f * REACH + m - high]

    for f in range(2):
        planes = mid_low[pl.ds(f * REACH, REACH)]
        totals = full_sums(padded, planes, 0, lambda m: mid_at(f, m), to_y[...])
        for p, total in enumerate(totals):
            value = 2.0 * planes[p] - now[f * depth + p] + rate[p] * total
            new_low[f * REACH + p] = value + sources_at(f, p, 2, sources)
    for f in range(2):
        for first, part in ((0, new_low), (high, new_high)):
            planes = part[pl.ds(f * REACH, REACH)]

            def plane_at(m):
                return new_at(f, m) if 0 <= m < depth else None

            for i, total in enumerate(full_sums(padded, planes, first, plane_at, to_y[...])):
                p = first + i
                value = 2.0 * planes[i] - mid_at(f, p) + rate[p] * total
                base[f * depth + p] = value + sources_at(f, p, 3, sources)
    for p in range(depth):
        total = new_at(0, p) * now[depth + p] + mid_at(0, p) * mid_at(1, p)
        partial[p] = total + now[p] * new_at(1, p)


def last_kernel(pick, far, near, base, rate, partial, src_first, rec_first, new, send):
    mine = partner()
    depth = rate.shape[0]
    count = pick.shape[1]
    for p in range(depth):
        fields = []
        for f in range(2):

            def plane_at(m):
                if m < 0:
                    return near[mine, f * REACH - 1 - m]
                return far[f * REACH + REACH - 1 - (m - depth)] if m >= depth else None

            value = base[f * depth + p] + rate[p] * beyond_sums(p, plane_at)
            new[f * depth + p] = value
            fields.append(value)
        image = partial[p] + fields[0] * rec_first[p] + src_first[p] * fields[1]
        for c in range(count):
            total = 0.0
            for k in range(max(0, c - (count - KT)), min(KT - 1, c) + 1):
                total += pick[k, c] * image[k * BX : (k + 1) * BX]
            send[c // CAP, (c % CAP) * depth + p] = total


def gather_kernel(put, got, new, out, src_out, rec_out, out_rows, src_rows, rec_rows, sems):
    depth = new.shape[0] // 2
    size_x = new.shape[1]
    count, held = put.shape[:2]
    copies = []
    for f, (rows, to) in enumerate(((src_rows, src_out), (rec_rows, rec_out))):
        for p in range(depth):
            rows[pl.ds(z_of(p, depth), size_x, stride=depth)] = new[f * depth + p]
        copies.append(pltpu.make_async_copy(rows, to, sems.at[f]))
        copies[-1].start()
    for t in range(held):
        for p in range(depth):
            total = 0.0
            for c in range(count):
                total += put[c, t] * got[c // CAP, (c % CAP) * depth + p]
            out_rows[pl.ds(t * BX * depth + z_of(p, depth), BX, stride=depth)] = total
    copies.append(pltpu.make_async_copy(out_rows, out, sems.at[2]))
    copies[-1].start()
    for copy in copies:
        copy.wait()


def local(
    src_prev,
    src_cur,
    rec_cur,
    rec_next,
    velocity,
    aperture_tiles,
    wavelet,
    src_x,
    src_z,
    src_y,
    rec_depth,
    rec_data,
):
    slabs = lax.axis_size("slab")
    shots = lax.axis_size("shot")
    far_pairs = []
    for i in range(1, slabs - 1, 2):
        far_pairs += [(i, i + 1), (i + 1, i)]
    near_groups = [[i, i + 1] for i in range(0, slabs, 2)]

    def flat(array):
        return array.reshape(-1, array.shape[-1])

    _, size_x, depth, size_y = src_cur.shape
    raw = (depth * size_x, size_y)
    model = (velocity.shape[0] * depth, size_y)
    one, two = (depth, size_x, size_y), (2 * depth, size_x, size_y)
    halo = (2 * REACH, size_x, size_y)
    wide = (2 * depth + REACH, size_x, size_y)
    buffer = (shots, CAP * depth, BX, size_y)
    dma = pltpu.SemaphoreType.DMA
    padded = VMEM((REACH, size_x + 2 * PAD, size_y), jnp.float32)
    count = shots * CAP
    held = velocity.shape[0] // BX
    given = (flat(src_cur), flat(rec_cur), flat(velocity), aperture_tiles)
    given += (src_x, src_z, src_y, rec_depth, wavelet.T)
    scalars = [SMEM(a.shape, a.dtype) for a in given[3:]]
    send, to_far, src, rec, pick, put, where, spots = call(
        start_kernel,
        [
            ((shots, CAP, BX * depth, size_y), HBM), halo, one, one, (KT, count, 8, size_y),
            (count, held, 8, size_y), (2, 8, size_y), (STEPS, size_x, size_y),
        ],
        [HBM] * 9, *[pltpu.with_memory_space_constraint(a, HBM) for a in given],
        scratch=[
            VMEM(raw, jnp.float32), VMEM(raw, jnp.float32), VMEM(model, jnp.float32), *scalars,
            dma((9,)), dma((count,)),
        ],
    )
    sources = (where, spots, rec_data[0])

    vel_got = lax.all_to_all(send, "shot", 0, 0)
    far = lax.ppermute(to_far, "slab", far_pairs)
    to_near, sums, base, to_y = call(
        first_interior_kernel, [halo, two, two, ((2 * size_y, size_y), VMEM, jnp.bfloat16)],
        [VMEM] * 4, src, rec, flat(src_prev), flat(rec_next), scratch=[padded],
    )
    near = lax.all_gather(to_near, "slab", axis_index_groups=near_groups)
    rate, part = call(
        rate_kernel, [one, two], [VMEM] * 8, pick, vel_got, near, sums, base, *sources
    )
    (now,) = call(first_kernel, [wide], [VMEM] * 3, far, part, rate)

    wide_far = lax.ppermute(now, "slab", far_pairs)
    src_near, rec_near, base = call(
        wide_interior_kernel, [(depth + REACH, size_x, size_y), one, two], [VMEM] * 5,
        now, src, rec, rate, to_y, scratch=[padded],
    )
    src_near = lax.all_gather(src_near, "slab", axis_index_groups=near_groups)
    rec_near = lax.all_gather(rec_near, "slab", axis_index_groups=near_groups)
    mid_near, mid_low, mid_part = call(
        wide_near_kernel, [halo] * 3, [VMEM] * 10,
        *sources, src_near, rec_near, near, now, base, rate, to_y, scratch=[padded],
    )
    mid_high, new_high = call(
        wide_far_kernel, [halo] * 2, [VMEM] * 10,
        *sources, wide_far, far, now, mid_low, mid_part, rate, to_y,
        scratch=[VMEM(halo, jnp.float32), padded],
    )

    far = lax.ppermute(new_high, "slab", far_pairs)
    new_low, base, partial = call(
        interior_kernel, [halo, two, one], [VMEM] * 10,
        *sources, now, mid_near, mid_low, mid_high, new_high, rate, to_y, scratch=[padded],
    )
    near = lax.all_gather(new_low, "slab", axis_index_groups=near_groups)
    new, send = call(
        last_kernel, [two, buffer], [VMEM] * 8,
        pick, far, near, base, rate, partial, src, rec,
    )
    image_got = lax.all_to_all(send, "shot", 0, 0)
    image, src, rec = call(
        gather_kernel, [(model, HBM), (raw, HBM), (raw, HBM)], [VMEM] * 3, put, image_got, new,
        scratch=[
            VMEM(model, jnp.float32), VMEM(raw, jnp.float32), VMEM(raw, jnp.float32), dma((3,)),
        ],
    )
    return image.reshape(velocity.shape), src.reshape(src_cur.shape), rec.reshape(src_cur.shape)


def solution(mesh):
    wave = P("shot", None, "slab", None)
    model = P("shot", "slab", None)
    return jax.shard_map(
        local,
        mesh=mesh,
        in_specs=(wave,) * 4 + (model,) + (P(),) * 6 + (P("shot", None, None, None),),
        out_specs=(model, wave, wave),
        check_vma=False,
    )
```

```python
import jax
import jax.numpy as jnp
from jax import lax
from jax.experimental import pallas as pl
from jax.experimental.pallas import tpu as pltpu
from jax.sharding import PartitionSpec as P


BX = 8
KT = 8
STEPS = 4
CAP = 2
REACH = 4
PAD = 8
VMEM = pltpu.VMEM
SMEM = pltpu.SMEM
HBM = pltpu.HBM

SCALE = 5040.0
TAPS = (-43050.0, 8064.0, -1008.0, 128.0, -9.0)


def call(body, outs, in_spaces, *args, scratch=()):
    outs = [o if isinstance(o[0], tuple) else (o, VMEM) for o in outs]
    outs = [o if len(o) == 3 else o + (jnp.float32,) for o in outs]
    size = 8 * 64 * 128
    return pl.pallas_call(
        body,
        out_shape=[jax.ShapeDtypeStruct(s, t) for s, _, t in outs],
        in_specs=[pl.BlockSpec(memory_space=s) for s in in_spaces],
        out_specs=[pl.BlockSpec(memory_space=m) for _, m, _ in outs],
        scratch_shapes=list(scratch),
        compiler_params=pltpu.CompilerParams(vmem_limit_bytes=24 * 1024 * 1024),
        cost_estimate=pl.CostEstimate(
            flops=90 * size, bytes_accessed=32 * size, transcendentals=0
        ),
    )(*args)


def is_odd():
    return lax.rem(lax.axis_index("slab"), 2) == 1


def partner():
    return jnp.where(is_odd(), 0, 1)


def z_of(plane, depth):
    return jnp.where(is_odd(), plane, depth - 1 - plane)


def tap_of(reach):
    weight = jnp.zeros(reach.shape, jnp.float32)
    for r in range(1, REACH + 1):
        weight = jnp.where(reach == r, TAPS[r], weight)
    return weight


def along_y_matrix(size_y):
    shape = (2 * size_y, size_y)
    row = lax.rem(lax.broadcasted_iota(jnp.int32, shape, 0), size_y)
    return tap_of(jnp.abs(row - lax.broadcasted_iota(jnp.int32, shape, 1))).astype(jnp.bfloat16)


def along_y(planes, to_y):
    rows = planes.reshape(-1, planes.shape[2])
    high = rows.astype(jnp.bfloat16)
    low = (rows - high.astype(jnp.float32)).astype(jnp.bfloat16)
    sums = jnp.dot(
        jnp.concatenate([high, low], axis=1), to_y, preferred_element_type=jnp.float32
    )
    return sums.reshape(planes.shape)


def clear_edges(padded):
    count, rows, size_y = padded.shape
    zeros = jnp.zeros((count, PAD, size_y), jnp.float32)
    padded[:, pl.ds(0, PAD)] = zeros
    padded[:, pl.ds(rows - PAD, PAD)] = zeros


def full_sums(padded, planes, first, plane_at, to_y):
    count, size_x, _ = planes.shape
    padded[pl.ds(0, count), pl.ds(PAD, size_x)] = planes
    lines = along_y(planes, to_y)
    sums = []
    for p in range(count):
        total = lines[p] + TAPS[0] * planes[p]
        for r in range(1, REACH + 1):
            terms = padded[p, pl.ds(PAD + r, size_x)] + padded[p, pl.ds(PAD - r, size_x)]
            for other in (plane_at(first + p + r), plane_at(first + p - r)):
                if other is not None:
                    terms += other
            total += TAPS[r] * terms
        sums.append(total)
    return sums


def beyond_sums(plane, plane_at):
    total = 0.0
    for r in range(1, REACH + 1):
        for other in (plane_at(plane + r), plane_at(plane - r)):
            if other is not None:
                total += TAPS[r] * other
    return total


def sources_at(f, number, step, sources):
    where, spots, traces = sources
    added = traces[STEPS - 1 - step].astype(jnp.float32) if f else spots[step]
    here = (where[f] == float(number))[None]
    return jnp.where(here, added.reshape(-1, 8, added.shape[1]), 0.0).reshape(added.shape)


def start_kernel(
    src_in, rec_in, vel_in, tiles_in, x_in, z_in, y_in, depth_in, wavelet_in,
    send, to_far, src, rec, pick, put, where, spots,
    src_raw, rec_raw, vel, tiles, spot_x, spot_z, spot_y, depth_at, wavelet, sems, send_sems,
):
    shot = lax.axis_index("shot")
    moves = [(tiles_in, tiles), (vel_in, vel), (src_in, src_raw), (rec_in, rec_raw)]
    moves += [(x_in, spot_x), (z_in, spot_z), (y_in, spot_y), (depth_in, depth_at)]
    moves += [(wavelet_in, wavelet)]
    copies = [pltpu.make_async_copy(a, b, sems.at[i]) for i, (a, b) in enumerate(moves)]
    for copy in copies:
        copy.start()
    depth, size_x, size_y = src.shape
    rows = BX * depth
    held = vel.shape[0] // rows
    copies[0].wait()
    copies[1].wait()
    places = []
    for g in range(send.shape[0]):
        before = jnp.int32(0)
        for k in range(KT):
            before += (tiles[g, k] < shot * BX).astype(jnp.int32)
        for j in range(CAP):
            own = tiles[g, jnp.minimum(before + j, KT - 1)] - shot * BX
            filled = (before + j < KT) & (own >= 0) & (own < held)
            places.append(jnp.where(filled, own, -1))
            at = pl.multiple_of(jnp.clip(own, 0, held - 1) * rows, rows)
            copy = pltpu.make_async_copy(
                vel.at[pl.ds(at, rows)], send.at[g, j], send_sems.at[g * CAP + j]
            )
            copy.start()
            copies.append(copy)
    for f, (raw, field) in enumerate(((src_raw, src), (rec_raw, rec))):
        copies[2 + f].wait()
        for p in range(depth):
            plane = raw[pl.ds(z_of(p, depth), size_x, stride=depth)]
            field[p] = plane
            if p >= depth - REACH:
                to_far[f * REACH + p - (depth - REACH)] = plane
    tile = (8, size_y)
    for c, own in enumerate(places):
        put[c] = jnp.full(tile, own)
    previous = jnp.int32(-1)
    for k in range(KT):
        owner = lax.shift_right_logical(tiles[shot, k], 3)
        place = owner * CAP + (previous == owner).astype(jnp.int32)
        previous = owner
        pick[k] = jnp.full(tile, place)
    for copy in copies[4:9]:
        copy.wait()
    first = lax.axis_index("slab") * depth
    for f, local in enumerate((spot_z[shot] - first, depth_at[shot] - first)):
        where[f] = jnp.full(tile, z_of(local, depth)).astype(jnp.float32)
    row = lax.broadcasted_iota(jnp.int32, (size_x, size_y), 0)
    lane = lax.broadcasted_iota(jnp.int32, (size_x, size_y), 1)
    here = (row == spot_x[shot]) & (lane == spot_y[shot])
    for step in range(STEPS):
        spots[step] = jnp.where(here, wavelet[step, shot], 0.0)
    for copy in copies[9:]:
        copy.wait()


def first_interior_kernel(src, rec, src_old, rec_old, to_near, sums, base, to_y, padded):
    depth, size_x, size_y = src.shape
    to_y[...] = along_y_matrix(size_y)
    clear_edges(padded)
    for f, (field, old) in enumerate(((src, src_old), (rec, rec_old))):

        def plane_at(m):
            return field[m] if 0 <= m < depth else None

        for first in range(0, depth, REACH):
            planes = field[pl.ds(first, REACH)]
            if first == 0:
                to_near[pl.ds(f * REACH, REACH)] = planes
            for i, total in enumerate(full_sums(padded, planes, first, plane_at, to_y[...])):
                p = first + i
                sums[f * depth + p] = total
                before = old[pl.ds(z_of(p, depth), size_x, stride=depth)]
                base[f * depth + p] = 2.0 * planes[i] - before


def rate_kernel(pick, vel_got, near, sums, base, where, spots, traces, rate, part):
    mine = partner()
    depth = rate.shape[0]
    count = vel_got.shape[0] * CAP
    rows = [pl.ds(z_of(p, depth), BX, stride=depth) for p in range(depth)]
    for k in range(KT):
        tiles = [vel_got[k // CAP, k % CAP, at] for at in rows]
        for c in range(k + 1, count - (KT - 1 - k)):
            here = pick[k] == c
            tiles = [
                jnp.where(here, vel_got[c // CAP, c % CAP, at], tile)
                for at, tile in zip(rows, tiles, strict=True)
            ]
        for p, tile in enumerate(tiles):
            rate[p, pl.ds(k * BX, BX)] = tile * tile * (1.0 / SCALE)
    for f in range(2):

        def plane_at(m):
            return near[mine, f * REACH - 1 - m] if m < 0 else None

        for p in range(depth):
            total = sums[f * depth + p]
            if p < REACH:
                total += beyond_sums(p, plane_at)
            added = sources_at(f, p, 0, (where, spots, traces))
            part[f * depth + p] = base[f * depth + p] + rate[p] * total + added


def first_kernel(far, part, rate, now):
    depth = rate.shape[0]
    for f in range(2):

        def plane_at(m):
            return far[f * REACH + REACH - 1 - (m - depth)] if m >= depth else None

        for p in range(depth):
            value = part[f * depth + p]
            if p >= depth - REACH:
                value += rate[p] * beyond_sums(p, plane_at)
            now[f * depth + p] = value
    now[pl.ds(2 * depth, REACH)] = rate[pl.ds(depth - REACH, REACH)]


def wide_interior_kernel(
    now, src_old, rec_old, rate, to_y, src_near, rec_near, base, padded
):
    depth = rate.shape[0]
    clear_edges(padded)
    src_near[pl.ds(0, depth)] = now[pl.ds(0, depth)]
    src_near[pl.ds(depth, REACH)] = rate[pl.ds(0, REACH)]
    rec_near[...] = now[pl.ds(depth, depth)]
    for f, old in enumerate((src_old, rec_old)):

        def plane_at(m):
            return now[f * depth + m] if 0 <= m < depth else None

        for first in range(0, depth, REACH):
            planes = now[pl.ds(f * depth + first, REACH)]
            for i, total in enumerate(full_sums(padded, planes, first, plane_at, to_y[...])):
                p = first + i
                base[f * depth + p] = 2.0 * planes[i] - old[p] + rate[p] * total


def wide_near_kernel(
    where, spots, traces, src_near, rec_near, near_old, now, base, rate, to_y,
    mid_near, mid_low, mid_part, padded,
):
    depth = rate.shape[0]
    mine = partner()
    sources = (where, spots, traces)
    clear_edges(padded)
    for f, near in enumerate((src_near, rec_near)):

        def plane_at(m):
            if m >= 0:
                return now[f * depth + m]
            return near[mine, -1 - m]

        planes = near[mine, pl.ds(0, REACH)]
        totals = full_sums(padded, planes, 0, lambda m: plane_at(-1 - m), to_y[...])
        for i, total in enumerate(totals):
            value = 2.0 * planes[i] - near_old[mine, f * REACH + i]
            value += src_near[mine, depth + i] * total
            mid_near[f * REACH + i] = value + sources_at(f, -1 - i, 1, sources)
        for p in range(depth):
            value = base[f * depth + p] + sources_at(f, p, 1, sources)
            if p < REACH:
                share = beyond_sums(p, lambda m: plane_at(m) if m < 0 else None)
                mid_low[f * REACH + p] = value + rate[p] * share
            else:
                mid_part[f * REACH + p - REACH] = value


def wide_far_kernel(
    where, spots, traces, far, far_old, now, mid_low, mid_part, rate, to_y,
    mid_high, to_far, mid_far, padded,
):
    depth = rate.shape[0]
    high = depth - REACH
    sources = (where, spots, traces)
    clear_edges(padded)
    for f in range(2):

        def plane_at(m):
            if m < depth:
                return now[f * depth + m]
            return far[f * depth + 2 * depth - 1 - m]

        def mid_at(m):
            if m < high:
                return mid_low[f * REACH + m]
            return mid_high[f * REACH + m - high] if m < depth else mid_far[f * REACH + m - depth]

        planes = jnp.stack([plane_at(depth + i) for i in range(REACH)])
        totals = full_sums(padded, planes, depth, plane_at, to_y[...])
        for i, total in enumerate(totals):
            value = 2.0 * planes[i] - far_old[f * REACH + REACH - 1 - i]
            value += far[2 * depth + REACH - 1 - i] * total
            mid_far[f * REACH + i] = value + sources_at(f, depth + i, 1, sources)
        for p in range(high, depth):
            share = beyond_sums(p, lambda m: plane_at(m) if m >= depth else None)
            mid_high[f * REACH + p - high] = mid_part[f * REACH + p - high] + rate[p] * share
        planes = mid_high[pl.ds(f * REACH, REACH)]
        for i, total in enumerate(full_sums(padded, planes, high, mid_at, to_y[...])):
            p = high + i
            value = 2.0 * planes[i] - now[f * depth + p] + rate[p] * total
            to_far[f * REACH + i] = value + sources_at(f, p, 2, sources)


def interior_kernel(
    where, spots, traces, now, mid_near, mid_low, mid_high, new_high, rate, to_y,
    new_low, base, partial, padded,
):
    depth = rate.shape[0]
    high = depth - REACH
    sources = (where, spots, traces)
    clear_edges(padded)

    def mid_at(f, m):
        if m < 0:
            return mid_near[f * REACH - 1 - m]
        return mid_low[f * REACH + m] if m < high else mid_high[f * REACH + m - high]

    def new_at(f, m):
        return new_low[f * REACH + m] if m < high else new_high[f * REACH + m - high]

    for f in range(2):
        planes = mid_low[pl.ds(f * REACH, REACH)]
        totals = full_sums(padded, planes, 0, lambda m: mid_at(f, m), to_y[...])
        for p, total in enumerate(totals):
            value = 2.0 * planes[p] - now[f * depth + p] + rate[p] * total
            new_low[f * REACH + p] = value + sources_at(f, p, 2, sources)
    for f in range(2):
        for first, part in ((0, new_low), (high, new_high)):
            planes = part[pl.ds(f * REACH, REACH)]

            def plane_at(m):
                return new_at(f, m) if 0 <= m < depth else None

            for i, total in enumerate(full_sums(padded, planes, first, plane_at, to_y[...])):
                p = first + i
                value = 2.0 * planes[i] - mid_at(f, p) + rate[p] * total
                base[f * depth + p] = value + sources_at(f, p, 3, sources)
    for p in range(depth):
        total = new_at(0, p) * now[depth + p] + mid_at(0, p) * mid_at(1, p)
        partial[p] = total + now[p] * new_at(1, p)


def last_kernel(pick, far, near, base, rate, partial, src_first, rec_first, new, send, image):
    mine = partner()
    depth = rate.shape[0]
    count = send.shape[0] * CAP
    for p in range(depth):
        fields = []
        for f in range(2):

            def plane_at(m):
                if m < 0:
                    return near[mine, f * REACH - 1 - m]
                return far[f * REACH + REACH - 1 - (m - depth)] if m >= depth else None

            value = base[f * depth + p] + rate[p] * beyond_sums(p, plane_at)
            new[f * depth + p] = value
            fields.append(value)
        image[p] = partial[p] + fields[0] * rec_first[p] + src_first[p] * fields[1]
    for c in range(count):
        tiles = [jnp.zeros(send.shape[2:], jnp.float32)] * depth
        for k in range(max(0, c - (count - KT)), min(KT - 1, c) + 1):
            here = pick[k] == c
            at = pl.ds(k * BX, BX)
            tiles = [jnp.where(here, image[p, at], tile) for p, tile in enumerate(tiles)]
        for p, tile in enumerate(tiles):
            send[c // CAP, (c % CAP) * depth + p] = tile


def gather_kernel(put, got, new, out, src_out, rec_out, out_rows, src_rows, rec_rows, sems):
    depth = new.shape[0] // 2
    size_x = new.shape[1]
    count = put.shape[0]
    held = out_rows.shape[0] // (BX * depth)
    copies = []
    for f, (rows, to) in enumerate(((src_rows, src_out), (rec_rows, rec_out))):
        for p in range(depth):
            rows[pl.ds(z_of(p, depth), size_x, stride=depth)] = new[f * depth + p]
        copies.append(pltpu.make_async_copy(rows, to, sems.at[f]))
        copies[-1].start()
    for t in range(held):
        totals = [jnp.zeros(got.shape[2:], jnp.float32)] * depth
        for c in range(count):
            here = put[c] == t
            first = (c % CAP) * depth
            totals = [
                total + jnp.where(here, got[c // CAP, first + p], 0.0)
                for p, total in enumerate(totals)
            ]
        for p, total in enumerate(totals):
            out_rows[pl.ds(t * BX * depth + z_of(p, depth), BX, stride=depth)] = total
    copies.append(pltpu.make_async_copy(out_rows, out, sems.at[2]))
    copies[-1].start()
    for copy in copies:
        copy.wait()


def local(
    src_prev,
    src_cur,
    rec_cur,
    rec_next,
    velocity,
    aperture_tiles,
    wavelet,
    src_x,
    src_z,
    src_y,
    rec_depth,
    rec_data,
):
    slabs = lax.axis_size("slab")
    shots = lax.axis_size("shot")
    far_pairs = []
    for i in range(1, slabs - 1, 2):
        far_pairs += [(i, i + 1), (i + 1, i)]
    near_groups = [[i, i + 1] for i in range(0, slabs, 2)]

    def flat(array):
        return array.reshape(-1, array.shape[-1])

    _, size_x, depth, size_y = src_cur.shape
    raw = (depth * size_x, size_y)
    model = (velocity.shape[0] * depth, size_y)
    one, two = (depth, size_x, size_y), (2 * depth, size_x, size_y)
    halo = (2 * REACH, size_x, size_y)
    wide = (2 * depth + REACH, size_x, size_y)
    buffer = (shots, CAP * depth, BX, size_y)
    dma = pltpu.SemaphoreType.DMA
    padded = VMEM((REACH, size_x + 2 * PAD, size_y), jnp.float32)
    count = shots * CAP
    given = (flat(src_cur), flat(rec_cur), flat(velocity), aperture_tiles)
    given += (src_x, src_z, src_y, rec_depth, wavelet.T)
    scalars = [SMEM(a.shape, a.dtype) for a in given[3:]]
    send, to_far, src, rec, pick, put, where, spots = call(
        start_kernel,
        [
            ((shots, CAP, BX * depth, size_y), HBM), halo, one, one, ((KT, 8, size_y), VMEM, jnp.int32),
            ((count, 8, size_y), VMEM, jnp.int32), (2, 8, size_y), (STEPS, size_x, size_y),
        ],
        [HBM] * 9, *[pltpu.with_memory_space_constraint(a, HBM) for a in given],
        scratch=[
            VMEM(raw, jnp.float32), VMEM(raw, jnp.float32), VMEM(model, jnp.float32), *scalars,
            dma((9,)), dma((count,)),
        ],
    )
    sources = (where, spots, rec_data[0])

    vel_got = lax.all_to_all(send, "shot", 0, 0)
    far = lax.ppermute(to_far, "slab", far_pairs)
    to_near, sums, base, to_y = call(
        first_interior_kernel, [halo, two, two, ((2 * size_y, size_y), VMEM, jnp.bfloat16)],
        [VMEM] * 4, src, rec, flat(src_prev), flat(rec_next), scratch=[padded],
    )
    near = lax.all_gather(to_near, "slab", axis_index_groups=near_groups)
    rate, part = call(
        rate_kernel, [one, two], [VMEM] * 8, pick, vel_got, near, sums, base, *sources
    )
    (now,) = call(first_kernel, [wide], [VMEM] * 3, far, part, rate)

    wide_far = lax.ppermute(now, "slab", far_pairs)
    src_near, rec_near, base = call(
        wide_interior_kernel, [(depth + REACH, size_x, size_y), one, two], [VMEM] * 5,
        now, src, rec, rate, to_y, scratch=[padded],
    )
    src_near = lax.all_gather(src_near, "slab", axis_index_groups=near_groups)
    rec_near = lax.all_gather(rec_near, "slab", axis_index_groups=near_groups)
    mid_near, mid_low, mid_part = call(
        wide_near_kernel, [halo] * 3, [VMEM] * 10,
        *sources, src_near, rec_near, near, now, base, rate, to_y, scratch=[padded],
    )
    mid_high, new_high = call(
        wide_far_kernel, [halo] * 2, [VMEM] * 10,
        *sources, wide_far, far, now, mid_low, mid_part, rate, to_y,
        scratch=[VMEM(halo, jnp.float32), padded],
    )

    far = lax.ppermute(new_high, "slab", far_pairs)
    new_low, base, partial = call(
        interior_kernel, [halo, two, one], [VMEM] * 10,
        *sources, now, mid_near, mid_low, mid_high, new_high, rate, to_y, scratch=[padded],
    )
    near = lax.all_gather(new_low, "slab", axis_index_groups=near_groups)
    new, send = call(
        last_kernel, [two, buffer], [VMEM] * 8,
        pick, far, near, base, rate, partial, src, rec, scratch=[VMEM(one, jnp.float32)],
    )
    image_got = lax.all_to_all(send, "shot", 0, 0)
    image, src, rec = call(
        gather_kernel, [(model, HBM), (raw, HBM), (raw, HBM)], [VMEM] * 3, put, image_got, new,
        scratch=[
            VMEM(model, jnp.float32), VMEM(raw, jnp.float32), VMEM(raw, jnp.float32), dma((3,)),
        ],
    )
    return image.reshape(velocity.shape), src.reshape(src_cur.shape), rec.reshape(src_cur.shape)


def solution(mesh):
    wave = P("shot", None, "slab", None)
    model = P("shot", "slab", None)
    return jax.shard_map(
        local,
        mesh=mesh,
        in_specs=(wave,) * 4 + (model,) + (P(),) * 6 + (P("shot", None, None, None),),
        out_specs=(model, wave, wave),
        check_vma=False,
    )
```

```python
import jax
import jax.numpy as jnp
from jax import lax
from jax.experimental import pallas as pl
from jax.experimental.pallas import tpu as pltpu
from jax.sharding import PartitionSpec as P


BX = 8
KT = 8
STEPS = 4
CAP = 2
REACH = 4
PAD = 8
VMEM = pltpu.VMEM
SMEM = pltpu.SMEM
HBM = pltpu.HBM

SCALE = 5040.0
TAPS = (-43050.0, 8064.0, -1008.0, 128.0, -9.0)


def call(body, outs, in_spaces, *args, scratch=()):
    outs = [o if isinstance(o[0], tuple) else (o, VMEM) for o in outs]
    outs = [o if len(o) == 3 else o + (jnp.float32,) for o in outs]
    size = 8 * 64 * 128
    return pl.pallas_call(
        body,
        out_shape=[jax.ShapeDtypeStruct(s, t) for s, _, t in outs],
        in_specs=[pl.BlockSpec(memory_space=s) for s in in_spaces],
        out_specs=[pl.BlockSpec(memory_space=m) for _, m, _ in outs],
        scratch_shapes=list(scratch),
        compiler_params=pltpu.CompilerParams(vmem_limit_bytes=24 * 1024 * 1024),
        cost_estimate=pl.CostEstimate(
            flops=90 * size, bytes_accessed=32 * size, transcendentals=0
        ),
    )(*args)


def is_odd():
    return lax.rem(lax.axis_index("slab"), 2) == 1


def partner():
    return jnp.where(is_odd(), 0, 1)


def z_of(plane, depth):
    return jnp.where(is_odd(), plane, depth - 1 - plane)


def tap_of(reach):
    weight = jnp.zeros(reach.shape, jnp.float32)
    for r in range(1, REACH + 1):
        weight = jnp.where(reach == r, TAPS[r], weight)
    return weight


def along_y_matrix(size_y):
    shape = (2 * size_y, size_y)
    row = lax.rem(lax.broadcasted_iota(jnp.int32, shape, 0), size_y)
    return tap_of(jnp.abs(row - lax.broadcasted_iota(jnp.int32, shape, 1))).astype(jnp.bfloat16)


def along_y(planes, to_y):
    rows = planes.reshape(-1, planes.shape[2])
    high = rows.astype(jnp.bfloat16)
    low = (rows - high.astype(jnp.float32)).astype(jnp.bfloat16)
    sums = jnp.dot(
        jnp.concatenate([high, low], axis=1), to_y, preferred_element_type=jnp.float32
    )
    return sums.reshape(planes.shape)


def clear_edges(padded):
    count, rows, size_y = padded.shape
    zeros = jnp.zeros((count, PAD, size_y), jnp.float32)
    padded[:, pl.ds(0, PAD)] = zeros
    padded[:, pl.ds(rows - PAD, PAD)] = zeros


def full_sums(padded, planes, first, plane_at, to_y):
    count, size_x, _ = planes.shape
    padded[pl.ds(0, count), pl.ds(PAD, size_x)] = planes
    lines = along_y(planes, to_y)
    sums = []
    for p in range(count):
        total = lines[p] + TAPS[0] * planes[p]
        for r in range(1, REACH + 1):
            terms = padded[p, pl.ds(PAD + r, size_x)] + padded[p, pl.ds(PAD - r, size_x)]
            for other in (plane_at(first + p + r), plane_at(first + p - r)):
                if other is not None:
                    terms += other
            total += TAPS[r] * terms
        sums.append(total)
    return sums


def beyond_sums(plane, plane_at):
    total = 0.0
    for r in range(1, REACH + 1):
        for other in (plane_at(plane + r), plane_at(plane - r)):
            if other is not None:
                total += TAPS[r] * other
    return total


def sources_at(f, number, step, sources):
    where, spots, traces = sources
    added = traces[STEPS - 1 - step].astype(jnp.float32) if f else spots[step]
    here = (where[f] == float(number))[None]
    return jnp.where(here, added.reshape(-1, 8, added.shape[1]), 0.0).reshape(added.shape)


def start_kernel(
    src_in, rec_in, vel_in, tiles_in, x_in, z_in, y_in, depth_in, wavelet_in,
    send, to_far, src, rec, pick, put, where, spots,
    src_raw, rec_raw, vel, tiles, spot_x, spot_z, spot_y, depth_at, wavelet, sems, send_sems,
):
    shot = lax.axis_index("shot")
    moves = [(tiles_in, tiles), (vel_in, vel), (src_in, src_raw), (rec_in, rec_raw)]
    moves += [(x_in, spot_x), (z_in, spot_z), (y_in, spot_y), (depth_in, depth_at)]
    moves += [(wavelet_in, wavelet)]
    copies = [pltpu.make_async_copy(a, b, sems.at[i]) for i, (a, b) in enumerate(moves)]
    for copy in copies:
        copy.start()
    depth, size_x, size_y = src.shape
    rows = BX * depth
    held = vel.shape[0] // rows
    copies[0].wait()
    places = []
    for g in range(send.shape[0]):
        before = jnp.int32(0)
        for k in range(KT):
            before += (tiles[g, k] < shot * BX).astype(jnp.int32)
        for j in range(CAP):
            own = tiles[g, jnp.minimum(before + j, KT - 1)] - shot * BX
            filled = (before + j < KT) & (own >= 0) & (own < held)
            places.append(jnp.where(filled, own, -1))
    copies[1].wait()
    for c, own in enumerate(places):
        at = pl.multiple_of(jnp.maximum(own, 0) * rows, rows)
        copy = pltpu.make_async_copy(
            vel.at[pl.ds(at, rows)], send.at[c // CAP, c % CAP], send_sems.at[c]
        )
        copy.start()
        copies.append(copy)
    for f, (raw, field) in enumerate(((src_raw, src), (rec_raw, rec))):
        copies[2 + f].wait()
        for p in range(depth):
            plane = raw[pl.ds(z_of(p, depth), size_x, stride=depth)]
            field[p] = plane
            if p >= depth - REACH:
                to_far[f * REACH + p - (depth - REACH)] = plane
    tile = (8, size_y)
    for c, own in enumerate(places):
        put[c] = jnp.full(tile, own)
    previous = jnp.int32(-1)
    for k in range(KT):
        owner = lax.shift_right_logical(tiles[shot, k], 3)
        place = owner * CAP + (previous == owner).astype(jnp.int32)
        previous = owner
        pick[k] = jnp.full(tile, place)
    for copy in copies[4:9]:
        copy.wait()
    first = lax.axis_index("slab") * depth
    for f, local in enumerate((spot_z[shot] - first, depth_at[shot] - first)):
        where[f] = jnp.full(tile, z_of(local, depth)).astype(jnp.float32)
    row = lax.broadcasted_iota(jnp.int32, (size_x, size_y), 0)
    lane = lax.broadcasted_iota(jnp.int32, (size_x, size_y), 1)
    here = (row == spot_x[shot]) & (lane == spot_y[shot])
    for step in range(STEPS):
        spots[step] = jnp.where(here, wavelet[step, shot], 0.0)
    for copy in copies[9:]:
        copy.wait()


def first_interior_kernel(src, rec, src_old, rec_old, to_near, sums, base, to_y, padded):
    depth, size_x, size_y = src.shape
    to_y[...] = along_y_matrix(size_y)
    clear_edges(padded)
    for f, (field, old) in enumerate(((src, src_old), (rec, rec_old))):

        def plane_at(m):
            return field[m] if 0 <= m < depth else None

        for first in range(0, depth, REACH):
            planes = field[pl.ds(first, REACH)]
            if first == 0:
                to_near[pl.ds(f * REACH, REACH)] = planes
            for i, total in enumerate(full_sums(padded, planes, first, plane_at, to_y[...])):
                p = first + i
                sums[f * depth + p] = total
                before = old[pl.ds(z_of(p, depth), size_x, stride=depth)]
                base[f * depth + p] = 2.0 * planes[i] - before


def rate_kernel(pick, vel_got, near, sums, base, where, spots, traces, rate, part):
    mine = partner()
    depth = rate.shape[0]
    count = vel_got.shape[0] * CAP
    rows = [pl.ds(z_of(p, depth), BX, stride=depth) for p in range(depth)]
    for k in range(KT):
        tiles = [vel_got[k // CAP, k % CAP, at] for at in rows]
        for c in range(k + 1, count - (KT - 1 - k)):
            here = pick[k] == c
            tiles = [
                jnp.where(here, vel_got[c // CAP, c % CAP, at], tile)
                for at, tile in zip(rows, tiles, strict=True)
            ]
        for p, tile in enumerate(tiles):
            rate[p, pl.ds(k * BX, BX)] = tile * tile * (1.0 / SCALE)
    for f in range(2):

        def plane_at(m):
            return near[mine, f * REACH - 1 - m] if m < 0 else None

        for p in range(depth):
            total = sums[f * depth + p]
            if p < REACH:
                total += beyond_sums(p, plane_at)
            added = sources_at(f, p, 0, (where, spots, traces))
            part[f * depth + p] = base[f * depth + p] + rate[p] * total + added


def first_kernel(far, part, rate, now):
    depth = rate.shape[0]
    for f in range(2):

        def plane_at(m):
            return far[f * REACH + REACH - 1 - (m - depth)] if m >= depth else None

        for p in range(depth):
            value = part[f * depth + p]
            if p >= depth - REACH:
                value += rate[p] * beyond_sums(p, plane_at)
            now[f * depth + p] = value
    now[pl.ds(2 * depth, REACH)] = rate[pl.ds(depth - REACH, REACH)]


def wide_interior_kernel(
    now, src_old, rec_old, rate, to_y, src_near, rec_near, base, padded
):
    depth = rate.shape[0]
    clear_edges(padded)
    src_near[pl.ds(0, depth)] = now[pl.ds(0, depth)]
    src_near[pl.ds(depth, REACH)] = rate[pl.ds(0, REACH)]
    rec_near[...] = now[pl.ds(depth, depth)]
    for f, old in enumerate((src_old, rec_old)):

        def plane_at(m):
            return now[f * depth + m] if 0 <= m < depth else None

        for first in range(0, depth, REACH):
            planes = now[pl.ds(f * depth + first, REACH)]
            for i, total in enumerate(full_sums(padded, planes, first, plane_at, to_y[...])):
                p = first + i
                base[f * depth + p] = 2.0 * planes[i] - old[p] + rate[p] * total


def wide_near_kernel(
    where, spots, traces, src_near, rec_near, near_old, now, base, rate, to_y,
    mid_near, mid_low, mid_part, padded,
):
    depth = rate.shape[0]
    mine = partner()
    sources = (where, spots, traces)
    clear_edges(padded)
    for f, near in enumerate((src_near, rec_near)):

        def plane_at(m):
            if m >= 0:
                return now[f * depth + m]
            return near[mine, -1 - m]

        planes = near[mine, pl.ds(0, REACH)]
        totals = full_sums(padded, planes, 0, lambda m: plane_at(-1 - m), to_y[...])
        for i, total in enumerate(totals):
            value = 2.0 * planes[i] - near_old[mine, f * REACH + i]
            value += src_near[mine, depth + i] * total
            mid_near[f * REACH + i] = value + sources_at(f, -1 - i, 1, sources)
        for p in range(depth):
            value = base[f * depth + p] + sources_at(f, p, 1, sources)
            if p < REACH:
                share = beyond_sums(p, lambda m: plane_at(m) if m < 0 else None)
                mid_low[f * REACH + p] = value + rate[p] * share
            else:
                mid_part[f * REACH + p - REACH] = value


def wide_far_kernel(
    where, spots, traces, far, far_old, now, mid_low, mid_part, rate, to_y,
    mid_high, to_far, mid_far, padded,
):
    depth = rate.shape[0]
    high = depth - REACH
    sources = (where, spots, traces)
    clear_edges(padded)
    work = [padded.at[pl.ds(i * REACH, REACH)] for i in range(4)]

    def mid_at(f, m):
        if m < high:
            return mid_low[f * REACH + m]
        return mid_high[f * REACH + m - high] if m < depth else mid_far[f * REACH + m - depth]

    for f in range(2):

        def plane_at(m):
            if m < depth:
                return now[f * depth + m]
            return far[f * depth + 2 * depth - 1 - m]

        for p in range(high, depth):
            share = beyond_sums(p, lambda m: plane_at(m) if m >= depth else None)
            mid_high[f * REACH + p - high] = mid_part[f * REACH + p - high] + rate[p] * share
        planes = jnp.stack([plane_at(depth + i) for i in range(REACH)])
        totals = full_sums(work[f], planes, depth, plane_at, to_y[...])
        for i, total in enumerate(totals):
            value = 2.0 * planes[i] - far_old[f * REACH + REACH - 1 - i]
            value += far[2 * depth + REACH - 1 - i] * total
            mid_far[f * REACH + i] = value + sources_at(f, depth + i, 1, sources)
    for f in range(2):
        planes = mid_high[pl.ds(f * REACH, REACH)]
        totals = full_sums(work[2 + f], planes, high, lambda m: mid_at(f, m), to_y[...])
        for i, total in enumerate(totals):
            p = high + i
            value = 2.0 * planes[i] - now[f * depth + p] + rate[p] * total
            to_far[f * REACH + i] = value + sources_at(f, p, 2, sources)


def interior_kernel(
    where, spots, traces, now, mid_near, mid_low, mid_high, new_high, rate, to_y,
    new_low, base, partial, padded,
):
    depth = rate.shape[0]
    high = depth - REACH
    sources = (where, spots, traces)
    clear_edges(padded)

    def mid_at(f, m):
        if m < 0:
            return mid_near[f * REACH - 1 - m]
        return mid_low[f * REACH + m] if m < high else mid_high[f * REACH + m - high]

    def new_at(f, m):
        return new_low[f * REACH + m] if m < high else new_high[f * REACH + m - high]

    for f in range(2):
        planes = mid_low[pl.ds(f * REACH, REACH)]
        totals = full_sums(padded, planes, 0, lambda m: mid_at(f, m), to_y[...])
        for p, total in enumerate(totals):
            value = 2.0 * planes[p] - now[f * depth + p] + rate[p] * total
            new_low[f * REACH + p] = value + sources_at(f, p, 2, sources)
    for f in range(2):
        for first, part in ((0, new_low), (high, new_high)):
            planes = part[pl.ds(f * REACH, REACH)]

            def plane_at(m):
                return new_at(f, m) if 0 <= m < depth else None

            for i, total in enumerate(full_sums(padded, planes, first, plane_at, to_y[...])):
                p = first + i
                value = 2.0 * planes[i] - mid_at(f, p) + rate[p] * total
                base[f * depth + p] = value + sources_at(f, p, 3, sources)
    for p in range(depth):
        total = new_at(0, p) * now[depth + p] + mid_at(0, p) * mid_at(1, p)
        partial[p] = total + now[p] * new_at(1, p)


def last_kernel(
    pick, far, near, base, rate, partial, src_first, rec_first, src_rows, rec_rows, send, image
):
    mine = partner()
    depth = rate.shape[0]
    count = send.shape[0] * CAP
    for p in range(depth):
        fields = []
        at = pl.ds(z_of(p, depth), rate.shape[1], stride=depth)
        for f, rows in enumerate((src_rows, rec_rows)):

            def plane_at(m):
                if m < 0:
                    return near[mine, f * REACH - 1 - m]
                return far[f * REACH + REACH - 1 - (m - depth)] if m >= depth else None

            value = base[f * depth + p] + rate[p] * beyond_sums(p, plane_at)
            rows[at] = value
            fields.append(value)
        image[p] = partial[p] + fields[0] * rec_first[p] + src_first[p] * fields[1]
    for c in range(count):
        tiles = [jnp.zeros(send.shape[2:], jnp.float32)] * depth
        for k in range(max(0, c - (count - KT)), min(KT - 1, c) + 1):
            here = pick[k] == c
            at = pl.ds(k * BX, BX)
            tiles = [jnp.where(here, image[p, at], tile) for p, tile in enumerate(tiles)]
        for p, tile in enumerate(tiles):
            send[c // CAP, (c % CAP) * depth + p] = tile


def gather_kernel(put, got, src_rows, rec_rows, out, src_out, rec_out, out_rows, sems):
    depth = got.shape[1] // CAP
    count = put.shape[0]
    held = out_rows.shape[0] // (BX * depth)
    copies = []
    for f, (rows, to) in enumerate(((src_rows, src_out), (rec_rows, rec_out))):
        copies.append(pltpu.make_async_copy(rows, to, sems.at[f]))
        copies[-1].start()
    for t in range(held):
        totals = [jnp.zeros(got.shape[2:], jnp.float32)] * depth
        for c in range(count):
            here = put[c] == t
            first = (c % CAP) * depth
            totals = [
                total + jnp.where(here, got[c // CAP, first + p], 0.0)
                for p, total in enumerate(totals)
            ]
        for p, total in enumerate(totals):
            out_rows[pl.ds(t * BX * depth + z_of(p, depth), BX, stride=depth)] = total
        if t % 2:
            part = pl.ds((t - 1) * BX * depth, 2 * BX * depth)
            copies.append(pltpu.make_async_copy(out_rows.at[part], out.at[part], sems.at[2 + t // 2]))
            copies[-1].start()
    for copy in copies:
        copy.wait()


def local(
    src_prev,
    src_cur,
    rec_cur,
    rec_next,
    velocity,
    aperture_tiles,
    wavelet,
    src_x,
    src_z,
    src_y,
    rec_depth,
    rec_data,
):
    slabs = lax.axis_size("slab")
    shots = lax.axis_size("shot")
    far_pairs = []
    for i in range(1, slabs - 1, 2):
        far_pairs += [(i, i + 1), (i + 1, i)]
    near_groups = [[i, i + 1] for i in range(0, slabs, 2)]

    def flat(array):
        return array.reshape(-1, array.shape[-1])

    _, size_x, depth, size_y = src_cur.shape
    raw = (depth * size_x, size_y)
    model = (velocity.shape[0] * depth, size_y)
    one, two = (depth, size_x, size_y), (2 * depth, size_x, size_y)
    halo = (2 * REACH, size_x, size_y)
    wide = (2 * depth + REACH, size_x, size_y)
    buffer = (shots, CAP * depth, BX, size_y)
    dma = pltpu.SemaphoreType.DMA
    padded = VMEM((REACH, size_x + 2 * PAD, size_y), jnp.float32)
    count = shots * CAP
    given = (flat(src_cur), flat(rec_cur), flat(velocity), aperture_tiles)
    given += (src_x, src_z, src_y, rec_depth, wavelet.T)
    scalars = [SMEM(a.shape, a.dtype) for a in given[3:]]
    send, to_far, src, rec, pick, put, where, spots = call(
        start_kernel,
        [
            ((shots, CAP, BX * depth, size_y), HBM), halo, one, one, ((KT, 8, size_y), VMEM, jnp.int32),
            ((count, 8, size_y), VMEM, jnp.int32), (2, 8, size_y), (STEPS, size_x, size_y),
        ],
        [HBM] * 9, *[pltpu.with_memory_space_constraint(a, HBM) for a in given],
        scratch=[
            VMEM(raw, jnp.float32), VMEM(raw, jnp.float32), VMEM(model, jnp.float32), *scalars,
            dma((9,)), dma((count,)),
        ],
    )
    sources = (where, spots, rec_data[0])

    vel_got = lax.all_to_all(send, "shot", 0, 0)
    far = lax.ppermute(to_far, "slab", far_pairs)
    to_near, sums, base, to_y = call(
        first_interior_kernel, [halo, two, two, ((2 * size_y, size_y), VMEM, jnp.bfloat16)],
        [VMEM] * 4, src, rec, flat(src_prev), flat(rec_next), scratch=[padded],
    )
    near = lax.all_gather(to_near, "slab", axis_index_groups=near_groups)
    rate, part = call(
        rate_kernel, [one, two], [VMEM] * 8, pick, vel_got, near, sums, base, *sources
    )
    (now,) = call(first_kernel, [wide], [VMEM] * 3, far, part, rate)

    wide_far = lax.ppermute(now, "slab", far_pairs)
    src_near, rec_near, base = call(
        wide_interior_kernel, [(depth + REACH, size_x, size_y), one, two], [VMEM] * 5,
        now, src, rec, rate, to_y, scratch=[padded],
    )
    src_near = lax.all_gather(src_near, "slab", axis_index_groups=near_groups)
    rec_near = lax.all_gather(rec_near, "slab", axis_index_groups=near_groups)
    mid_near, mid_low, mid_part = call(
        wide_near_kernel, [halo] * 3, [VMEM] * 10,
        *sources, src_near, rec_near, near, now, base, rate, to_y, scratch=[padded],
    )
    mid_high, new_high = call(
        wide_far_kernel, [halo] * 2, [VMEM] * 10,
        *sources, wide_far, far, now, mid_low, mid_part, rate, to_y,
        scratch=[
            VMEM(halo, jnp.float32),
            VMEM((4 * REACH, size_x + 2 * PAD, size_y), jnp.float32),
        ],
    )

    far = lax.ppermute(new_high, "slab", far_pairs)
    new_low, base, partial = call(
        interior_kernel, [halo, two, one], [VMEM] * 10,
        *sources, now, mid_near, mid_low, mid_high, new_high, rate, to_y, scratch=[padded],
    )
    near = lax.all_gather(new_low, "slab", axis_index_groups=near_groups)
    src_rows, rec_rows, send = call(
        last_kernel, [raw, raw, buffer], [VMEM] * 8,
        pick, far, near, base, rate, partial, src, rec, scratch=[VMEM(one, jnp.float32)],
    )
    image_got = lax.all_to_all(send, "shot", 0, 0)
    image, src, rec = call(
        gather_kernel, [(model, HBM), (raw, HBM), (raw, HBM)], [VMEM] * 4,
        put, image_got, src_rows, rec_rows,
        scratch=[VMEM(model, jnp.float32), dma((2 + velocity.shape[0] // BX // 2,))],
    )
    return image.reshape(velocity.shape), src.reshape(src_cur.shape), rec.reshape(src_cur.shape)


def solution(mesh):
    wave = P("shot", None, "slab", None)
    model = P("shot", "slab", None)
    return jax.shard_map(
        local,
        mesh=mesh,
        in_specs=(wave,) * 4 + (model,) + (P(),) * 6 + (P("shot", None, None, None),),
        out_specs=(model, wave, wave),
        check_vma=False,
    )
```

```python
import jax
import jax.numpy as jnp
from jax import lax
from jax.experimental import pallas as pl
from jax.experimental.pallas import tpu as pltpu
from jax.sharding import PartitionSpec as P


BX = 8
KT = 8
STEPS = 4
CAP = 2
REACH = 4
PAD = 8
VMEM = pltpu.VMEM
SMEM = pltpu.SMEM
HBM = pltpu.HBM

SCALE = 5040.0
TAPS = (-43050.0, 8064.0, -1008.0, 128.0, -9.0)


def call(body, outs, in_spaces, *args, scratch=()):
    outs = [o if isinstance(o[0], tuple) else (o, VMEM) for o in outs]
    outs = [o if len(o) == 3 else o + (jnp.float32,) for o in outs]
    size = 8 * 64 * 128
    return pl.pallas_call(
        body,
        out_shape=[jax.ShapeDtypeStruct(s, t) for s, _, t in outs],
        in_specs=[pl.BlockSpec(memory_space=s) for s in in_spaces],
        out_specs=[pl.BlockSpec(memory_space=m) for _, m, _ in outs],
        scratch_shapes=list(scratch),
        compiler_params=pltpu.CompilerParams(vmem_limit_bytes=24 * 1024 * 1024),
        cost_estimate=pl.CostEstimate(
            flops=90 * size, bytes_accessed=32 * size, transcendentals=0
        ),
    )(*args)


def is_odd():
    return lax.rem(lax.axis_index("slab"), 2) == 1


def partner():
    return jnp.where(is_odd(), 0, 1)


def z_of(plane, depth):
    return jnp.where(is_odd(), plane, depth - 1 - plane)


def tap_of(reach):
    weight = jnp.zeros(reach.shape, jnp.float32)
    for r in range(1, REACH + 1):
        weight = jnp.where(reach == r, TAPS[r], weight)
    return weight


def along_y_matrix(size_y):
    shape = (2 * size_y, size_y)
    row = lax.rem(lax.broadcasted_iota(jnp.int32, shape, 0), size_y)
    return tap_of(jnp.abs(row - lax.broadcasted_iota(jnp.int32, shape, 1))).astype(jnp.bfloat16)


def along_y(planes, to_y):
    rows = planes.reshape(-1, planes.shape[2])
    high = rows.astype(jnp.bfloat16)
    low = (rows - high.astype(jnp.float32)).astype(jnp.bfloat16)
    sums = jnp.dot(
        jnp.concatenate([high, low], axis=1), to_y, preferred_element_type=jnp.float32
    )
    return sums.reshape(planes.shape)


def clear_edges(padded):
    count, rows, size_y = padded.shape
    zeros = jnp.zeros((count, PAD, size_y), jnp.float32)
    padded[:, pl.ds(0, PAD)] = zeros
    padded[:, pl.ds(rows - PAD, PAD)] = zeros


def full_sums(padded, planes, first, plane_at, to_y):
    count, size_x, _ = planes.shape
    padded[pl.ds(0, count), pl.ds(PAD, size_x)] = planes
    lines = along_y(planes, to_y)
    sums = []
    for p in range(count):
        total = lines[p] + TAPS[0] * planes[p]
        for r in range(1, REACH + 1):
            terms = padded[p, pl.ds(PAD + r, size_x)] + padded[p, pl.ds(PAD - r, size_x)]
            for other in (plane_at(first + p + r), plane_at(first + p - r)):
                if other is not None:
                    terms += other
            total += TAPS[r] * terms
        sums.append(total)
    return sums


def beyond_sums(plane, plane_at):
    total = 0.0
    for r in range(1, REACH + 1):
        for other in (plane_at(plane + r), plane_at(plane - r)):
            if other is not None:
                total += TAPS[r] * other
    return total


def sources_at(f, number, step, sources):
    where, spots, traces = sources
    added = traces[STEPS - 1 - step].astype(jnp.float32) if f else spots[step]
    here = (where[f] == float(number))[None]
    return jnp.where(here, added.reshape(-1, 8, added.shape[1]), 0.0).reshape(added.shape)


def start_kernel(
    src_in, rec_in, vel_in, tiles_in, x_in, z_in, y_in, depth_in, wavelet_in,
    send, to_far, src, rec, pick, put, where, spots,
    src_raw, rec_raw, vel, tiles, spot_x, spot_z, spot_y, depth_at, wavelet, sems, send_sems,
):
    shot = lax.axis_index("shot")
    moves = [(tiles_in, tiles), (vel_in, vel), (src_in, src_raw), (rec_in, rec_raw)]
    moves += [(x_in, spot_x), (z_in, spot_z), (y_in, spot_y), (depth_in, depth_at)]
    moves += [(wavelet_in, wavelet)]
    copies = [pltpu.make_async_copy(a, b, sems.at[i]) for i, (a, b) in enumerate(moves)]
    for copy in copies:
        copy.start()
    depth, size_x, size_y = src.shape
    rows = BX * depth
    held = vel.shape[0] // rows
    copies[0].wait()
    places = []
    for g in range(send.shape[0]):
        before = jnp.int32(0)
        for k in range(KT):
            before += (tiles[g, k] < shot * BX).astype(jnp.int32)
        for j in range(CAP):
            own = tiles[g, jnp.minimum(before + j, KT - 1)] - shot * BX
            filled = (before + j < KT) & (own >= 0) & (own < held)
            places.append(jnp.where(filled, own, -1))
    copies[1].wait()
    sends = []
    for c, own in enumerate(places):
        at = pl.multiple_of(jnp.maximum(own, 0) * rows, rows)
        copy = pltpu.make_async_copy(
            vel.at[pl.ds(at, rows)], send.at[c // CAP, c % CAP], send_sems.at[c]
        )
        pl.when(own >= 0)(copy.start)
        sends.append((own, copy))
    for f, (raw, field) in enumerate(((src_raw, src), (rec_raw, rec))):
        copies[2 + f].wait()
        for p in range(depth):
            plane = raw[pl.ds(z_of(p, depth), size_x, stride=depth)]
            field[p] = plane
            if p >= depth - REACH:
                to_far[f * REACH + p - (depth - REACH)] = plane
    tile = (8, size_y)
    for c, own in enumerate(places):
        put[c] = jnp.full(tile, own)
    previous = jnp.int32(-1)
    for k in range(KT):
        owner = lax.shift_right_logical(tiles[shot, k], 3)
        place = owner * CAP + (previous == owner).astype(jnp.int32)
        previous = owner
        pick[k] = jnp.full(tile, place)
    for copy in copies[4:9]:
        copy.wait()
    first = lax.axis_index("slab") * depth
    for f, local in enumerate((spot_z[shot] - first, depth_at[shot] - first)):
        where[f] = jnp.full(tile, z_of(local, depth)).astype(jnp.float32)
    row = lax.broadcasted_iota(jnp.int32, (size_x, size_y), 0)
    lane = lax.broadcasted_iota(jnp.int32, (size_x, size_y), 1)
    here = (row == spot_x[shot]) & (lane == spot_y[shot])
    for step in range(STEPS):
        spots[step] = jnp.where(here, wavelet[step, shot], 0.0)
    for own, copy in sends:
        pl.when(own >= 0)(copy.wait)


def first_interior_kernel(src, rec, src_old, rec_old, to_near, sums, base, to_y, padded):
    depth, size_x, size_y = src.shape
    to_y[...] = along_y_matrix(size_y)
    clear_edges(padded)
    for f, (field, old) in enumerate(((src, src_old), (rec, rec_old))):

        def plane_at(m):
            return field[m] if 0 <= m < depth else None

        for first in range(0, depth, REACH):
            planes = field[pl.ds(first, REACH)]
            if first == 0:
                to_near[pl.ds(f * REACH, REACH)] = planes
            for i, total in enumerate(full_sums(padded, planes, first, plane_at, to_y[...])):
                p = first + i
                sums[f * depth + p] = total
                before = old[pl.ds(z_of(p, depth), size_x, stride=depth)]
                base[f * depth + p] = 2.0 * planes[i] - before


def rate_kernel(pick, vel_got, near, sums, base, where, spots, traces, rate, part):
    mine = partner()
    depth = rate.shape[0]
    count = vel_got.shape[0] * CAP
    rows = [pl.ds(z_of(p, depth), BX, stride=depth) for p in range(depth)]
    for k in range(KT):
        tiles = [vel_got[k // CAP, k % CAP, at] for at in rows]
        for c in range(k + 1, count - (KT - 1 - k)):
            here = pick[k] == c
            tiles = [
                jnp.where(here, vel_got[c // CAP, c % CAP, at], tile)
                for at, tile in zip(rows, tiles, strict=True)
            ]
        for p, tile in enumerate(tiles):
            rate[p, pl.ds(k * BX, BX)] = tile * tile * (1.0 / SCALE)
    for f in range(2):

        def plane_at(m):
            return near[mine, f * REACH - 1 - m] if m < 0 else None

        for p in range(depth):
            total = sums[f * depth + p]
            if p < REACH:
                total += beyond_sums(p, plane_at)
            added = sources_at(f, p, 0, (where, spots, traces))
            part[f * depth + p] = base[f * depth + p] + rate[p] * total + added


def first_kernel(far, part, rate, now):
    depth = rate.shape[0]
    for f in range(2):

        def plane_at(m):
            return far[f * REACH + REACH - 1 - (m - depth)] if m >= depth else None

        for p in range(depth):
            value = part[f * depth + p]
            if p >= depth - REACH:
                value += rate[p] * beyond_sums(p, plane_at)
            now[f * depth + p] = value
    now[pl.ds(2 * depth, REACH)] = rate[pl.ds(depth - REACH, REACH)]


def wide_interior_kernel(
    now, src_old, rec_old, rate, to_y, src_near, rec_near, base, padded
):
    depth = rate.shape[0]
    clear_edges(padded)
    src_near[pl.ds(0, depth)] = now[pl.ds(0, depth)]
    src_near[pl.ds(depth, REACH)] = rate[pl.ds(0, REACH)]
    rec_near[...] = now[pl.ds(depth, depth)]
    for f, old in enumerate((src_old, rec_old)):

        def plane_at(m):
            return now[f * depth + m] if 0 <= m < depth else None

        for first in range(0, depth, REACH):
            planes = now[pl.ds(f * depth + first, REACH)]
            for i, total in enumerate(full_sums(padded, planes, first, plane_at, to_y[...])):
                p = first + i
                base[f * depth + p] = 2.0 * planes[i] - old[p] + rate[p] * total


def wide_near_kernel(
    where, spots, traces, src_near, rec_near, near_old, now, base, rate, to_y,
    mid_near, mid_low, mid_part, padded,
):
    depth = rate.shape[0]
    mine = partner()
    sources = (where, spots, traces)
    clear_edges(padded)
    for f, near in enumerate((src_near, rec_near)):

        def plane_at(m):
            if m >= 0:
                return now[f * depth + m]
            return near[mine, -1 - m]

        planes = near[mine, pl.ds(0, REACH)]
        totals = full_sums(padded, planes, 0, lambda m: plane_at(-1 - m), to_y[...])
        for i, total in enumerate(totals):
            value = 2.0 * planes[i] - near_old[mine, f * REACH + i]
            value += src_near[mine, depth + i] * total
            mid_near[f * REACH + i] = value + sources_at(f, -1 - i, 1, sources)
        for p in range(depth):
            value = base[f * depth + p] + sources_at(f, p, 1, sources)
            if p < REACH:
                share = beyond_sums(p, lambda m: plane_at(m) if m < 0 else None)
                mid_low[f * REACH + p] = value + rate[p] * share
            else:
                mid_part[f * REACH + p - REACH] = value


def wide_far_kernel(
    where, spots, traces, far, far_old, now, mid_low, mid_part, rate, to_y,
    mid_high, to_far, mid_far, padded,
):
    depth = rate.shape[0]
    high = depth - REACH
    sources = (where, spots, traces)
    clear_edges(padded)
    work = [padded.at[pl.ds(i * REACH, REACH)] for i in range(4)]

    def mid_at(f, m):
        if m < high:
            return mid_low[f * REACH + m]
        return mid_high[f * REACH + m - high] if m < depth else mid_far[f * REACH + m - depth]

    for f in range(2):

        def plane_at(m):
            if m < depth:
                return now[f * depth + m]
            return far[f * depth + 2 * depth - 1 - m]

        for p in range(high, depth):
            share = beyond_sums(p, lambda m: plane_at(m) if m >= depth else None)
            mid_high[f * REACH + p - high] = mid_part[f * REACH + p - high] + rate[p] * share
        planes = jnp.stack([plane_at(depth + i) for i in range(REACH)])
        totals = full_sums(work[f], planes, depth, plane_at, to_y[...])
        for i, total in enumerate(totals):
            value = 2.0 * planes[i] - far_old[f * REACH + REACH - 1 - i]
            value += far[2 * depth + REACH - 1 - i] * total
            mid_far[f * REACH + i] = value + sources_at(f, depth + i, 1, sources)
    for f in range(2):
        planes = mid_high[pl.ds(f * REACH, REACH)]
        totals = full_sums(work[2 + f], planes, high, lambda m: mid_at(f, m), to_y[...])
        for i, total in enumerate(totals):
            p = high + i
            value = 2.0 * planes[i] - now[f * depth + p] + rate[p] * total
            to_far[f * REACH + i] = value + sources_at(f, p, 2, sources)


def interior_kernel(
    where, spots, traces, now, mid_near, mid_low, mid_high, new_high, rate, to_y,
    new_low, base, partial, padded,
):
    depth = rate.shape[0]
    high = depth - REACH
    sources = (where, spots, traces)
    clear_edges(padded)

    def mid_at(f, m):
        if m < 0:
            return mid_near[f * REACH - 1 - m]
        return mid_low[f * REACH + m] if m < high else mid_high[f * REACH + m - high]

    def new_at(f, m):
        return new_low[f * REACH + m] if m < high else new_high[f * REACH + m - high]

    for f in range(2):
        planes = mid_low[pl.ds(f * REACH, REACH)]
        totals = full_sums(padded, planes, 0, lambda m: mid_at(f, m), to_y[...])
        for p, total in enumerate(totals):
            value = 2.0 * planes[p] - now[f * depth + p] + rate[p] * total
            new_low[f * REACH + p] = value + sources_at(f, p, 2, sources)
    for f in range(2):
        for first, part in ((0, new_low), (high, new_high)):
            planes = part[pl.ds(f * REACH, REACH)]

            def plane_at(m):
                return new_at(f, m) if 0 <= m < depth else None

            for i, total in enumerate(full_sums(padded, planes, first, plane_at, to_y[...])):
                p = first + i
                value = 2.0 * planes[i] - mid_at(f, p) + rate[p] * total
                base[f * depth + p] = value + sources_at(f, p, 3, sources)
    for p in range(depth):
        total = new_at(0, p) * now[depth + p] + mid_at(0, p) * mid_at(1, p)
        partial[p] = total + now[p] * new_at(1, p)


def last_kernel(
    pick, far, near, base, rate, partial, src_first, rec_first, src_rows, rec_rows, send, image
):
    mine = partner()
    depth = rate.shape[0]
    count = send.shape[0] * CAP
    for p in range(depth):
        fields = []
        at = pl.ds(z_of(p, depth), rate.shape[1], stride=depth)
        for f, rows in enumerate((src_rows, rec_rows)):

            def plane_at(m):
                if m < 0:
                    return near[mine, f * REACH - 1 - m]
                return far[f * REACH + REACH - 1 - (m - depth)] if m >= depth else None

            value = base[f * depth + p] + rate[p] * beyond_sums(p, plane_at)
            rows[at] = value
            fields.append(value)
        image[p] = partial[p] + fields[0] * rec_first[p] + src_first[p] * fields[1]
    for c in range(count):
        tiles = [jnp.zeros(send.shape[2:], jnp.float32)] * depth
        for k in range(max(0, c - (count - KT)), min(KT - 1, c) + 1):
            here = pick[k] == c
            at = pl.ds(k * BX, BX)
            tiles = [jnp.where(here, image[p, at], tile) for p, tile in enumerate(tiles)]
        for p, tile in enumerate(tiles):
            send[c // CAP, (c % CAP) * depth + p] = tile


def gather_kernel(put, got, src_rows, rec_rows, out, src_out, rec_out, out_rows, sems):
    depth = got.shape[1] // CAP
    count = put.shape[0]
    held = out_rows.shape[0] // (BX * depth)
    copies = []
    for f, (rows, to) in enumerate(((src_rows, src_out), (rec_rows, rec_out))):
        copies.append(pltpu.make_async_copy(rows, to, sems.at[f]))
        copies[-1].start()
    for t in range(held):
        totals = [jnp.zeros(got.shape[2:], jnp.float32)] * depth
        for c in range(count):
            here = put[c] == t
            first = (c % CAP) * depth
            totals = [
                total + jnp.where(here, got[c // CAP, first + p], 0.0)
                for p, total in enumerate(totals)
            ]
        for p, total in enumerate(totals):
            out_rows[pl.ds(t * BX * depth + z_of(p, depth), BX, stride=depth)] = total
        if t % 2:
            part = pl.ds((t - 1) * BX * depth, 2 * BX * depth)
            copies.append(pltpu.make_async_copy(out_rows.at[part], out.at[part], sems.at[2 + t // 2]))
            copies[-1].start()
    for copy in copies:
        copy.wait()


def local(
    src_prev,
    src_cur,
    rec_cur,
    rec_next,
    velocity,
    aperture_tiles,
    wavelet,
    src_x,
    src_z,
    src_y,
    rec_depth,
    rec_data,
):
    slabs = lax.axis_size("slab")
    shots = lax.axis_size("shot")
    far_pairs = []
    for i in range(1, slabs - 1, 2):
        far_pairs += [(i, i + 1), (i + 1, i)]
    near_groups = [[i, i + 1] for i in range(0, slabs, 2)]

    def flat(array):
        return array.reshape(-1, array.shape[-1])

    _, size_x, depth, size_y = src_cur.shape
    raw = (depth * size_x, size_y)
    model = (velocity.shape[0] * depth, size_y)
    one, two = (depth, size_x, size_y), (2 * depth, size_x, size_y)
    halo = (2 * REACH, size_x, size_y)
    wide = (2 * depth + REACH, size_x, size_y)
    buffer = (shots, CAP * depth, BX, size_y)
    dma = pltpu.SemaphoreType.DMA
    padded = VMEM((REACH, size_x + 2 * PAD, size_y), jnp.float32)
    count = shots * CAP
    given = (flat(src_cur), flat(rec_cur), flat(velocity), aperture_tiles)
    given += (src_x, src_z, src_y, rec_depth, wavelet.T)
    scalars = [SMEM(a.shape, a.dtype) for a in given[3:]]
    send, to_far, src, rec, pick, put, where, spots = call(
        start_kernel,
        [
            ((shots, CAP, BX * depth, size_y), HBM), halo, one, one, ((KT, 8, size_y), VMEM, jnp.int32),
            ((count, 8, size_y), VMEM, jnp.int32), (2, 8, size_y), (STEPS, size_x, size_y),
        ],
        [HBM] * 9, *[pltpu.with_memory_space_constraint(a, HBM) for a in given],
        scratch=[
            VMEM(raw, jnp.float32), VMEM(raw, jnp.float32), VMEM(model, jnp.float32), *scalars,
            dma((9,)), dma((count,)),
        ],
    )
    sources = (where, spots, rec_data[0])

    vel_got = lax.all_to_all(send, "shot", 0, 0)
    far = lax.ppermute(to_far, "slab", far_pairs)
    to_near, sums, base, to_y = call(
        first_interior_kernel, [halo, two, two, ((2 * size_y, size_y), VMEM, jnp.bfloat16)],
        [VMEM] * 4, src, rec, flat(src_prev), flat(rec_next), scratch=[padded],
    )
    near = lax.all_gather(to_near, "slab", axis_index_groups=near_groups)
    rate, part = call(
        rate_kernel, [one, two], [VMEM] * 8, pick, vel_got, near, sums, base, *sources
    )
    (now,) = call(first_kernel, [wide], [VMEM] * 3, far, part, rate)

    wide_far = lax.ppermute(now, "slab", far_pairs)
    src_near, rec_near, base = call(
        wide_interior_kernel, [(depth + REACH, size_x, size_y), one, two], [VMEM] * 5,
        now, src, rec, rate, to_y, scratch=[padded],
    )
    src_near = lax.all_gather(src_near, "slab", axis_index_groups=near_groups)
    rec_near = lax.all_gather(rec_near, "slab", axis_index_groups=near_groups)
    mid_near, mid_low, mid_part = call(
        wide_near_kernel, [halo] * 3, [VMEM] * 10,
        *sources, src_near, rec_near, near, now, base, rate, to_y, scratch=[padded],
    )
    mid_high, new_high = call(
        wide_far_kernel, [halo] * 2, [VMEM] * 10,
        *sources, wide_far, far, now, mid_low, mid_part, rate, to_y,
        scratch=[
            VMEM(halo, jnp.float32),
            VMEM((4 * REACH, size_x + 2 * PAD, size_y), jnp.float32),
        ],
    )

    far = lax.ppermute(new_high, "slab", far_pairs)
    new_low, base, partial = call(
        interior_kernel, [halo, two, one], [VMEM] * 10,
        *sources, now, mid_near, mid_low, mid_high, new_high, rate, to_y, scratch=[padded],
    )
    near = lax.all_gather(new_low, "slab", axis_index_groups=near_groups)
    src_rows, rec_rows, send = call(
        last_kernel, [raw, raw, buffer], [VMEM] * 8,
        pick, far, near, base, rate, partial, src, rec, scratch=[VMEM(one, jnp.float32)],
    )
    image_got = lax.all_to_all(send, "shot", 0, 0)
    image, src, rec = call(
        gather_kernel, [(model, HBM), (raw, HBM), (raw, HBM)], [VMEM] * 4,
        put, image_got, src_rows, rec_rows,
        scratch=[VMEM(model, jnp.float32), dma((2 + velocity.shape[0] // BX // 2,))],
    )
    return image.reshape(velocity.shape), src.reshape(src_cur.shape), rec.reshape(src_cur.shape)


def solution(mesh):
    wave = P("shot", None, "slab", None)
    model = P("shot", "slab", None)
    return jax.shard_map(
        local,
        mesh=mesh,
        in_specs=(wave,) * 4 + (model,) + (P(),) * 6 + (P("shot", None, None, None),),
        out_specs=(model, wave, wave),
        check_vma=False,
    )
```

```python
import jax
import jax.numpy as jnp
from jax import lax
from jax.experimental import pallas as pl
from jax.experimental.pallas import tpu as pltpu
from jax.sharding import PartitionSpec as P


BX = 8
KT = 8
STEPS = 4
CAP = 2
REACH = 4
PAD = 8
VMEM = pltpu.VMEM
SMEM = pltpu.SMEM
HBM = pltpu.HBM

SCALE = 5040.0
TAPS = (-43050.0, 8064.0, -1008.0, 128.0, -9.0)


def call(body, outs, in_spaces, *args, scratch=()):
    outs = [o if isinstance(o[0], tuple) else (o, VMEM) for o in outs]
    outs = [o if len(o) == 3 else o + (jnp.float32,) for o in outs]
    size = 8 * 64 * 128
    return pl.pallas_call(
        body,
        out_shape=[jax.ShapeDtypeStruct(s, t) for s, _, t in outs],
        in_specs=[pl.BlockSpec(memory_space=s) for s in in_spaces],
        out_specs=[pl.BlockSpec(memory_space=m) for _, m, _ in outs],
        scratch_shapes=list(scratch),
        compiler_params=pltpu.CompilerParams(vmem_limit_bytes=24 * 1024 * 1024),
        cost_estimate=pl.CostEstimate(
            flops=90 * size, bytes_accessed=32 * size, transcendentals=0
        ),
    )(*args)


def is_odd():
    return lax.rem(lax.axis_index("slab"), 2) == 1


def partner():
    return jnp.where(is_odd(), 0, 1)


def z_of(plane, depth):
    return jnp.where(is_odd(), plane, depth - 1 - plane)


def tap_of(reach):
    weight = jnp.zeros(reach.shape, jnp.float32)
    for r in range(1, REACH + 1):
        weight = jnp.where(reach == r, TAPS[r], weight)
    return weight


def along_y_matrix(size_y):
    shape = (2 * size_y, size_y)
    row = lax.rem(lax.broadcasted_iota(jnp.int32, shape, 0), size_y)
    return tap_of(jnp.abs(row - lax.broadcasted_iota(jnp.int32, shape, 1))).astype(jnp.bfloat16)


def along_y(planes, to_y):
    rows = planes.reshape(-1, planes.shape[2])
    high = rows.astype(jnp.bfloat16)
    low = (rows - high.astype(jnp.float32)).astype(jnp.bfloat16)
    sums = jnp.dot(
        jnp.concatenate([high, low], axis=1), to_y, preferred_element_type=jnp.float32
    )
    return sums.reshape(planes.shape)


def clear_edges(padded):
    count, rows, size_y = padded.shape
    zeros = jnp.zeros((count, PAD, size_y), jnp.float32)
    padded[:, pl.ds(0, PAD)] = zeros
    padded[:, pl.ds(rows - PAD, PAD)] = zeros


def full_sums(padded, planes, first, plane_at, to_y, lines=None):
    count, size_x, _ = planes.shape
    padded[pl.ds(0, count), pl.ds(PAD, size_x)] = planes
    if lines is None:
        lines = along_y(planes, to_y)
    sums = []
    for p in range(count):
        total = lines[p] + TAPS[0] * planes[p]
        for r in range(1, REACH + 1):
            terms = padded[p, pl.ds(PAD + r, size_x)] + padded[p, pl.ds(PAD - r, size_x)]
            for other in (plane_at(first + p + r), plane_at(first + p - r)):
                if other is not None:
                    terms += other
            total += TAPS[r] * terms
        sums.append(total)
    return sums


def beyond_sums(plane, plane_at):
    total = 0.0
    for r in range(1, REACH + 1):
        for other in (plane_at(plane + r), plane_at(plane - r)):
            if other is not None:
                total += TAPS[r] * other
    return total


def sources_at(f, number, step, sources):
    where, spots, traces = sources
    added = traces[STEPS - 1 - step].astype(jnp.float32) if f else spots[step]
    here = (where[f] == float(number))[None]
    return jnp.where(here, added.reshape(-1, 8, added.shape[1]), 0.0).reshape(added.shape)


def start_kernel(
    src_in, rec_in, vel_in, tiles_in, x_in, z_in, y_in, depth_in, wavelet_in,
    send, to_far, src, rec, pick, put, where, spots,
    src_raw, rec_raw, vel, tiles, spot_x, spot_z, spot_y, depth_at, wavelet, sems, send_sems,
):
    shot = lax.axis_index("shot")
    moves = [(tiles_in, tiles), (vel_in, vel), (src_in, src_raw), (rec_in, rec_raw)]
    moves += [(x_in, spot_x), (z_in, spot_z), (y_in, spot_y), (depth_in, depth_at)]
    moves += [(wavelet_in, wavelet)]
    copies = [pltpu.make_async_copy(a, b, sems.at[i]) for i, (a, b) in enumerate(moves)]
    for copy in copies:
        copy.start()
    depth, size_x, size_y = src.shape
    rows = BX * depth
    held = vel.shape[0] // rows
    copies[0].wait()
    places = []
    for g in range(send.shape[0]):
        before = jnp.int32(0)
        for k in range(KT):
            before += (tiles[g, k] < shot * BX).astype(jnp.int32)
        for j in range(CAP):
            own = tiles[g, jnp.minimum(before + j, KT - 1)] - shot * BX
            filled = (before + j < KT) & (own >= 0) & (own < held)
            places.append(jnp.where(filled, own, -1))
    copies[1].wait()
    for c, own in enumerate(places):
        at = pl.multiple_of(jnp.maximum(own, 0) * rows, rows)
        copy = pltpu.make_async_copy(
            vel.at[pl.ds(at, rows)], send.at[c // CAP, c % CAP], send_sems.at[c]
        )
        copy.start()
        copies.append(copy)
    for f, (raw, field) in enumerate(((src_raw, src), (rec_raw, rec))):
        copies[2 + f].wait()
        for p in range(depth):
            plane = raw[pl.ds(z_of(p, depth), size_x, stride=depth)]
            field[p] = plane
            if p >= depth - REACH:
                to_far[f * REACH + p - (depth - REACH)] = plane
    tile = (8, size_y)
    for c, own in enumerate(places):
        put[c] = jnp.full(tile, own)
    previous = jnp.int32(-1)
    for k in range(KT):
        owner = lax.shift_right_logical(tiles[shot, k], 3)
        place = owner * CAP + (previous == owner).astype(jnp.int32)
        previous = owner
        pick[k] = jnp.full(tile, place)
    for copy in copies[4:9]:
        copy.wait()
    first = lax.axis_index("slab") * depth
    for f, local in enumerate((spot_z[shot] - first, depth_at[shot] - first)):
        where[f] = jnp.full(tile, z_of(local, depth)).astype(jnp.float32)
    row = lax.broadcasted_iota(jnp.int32, (size_x, size_y), 0)
    lane = lax.broadcasted_iota(jnp.int32, (size_x, size_y), 1)
    here = (row == spot_x[shot]) & (lane == spot_y[shot])
    for step in range(STEPS):
        spots[step] = jnp.where(here, wavelet[step, shot], 0.0)
    for copy in copies[9:]:
        copy.wait()


def first_interior_kernel(src, rec, src_old, rec_old, to_near, sums, base, to_y, padded):
    depth, size_x, size_y = src.shape
    to_y[...] = along_y_matrix(size_y)
    clear_edges(padded)
    for f, (field, old) in enumerate(((src, src_old), (rec, rec_old))):

        def plane_at(m):
            return field[m] if 0 <= m < depth else None

        for first in range(0, depth, REACH):
            planes = field[pl.ds(first, REACH)]
            if first == 0:
                to_near[pl.ds(f * REACH, REACH)] = planes
            for i, total in enumerate(full_sums(padded, planes, first, plane_at, to_y[...])):
                p = first + i
                sums[f * depth + p] = total
                before = old[pl.ds(z_of(p, depth), size_x, stride=depth)]
                base[f * depth + p] = 2.0 * planes[i] - before


def rate_kernel(pick, vel_got, near, sums, base, where, spots, traces, rate, part):
    mine = partner()
    depth = rate.shape[0]
    count = vel_got.shape[0] * CAP
    rows = [pl.ds(z_of(p, depth), BX, stride=depth) for p in range(depth)]
    for k in range(KT):
        tiles = [vel_got[k // CAP, k % CAP, at] for at in rows]
        for c in range(k + 1, count - (KT - 1 - k)):
            here = pick[k] == c
            tiles = [
                jnp.where(here, vel_got[c // CAP, c % CAP, at], tile)
                for at, tile in zip(rows, tiles, strict=True)
            ]
        for p, tile in enumerate(tiles):
            rate[p, pl.ds(k * BX, BX)] = tile * tile * (1.0 / SCALE)
    for f in range(2):

        def plane_at(m):
            return near[mine, f * REACH - 1 - m] if m < 0 else None

        for p in range(depth):
            total = sums[f * depth + p]
            if p < REACH:
                total += beyond_sums(p, plane_at)
            added = sources_at(f, p, 0, (where, spots, traces))
            part[f * depth + p] = base[f * depth + p] + rate[p] * total + added


def first_kernel(far, part, rate, now):
    depth = rate.shape[0]
    for f in range(2):

        def plane_at(m):
            return far[f * REACH + REACH - 1 - (m - depth)] if m >= depth else None

        for p in range(depth):
            value = part[f * depth + p]
            if p >= depth - REACH:
                value += rate[p] * beyond_sums(p, plane_at)
            now[f * depth + p] = value
    now[pl.ds(2 * depth, REACH)] = rate[pl.ds(depth - REACH, REACH)]


def wide_interior_kernel(
    now, src_old, rec_old, rate, to_y, src_near, rec_near, base, padded
):
    depth = rate.shape[0]
    clear_edges(padded)
    src_near[pl.ds(0, depth)] = now[pl.ds(0, depth)]
    src_near[pl.ds(depth, REACH)] = rate[pl.ds(0, REACH)]
    rec_near[...] = now[pl.ds(depth, depth)]
    for f, old in enumerate((src_old, rec_old)):

        def plane_at(m):
            return now[f * depth + m] if 0 <= m < depth else None

        for first in range(0, depth, REACH):
            planes = now[pl.ds(f * depth + first, REACH)]
            for i, total in enumerate(full_sums(padded, planes, first, plane_at, to_y[...])):
                p = first + i
                base[f * depth + p] = 2.0 * planes[i] - old[p] + rate[p] * total


def wide_near_kernel(
    where, spots, traces, src_near, rec_near, near_old, now, base, rate, to_y,
    mid_near, mid_low, mid_part, padded,
):
    depth = rate.shape[0]
    mine = partner()
    sources = (where, spots, traces)
    clear_edges(padded)
    for f, near in enumerate((src_near, rec_near)):

        def plane_at(m):
            if m >= 0:
                return now[f * depth + m]
            return near[mine, -1 - m]

        planes = near[mine, pl.ds(0, REACH)]
        totals = full_sums(padded, planes, 0, lambda m: plane_at(-1 - m), to_y[...])
        for i, total in enumerate(totals):
            value = 2.0 * planes[i] - near_old[mine, f * REACH + i]
            value += src_near[mine, depth + i] * total
            mid_near[f * REACH + i] = value + sources_at(f, -1 - i, 1, sources)
        for p in range(depth):
            value = base[f * depth + p] + sources_at(f, p, 1, sources)
            if p < REACH:
                share = beyond_sums(p, lambda m: plane_at(m) if m < 0 else None)
                mid_low[f * REACH + p] = value + rate[p] * share
            else:
                mid_part[f * REACH + p - REACH] = value


def wide_far_kernel(
    where, spots, traces, far, far_old, now, mid_low, mid_part, rate, to_y,
    mid_high, to_far, mid_far, padded,
):
    depth = rate.shape[0]
    high = depth - REACH
    sources = (where, spots, traces)
    clear_edges(padded)
    work = [padded.at[pl.ds(i * REACH, REACH)] for i in range(4)]

    def mid_at(f, m):
        if m < high:
            return mid_low[f * REACH + m]
        return mid_high[f * REACH + m - high] if m < depth else mid_far[f * REACH + m - depth]

    outside = [[far[f * depth + depth - 1 - i] for i in range(REACH)] for f in range(2)]
    lines = along_y(jnp.stack(outside[0] + outside[1]), to_y[...])
    for f in range(2):

        def plane_at(m):
            if m < depth:
                return now[f * depth + m]
            return far[f * depth + 2 * depth - 1 - m]

        for p in range(high, depth):
            share = beyond_sums(p, lambda m: plane_at(m) if m >= depth else None)
            mid_high[f * REACH + p - high] = mid_part[f * REACH + p - high] + rate[p] * share
        planes = jnp.stack(outside[f])
        own_lines = lines[f * REACH : (f + 1) * REACH]
        totals = full_sums(work[f], planes, depth, plane_at, None, own_lines)
        for i, total in enumerate(totals):
            value = 2.0 * planes[i] - far_old[f * REACH + REACH - 1 - i]
            value += far[2 * depth + REACH - 1 - i] * total
            mid_far[f * REACH + i] = value + sources_at(f, depth + i, 1, sources)
    lines = along_y(mid_high[...], to_y[...])
    for f in range(2):
        planes = mid_high[pl.ds(f * REACH, REACH)]
        own_lines = lines[f * REACH : (f + 1) * REACH]
        totals = full_sums(work[2 + f], planes, high, lambda m: mid_at(f, m), None, own_lines)
        for i, total in enumerate(totals):
            p = high + i
            value = 2.0 * planes[i] - now[f * depth + p] + rate[p] * total
            to_far[f * REACH + i] = value + sources_at(f, p, 2, sources)


def interior_kernel(
    where, spots, traces, now, mid_near, mid_low, mid_high, new_high, rate, to_y,
    new_low, base, partial, padded,
):
    depth = rate.shape[0]
    high = depth - REACH
    sources = (where, spots, traces)
    clear_edges(padded)

    def mid_at(f, m):
        if m < 0:
            return mid_near[f * REACH - 1 - m]
        return mid_low[f * REACH + m] if m < high else mid_high[f * REACH + m - high]

    def new_at(f, m):
        return new_low[f * REACH + m] if m < high else new_high[f * REACH + m - high]

    for f in range(2):
        planes = mid_low[pl.ds(f * REACH, REACH)]
        totals = full_sums(padded, planes, 0, lambda m: mid_at(f, m), to_y[...])
        for p, total in enumerate(totals):
            value = 2.0 * planes[p] - now[f * depth + p] + rate[p] * total
            new_low[f * REACH + p] = value + sources_at(f, p, 2, sources)
    for f in range(2):
        for first, part in ((0, new_low), (high, new_high)):
            planes = part[pl.ds(f * REACH, REACH)]

            def plane_at(m):
                return new_at(f, m) if 0 <= m < depth else None

            for i, total in enumerate(full_sums(padded, planes, first, plane_at, to_y[...])):
                p = first + i
                value = 2.0 * planes[i] - mid_at(f, p) + rate[p] * total
                base[f * depth + p] = value + sources_at(f, p, 3, sources)
    for p in range(depth):
        total = new_at(0, p) * now[depth + p] + mid_at(0, p) * mid_at(1, p)
        partial[p] = total + now[p] * new_at(1, p)


def last_kernel(
    pick, far, near, base, rate, partial, src_first, rec_first, src_rows, rec_rows, send, image
):
    mine = partner()
    depth = rate.shape[0]
    count = send.shape[0] * CAP
    for p in range(depth):
        fields = []
        at = pl.ds(z_of(p, depth), rate.shape[1], stride=depth)
        for f, rows in enumerate((src_rows, rec_rows)):

            def plane_at(m):
                if m < 0:
                    return near[mine, f * REACH - 1 - m]
                return far[f * REACH + REACH - 1 - (m - depth)] if m >= depth else None

            value = base[f * depth + p] + rate[p] * beyond_sums(p, plane_at)
            rows[at] = value
            fields.append(value)
        image[p] = partial[p] + fields[0] * rec_first[p] + src_first[p] * fields[1]
    for c in range(count):
        tiles = [jnp.zeros(send.shape[2:], jnp.float32)] * depth
        for k in range(max(0, c - (count - KT)), min(KT - 1, c) + 1):
            here = pick[k] == c
            at = pl.ds(k * BX, BX)
            tiles = [jnp.where(here, image[p, at], tile) for p, tile in enumerate(tiles)]
        for p, tile in enumerate(tiles):
            send[c // CAP, (c % CAP) * depth + p] = tile


def gather_kernel(put, got, src_rows, rec_rows, out, src_out, rec_out, out_rows, sems):
    depth = got.shape[1] // CAP
    count = put.shape[0]
    held = out_rows.shape[0] // (BX * depth)
    copies = []
    for f, (rows, to) in enumerate(((src_rows, src_out), (rec_rows, rec_out))):
        copies.append(pltpu.make_async_copy(rows, to, sems.at[f]))
        copies[-1].start()
    for t in range(held):
        totals = [jnp.zeros(got.shape[2:], jnp.float32)] * depth
        for c in range(count):
            here = put[c] == t
            first = (c % CAP) * depth
            totals = [
                total + jnp.where(here, got[c // CAP, first + p], 0.0)
                for p, total in enumerate(totals)
            ]
        for p, total in enumerate(totals):
            out_rows[pl.ds(t * BX * depth + z_of(p, depth), BX, stride=depth)] = total
        if t % 2:
            part = pl.ds((t - 1) * BX * depth, 2 * BX * depth)
            copies.append(pltpu.make_async_copy(out_rows.at[part], out.at[part], sems.at[2 + t // 2]))
            copies[-1].start()
    for copy in copies:
        copy.wait()


def local(
    src_prev,
    src_cur,
    rec_cur,
    rec_next,
    velocity,
    aperture_tiles,
    wavelet,
    src_x,
    src_z,
    src_y,
    rec_depth,
    rec_data,
):
    slabs = lax.axis_size("slab")
    shots = lax.axis_size("shot")
    far_pairs = []
    for i in range(1, slabs - 1, 2):
        far_pairs += [(i, i + 1), (i + 1, i)]
    near_groups = [[i, i + 1] for i in range(0, slabs, 2)]

    def flat(array):
        return array.reshape(-1, array.shape[-1])

    _, size_x, depth, size_y = src_cur.shape
    raw = (depth * size_x, size_y)
    model = (velocity.shape[0] * depth, size_y)
    one, two = (depth, size_x, size_y), (2 * depth, size_x, size_y)
    halo = (2 * REACH, size_x, size_y)
    wide = (2 * depth + REACH, size_x, size_y)
    buffer = (shots, CAP * depth, BX, size_y)
    dma = pltpu.SemaphoreType.DMA
    padded = VMEM((REACH, size_x + 2 * PAD, size_y), jnp.float32)
    count = shots * CAP
    given = (flat(src_cur), flat(rec_cur), flat(velocity), aperture_tiles)
    given += (src_x, src_z, src_y, rec_depth, wavelet.T)
    scalars = [SMEM(a.shape, a.dtype) for a in given[3:]]
    send, to_far, src, rec, pick, put, where, spots = call(
        start_kernel,
        [
            ((shots, CAP, BX * depth, size_y), HBM), halo, one, one, ((KT, 8, size_y), VMEM, jnp.int32),
            ((count, 8, size_y), VMEM, jnp.int32), (2, 8, size_y), (STEPS, size_x, size_y),
        ],
        [HBM] * 9, *[pltpu.with_memory_space_constraint(a, HBM) for a in given],
        scratch=[
            VMEM(raw, jnp.float32), VMEM(raw, jnp.float32), VMEM(model, jnp.float32), *scalars,
            dma((9,)), dma((count,)),
        ],
    )
    sources = (where, spots, rec_data[0])

    vel_got = lax.all_to_all(send, "shot", 0, 0)
    far = lax.ppermute(to_far, "slab", far_pairs)
    to_near, sums, base, to_y = call(
        first_interior_kernel, [halo, two, two, ((2 * size_y, size_y), VMEM, jnp.bfloat16)],
        [VMEM] * 4, src, rec, flat(src_prev), flat(rec_next), scratch=[padded],
    )
    near = lax.all_gather(to_near, "slab", axis_index_groups=near_groups)
    rate, part = call(
        rate_kernel, [one, two], [VMEM] * 8, pick, vel_got, near, sums, base, *sources
    )
    (now,) = call(first_kernel, [wide], [VMEM] * 3, far, part, rate)

    wide_far = lax.ppermute(now, "slab", far_pairs)
    src_near, rec_near, base = call(
        wide_interior_kernel, [(depth + REACH, size_x, size_y), one, two], [VMEM] * 5,
        now, src, rec, rate, to_y, scratch=[padded],
    )
    src_near = lax.all_gather(src_near, "slab", axis_index_groups=near_groups)
    rec_near = lax.all_gather(rec_near, "slab", axis_index_groups=near_groups)
    mid_near, mid_low, mid_part = call(
        wide_near_kernel, [halo] * 3, [VMEM] * 10,
        *sources, src_near, rec_near, near, now, base, rate, to_y, scratch=[padded],
    )
    mid_high, new_high = call(
        wide_far_kernel, [halo] * 2, [VMEM] * 10,
        *sources, wide_far, far, now, mid_low, mid_part, rate, to_y,
        scratch=[
            VMEM(halo, jnp.float32),
            VMEM((4 * REACH, size_x + 2 * PAD, size_y), jnp.float32),
        ],
    )

    far = lax.ppermute(new_high, "slab", far_pairs)
    new_low, base, partial = call(
        interior_kernel, [halo, two, one], [VMEM] * 10,
        *sources, now, mid_near, mid_low, mid_high, new_high, rate, to_y, scratch=[padded],
    )
    near = lax.all_gather(new_low, "slab", axis_index_groups=near_groups)
    src_rows, rec_rows, send = call(
        last_kernel, [raw, raw, buffer], [VMEM] * 8,
        pick, far, near, base, rate, partial, src, rec, scratch=[VMEM(one, jnp.float32)],
    )
    image_got = lax.all_to_all(send, "shot", 0, 0)
    image, src, rec = call(
        gather_kernel, [(model, HBM), (raw, HBM), (raw, HBM)], [VMEM] * 4,
        put, image_got, src_rows, rec_rows,
        scratch=[VMEM(model, jnp.float32), dma((2 + velocity.shape[0] // BX // 2,))],
    )
    return image.reshape(velocity.shape), src.reshape(src_cur.shape), rec.reshape(src_cur.shape)


def solution(mesh):
    wave = P("shot", None, "slab", None)
    model = P("shot", "slab", None)
    return jax.shard_map(
        local,
        mesh=mesh,
        in_specs=(wave,) * 4 + (model,) + (P(),) * 6 + (P("shot", None, None, None),),
        out_specs=(model, wave, wave),
        check_vma=False,
    )
```
